32 devices in a mesh: row: 8 (over z, core), col: 4 (over y, x).
Axes of the slice: x: 2, y: 2, z: 4, core: 2. Of those that a mesh axis runs over, the one named last changes fastest.
Arguments:
- tensor_slab: float32 [1024, 65536], P(None, ('row', 'col')), may hold values from 0.25 to 1500, as said below
- left_init: float32 [1024, 128], replicated, may hold values from 0.15 to 1.5
- right_init: float32 [128, 65536], P(None, ('row', 'col')), may hold values from 0.1 to 1
- second_left_init: float32 [16384, 128], P('row'), may hold values from 0.1 to 1
- second_right_init: float32 [128, 512], P(None, 'col'), may hold values from 0.003 to 0.03
Outputs:
- left_out: float32 [1024, 128], replicated
- second_left_out: float32 [16384, 128], P(('row', 'col'))
The draws below stay inside these ranges and needn't reach their ends.
Inputs may be any that keep to these rules, and one draw needn't show every extreme that they name: `tensor_slab`: every entry is positive.
All inputs are finite; a program needn't handle non-finite values.
Results may differ from the reference program's by a relative error of at most 0.0003.
Values sent between devices are 32-bit elements; how exact they have to be, the bound alone decides.
No kernel may reach another device: no remote copies, remote signals or barrier semaphores. Data moves between devices by JAX's collectives and lax.ppermute only.
A program may use at most 128 MiB of HBM per device.

```python
import math
from functools import partial
import jax
import jax.numpy as jnp
from jax import lax

M = 1024
R = 128
K = 512
COLS_DEV = 2048
J = 128
NCOLS = 65536
ROWS2 = 16384


def draw_tensor_slab(key, part):
    row_key, col_key, jitter_key = jax.random.split(key, 3)
    position = jnp.arange(NCOLS, dtype=jnp.float32)[None, :] / NCOLS
    rising = jnp.exp(position * math.log(3.0))
    row_scale = jnp.exp(jax.random.uniform(row_key, (M, 1), jnp.float32, 0.0, math.log(10.0)))
    jitter = jnp.exp(jax.random.uniform(jitter_key, (M, NCOLS), jnp.float32, math.log(0.5), math.log(2.0)))
    col_scale = jnp.exp(jax.random.uniform(col_key, (1, NCOLS), jnp.float32, 0.0, math.log(10.0))) * rising
    return (row_scale * col_scale * jitter).astype(jnp.float32)


def block_levels(key, extent, cuts, low, top_value):
    def one(dim, shards_of):
        heights = jax.random.uniform(jax.random.fold_in(jax.random.fold_in(key, 6), dim), (shards_of,), jnp.float32, low / len(cuts), top_value / len(cuts))
        return jnp.repeat(jnp.exp(heights), extent[dim] // shards_of).reshape((-1,) + (1,) * (len(extent) - dim - 1))

    loudness = one(*cuts[0])
    for cut in cuts[1:]:
        loudness = loudness * one(*cut)
    return loudness


def setup_inputs(seed: int = 0) -> dict:
    key_list = jax.random.split(jax.random.key(seed), 6)
    return {
        "tensor_slab": draw_tensor_slab(jax.random.fold_in(key_list[5], 71), 0),
        "left_init": jnp.clip(jnp.exp(jax.random.uniform(key_list[1], (M, R), jnp.float32, math.log(0.15), math.log(1.5))), 0.15, 1.5),
        "right_init": jnp.clip(jnp.exp(math.log(1.0) - 2.3025851 * jax.random.uniform(key_list[2], (R, NCOLS), jnp.float32) ** block_levels(key_list[2], (R, NCOLS), ((1, 32),), -0.2, 0.2)), 0.1, 1.0),
        "second_left_init": jnp.clip(jnp.exp(math.log(1.0) - 2.3025851 * jax.random.uniform(key_list[3], (ROWS2, R), jnp.float32) ** block_levels(key_list[3], (ROWS2, R), ((0, 8),), -0.2, 0.2)), 0.1, 1.0),
        "second_right_init": jnp.clip(jnp.exp(math.log(0.03) - 2.3025851 * jax.random.uniform(key_list[4], (R, K), jnp.float32) ** block_levels(key_list[4], (R, K), ((1, 4),), -0.2, 0.2)), 0.003, 0.03),
    }


def segment_block(tensor_slab, left_fac, right_fac, col_sums, index_block):
    first_col = index_block.astype(jnp.int32) * COLS_DEV
    slab_part = lax.dynamic_slice_in_dim(tensor_slab, first_col, COLS_DEV, 1)
    right_part = lax.dynamic_slice_in_dim(right_fac, first_col, COLS_DEV, 1)
    product = jnp.dot(left_fac, right_part, precision=lax.Precision.HIGHEST)
    quotient = slab_part / product
    numerator = lax.dot_general(left_fac, quotient, (((0,), (0,)), ((), ())), precision=lax.Precision.HIGHEST)
    right_new = right_part * numerator / col_sums[:, None]
    product = jnp.dot(left_fac, right_new, precision=lax.Precision.HIGHEST)
    quotient = slab_part / product
    left_numer = lax.dot_general(quotient, right_new, (((1,), (1,)), ((), ())), precision=lax.Precision.HIGHEST)
    return right_new, left_numer, jnp.sum(right_new, axis=1)


def reference(tensor_slab, left_init, right_init, second_left_init, second_right_init):
    left_fac = left_init
    right_fac = right_init
    for repeat in range(2):
        col_sums = jnp.sum(left_fac, axis=0)
        pieces = lax.map(partial(segment_block, tensor_slab, left_fac, right_fac, col_sums),
                         jnp.arange(NCOLS // COLS_DEV, dtype=jnp.int32))
        right_blocks, left_numers, row_sums = pieces
        right_fac = jnp.transpose(right_blocks, (1, 0, 2)).reshape(R, NCOLS)
        left_fac = left_fac * jnp.sum(left_numers, axis=0) / jnp.sum(row_sums, axis=0)[None, :]
    unfolded = right_fac.reshape(R * J, K)
    product = jnp.dot(second_left_init, second_right_init, precision=lax.Precision.HIGHEST)
    numerator = lax.dot_general(second_left_init, unfolded / product, (((0,), (0,)), ((), ())), precision=lax.Precision.HIGHEST)
    second_right = second_right_init * numerator / jnp.sum(second_left_init, axis=0)[:, None]
    product = jnp.dot(second_left_init, second_right, precision=lax.Precision.HIGHEST)
    left_numer = lax.dot_general(unfolded / product, second_right, (((1,), (1,)), ((), ())), precision=lax.Precision.HIGHEST)
    second_left_out = second_left_init * left_numer / jnp.sum(second_right, axis=1)[None, :]
    return left_fac, second_left_out
```

```python
import jax
import jax.numpy as jnp
from jax import lax
from jax.sharding import PartitionSpec as P

AXES = ("row", "col")
HIGH = lax.Precision.HIGH


def exchange(parts):
    return lax.all_to_all(parts, AXES, split_axis=0, concat_axis=0, tiled=True)


def gather(part, devices):
    return exchange(jnp.broadcast_to(part[None], (devices,) + part.shape))


def body(tensor_slab, left_init, right_init, second_left_init, second_right_init):
    row_devices = lax.axis_size("row")
    col_devices = lax.axis_size("col")
    devices = row_devices * col_devices
    own = lax.axis_index("row") * col_devices + lax.axis_index("col")
    m, rank = left_init.shape
    k = second_right_init.shape[1] * col_devices
    slices = right_init.shape[1] // k
    per_owner = rank // devices
    rows_own = m // devices

    second_rows = second_left_init.shape[0] // col_devices
    own_left = lax.dynamic_slice_in_dim(
        second_left_init, lax.axis_index("col") * second_rows, second_rows, 0
    )
    own_left = own_left.reshape(per_owner, devices, slices, rank).transpose(1, 0, 2, 3)
    arrived = exchange(own_left.reshape(devices, per_owner * slices, rank))
    second_left = arrived.reshape(rank * slices, rank)
    col_sums = jnp.sum(second_left, axis=0)
    whole = lax.all_to_all(
        jnp.broadcast_to(second_right_init[None], (col_devices,) + second_right_init.shape),
        "col", split_axis=0, concat_axis=0, tiled=True,
    )
    whole = whole.transpose(1, 0, 2).reshape(rank, k // rank, rank).transpose(1, 0, 2)

    left_fac, right_fac = left_init, right_init
    for repeat in range(2):
        quotient = tensor_slab / jnp.dot(left_fac, right_fac, precision=HIGH)
        numerator = lax.dot_general(left_fac, quotient, (((0,), (0,)), ((), ())), precision=HIGH)
        right_fac = right_fac * numerator / jnp.sum(left_fac, axis=0)[:, None]
        quotient = tensor_slab / jnp.dot(left_fac, right_fac, precision=HIGH)
        left_numer = lax.dot_general(quotient, right_fac, (((1,), (1,)), ((), ())), precision=HIGH)
        sums = jnp.stack([jnp.sum(right_fac, axis=1), col_sums] + [jnp.zeros_like(col_sums)] * 6)
        parts = jnp.concatenate(
            [
                left_numer.reshape(devices, rows_own, rank),
                jnp.broadcast_to(sums[None], (devices, 8, rank)),
            ],
            axis=1,
        )
        total = jnp.sum(exchange(parts), axis=0)
        left_own = lax.dynamic_slice_in_dim(left_fac, own * rows_own, rows_own, 0)
        left_own = left_own * total[:rows_own] / total[rows_own][None, :]
        left_fac = gather(left_own, devices).reshape(m, rank)
    col_totals = total[rows_own + 1]

    block = right_fac.reshape(rank * slices, k)
    init = whole.transpose(1, 0, 2).reshape(rank, k)
    quotient = block / jnp.dot(second_left, init, precision=HIGH)
    numerator = lax.dot_general(second_left, quotient, (((0,), (0,)), ((), ())), precision=HIGH)
    scaled = numerator.reshape(rank, k // rank, rank).transpose(1, 0, 2)
    rows_part = k // devices
    part = jnp.sum(exchange(scaled.reshape(devices, rows_part, rank)), axis=0)
    init_over = (whole / col_totals[None, :, None]).reshape(k, rank)
    part = part * lax.dynamic_slice_in_dim(init_over, own * rows_part, rows_part, 0)
    second_right = gather(part, devices).reshape(k // rank, rank, rank)
    second_right = second_right.transpose(1, 0, 2).reshape(rank, k)
    quotient = block / jnp.dot(second_left, second_right, precision=HIGH)
    left_numer = lax.dot_general(quotient, second_right, (((1,), (1,)), ((), ())), precision=HIGH)
    rows_out = second_left * left_numer / jnp.sum(second_right, axis=1)[None, :]
    returned = exchange(rows_out.reshape(devices, per_owner * slices, rank))
    returned = returned.reshape(devices, per_owner, slices, rank).transpose(1, 0, 2, 3)
    return (left_fac, returned.reshape(second_rows, rank))


def solution(mesh):
    placed = (P(None, AXES), P(), P(None, AXES), P("row", None), P(None, "col"))
    return jax.shard_map(
        body, mesh=mesh, in_specs=placed, out_specs=(P(), P(AXES, None)), check_vma=False
    )
```

```python
import jax
import jax.numpy as jnp
from jax import lax
from jax.sharding import PartitionSpec as P

AXES = ("row", "col")
HIGH = lax.Precision.HIGH


def exchange(parts):
    return lax.all_to_all(parts, AXES, split_axis=0, concat_axis=0, tiled=True)


def send(values, row_flip, col_flip):
    rows, cols = lax.axis_size("row"), lax.axis_size("col")
    pairs = [
        (r * cols + c, (r ^ row_flip) * cols + (c ^ col_flip))
        for r in range(rows)
        for c in range(cols)
    ]
    return lax.ppermute(values, AXES, pairs)


def pick(values, index):
    return lax.dynamic_index_in_dim(values, index, 0, keepdims=False)


def tree_sum(terms):
    while len(terms) > 1:
        terms = [a + b for a, b in zip(terms[::2], terms[1::2])]
    return terms[0]


def reduce_parts(parts):
    core, col = lax.axis_index("row") % 2, lax.axis_index("col")
    cols = lax.axis_size("col")
    own = pick(parts, core) + send(pick(parts, 1 - core), 1, 0)
    own = tree_sum(
        [pick(own, col)] + [send(pick(own, col ^ flip), 0, flip) for flip in range(1, cols)]
    )
    return tree_sum([own] + [send(own, flip, 0) for flip in range(2, lax.axis_size("row"), 2)])


def spread_parts(part):
    core, col = lax.axis_index("row") % 2, lax.axis_index("col")
    cols = lax.axis_size("col")
    near = jnp.stack([part] + [send(part, 0, flip) for flip in range(1, cols)])
    near = jnp.stack([pick(near, index ^ col) for index in range(cols)])
    both = jnp.stack([near, send(near, 1, 0)])
    return jnp.stack([pick(both, core), pick(both, 1 - core)])


def body(tensor_slab, left_init, right_init, second_left_init, second_right_init):
    row_devices = lax.axis_size("row")
    col_devices = lax.axis_size("col")
    devices = row_devices * col_devices
    m, rank = left_init.shape
    k = second_right_init.shape[1] * col_devices
    slices = right_init.shape[1] // k
    per_owner = rank // devices
    own_part = (lax.axis_index("row") % 2) * col_devices + lax.axis_index("col")
    rows_own = m // (2 * col_devices)

    second_rows = second_left_init.shape[0] // col_devices
    own_left = lax.dynamic_slice_in_dim(
        second_left_init, lax.axis_index("col") * second_rows, second_rows, 0
    )
    own_left = own_left.reshape(per_owner, devices, slices, rank).transpose(1, 0, 2, 3)
    arrived = exchange(own_left.reshape(devices, per_owner * slices, rank))
    second_left = arrived.reshape(rank * slices, rank)
    col_sums = jnp.sum(second_left, axis=0)
    whole = lax.all_to_all(
        jnp.broadcast_to(second_right_init[None], (col_devices,) + second_right_init.shape),
        "col", split_axis=0, concat_axis=0, tiled=True,
    )
    whole = whole.transpose(1, 0, 2).reshape(rank, k // rank, rank).transpose(1, 0, 2)

    left_fac, right_fac = left_init, right_init
    for repeat in range(2):
        quotient = tensor_slab / jnp.dot(left_fac, right_fac, precision=HIGH)
        numerator = lax.dot_general(left_fac, quotient, (((0,), (0,)), ((), ())), precision=HIGH)
        right_fac = right_fac * numerator / jnp.sum(left_fac, axis=0)[:, None]
        quotient = tensor_slab / jnp.dot(left_fac, right_fac, precision=HIGH)
        left_numer = lax.dot_general(quotient, right_fac, (((1,), (1,)), ((), ())), precision=HIGH)
        sums = jnp.stack([jnp.sum(right_fac, axis=1), col_sums] + [jnp.zeros_like(col_sums)] * 6)
        parts = jnp.concatenate(
            [
                left_numer.reshape(2, col_devices, rows_own, rank),
                jnp.broadcast_to(sums[None, None], (2, col_devices, 8, rank)),
            ],
            axis=2,
        )
        total = reduce_parts(parts)
        left_own = lax.dynamic_slice_in_dim(left_fac, own_part * rows_own, rows_own, 0)
        left_own = left_own * total[:rows_own] / total[rows_own][None, :]
        left_fac = spread_parts(left_own).reshape(m, rank)
    col_totals = total[rows_own + 1]

    block = right_fac.reshape(rank * slices, k)
    init = whole.transpose(1, 0, 2).reshape(rank, k)
    quotient = block / jnp.dot(second_left, init, precision=HIGH)
    numerator = lax.dot_general(second_left, quotient, (((0,), (0,)), ((), ())), precision=HIGH)
    scaled = numerator.reshape(rank, k // rank, rank).transpose(1, 0, 2)
    rows_part = k // (2 * col_devices)
    part = reduce_parts(scaled.reshape(2, col_devices, rows_part, rank))
    init_over = (whole / col_totals[None, :, None]).reshape(k, rank)
    part = part * lax.dynamic_slice_in_dim(init_over, own_part * rows_part, rows_part, 0)
    second_right = spread_parts(part).reshape(k // rank, rank, rank)
    second_right = second_right.transpose(1, 0, 2).reshape(rank, k)
    quotient = block / jnp.dot(second_left, second_right, precision=HIGH)
    left_numer = lax.dot_general(quotient, second_right, (((1,), (1,)), ((), ())), precision=HIGH)
    rows_out = second_left * left_numer / jnp.sum(second_right, axis=1)[None, :]
    returned = exchange(rows_out.reshape(devices, per_owner * slices, rank))
    returned = returned.reshape(devices, per_owner, slices, rank).transpose(1, 0, 2, 3)
    return (left_fac, returned.reshape(second_rows, rank))


def solution(mesh):
    placed = (P(None, AXES), P(), P(None, AXES), P("row", None), P(None, "col"))
    return jax.shard_map(
        body, mesh=mesh, in_specs=placed, out_specs=(P(), P(AXES, None)), check_vma=False
    )
```

```python
import functools

import jax
import jax.numpy as jnp
from jax import lax
from jax.experimental import pallas as pl
from jax.experimental.pallas import tpu as pltpu
from jax.sharding import PartitionSpec as P

AXES = ("row", "col")
F32, BF16 = jnp.float32, jnp.bfloat16
PAD = 8
VMEM_BYTES = 40 * 1024 * 1024


def exchange(parts):
    return lax.all_to_all(parts, AXES, split_axis=0, concat_axis=0, tiled=True)


def send(values, row_flip, col_flip):
    rows, cols = lax.axis_size("row"), lax.axis_size("col")
    pairs = [
        (r * cols + c, (r ^ row_flip) * cols + (c ^ col_flip))
        for r in range(rows)
        for c in range(cols)
    ]
    return lax.ppermute(values, AXES, pairs)


def pick(values, index):
    return lax.dynamic_index_in_dim(values, index, 0, keepdims=False)


def tree_sum(terms):
    while len(terms) > 1:
        terms = [a + b for a, b in zip(terms[::2], terms[1::2])]
    return terms[0]


def reduce_parts(parts):
    core, col = lax.axis_index("row") % 2, lax.axis_index("col")
    cols = lax.axis_size("col")
    own = pick(parts, core) + send(pick(parts, 1 - core), 1, 0)
    own = tree_sum(
        [pick(own, col)] + [send(pick(own, col ^ flip), 0, flip) for flip in range(1, cols)]
    )
    return tree_sum([own] + [send(own, flip, 0) for flip in range(2, lax.axis_size("row"), 2)])


def spread_parts(part):
    core, col = lax.axis_index("row") % 2, lax.axis_index("col")
    cols = lax.axis_size("col")
    near = jnp.stack([part] + [send(part, 0, flip) for flip in range(1, cols)])
    near = jnp.stack([pick(near, index ^ col) for index in range(cols)])
    both = jnp.stack([near, send(near, 1, 0)])
    return jnp.stack([pick(both, core), pick(both, 1 - core)])


def split(x):
    high = x.astype(BF16)
    return high, (x - high.astype(F32)).astype(BF16)


def dot(a, b):
    return jnp.dot(a, b, preferred_element_type=F32)


def dot_nt(a, b):
    return lax.dot_general(a, b, (((1,), (1,)), ((), ())), preferred_element_type=F32)


def divide(x, y):
    guess = pl.reciprocal(y, approx=True)
    return x * (guess * (2.0 - y * guess))


def prepare_left(left_ref, pair_ref):
    rank = left_ref.shape[1]
    high, low = split(left_ref[...])
    pair_ref[:, :rank] = high
    pair_ref[:, rank:] = low


def prepare_left_t(left_ref, pair_t_ref, sums_ref):
    rank = left_ref.shape[1]
    turned = left_ref[...].T
    high, low = split(turned)
    pair_t_ref[:rank, :] = high
    pair_t_ref[rank:, :] = low
    sums_ref[...] = jnp.broadcast_to(jnp.sum(turned, axis=1, keepdims=True), sums_ref.shape)


def row_chunks(m):
    size = min(256, m)
    return [pl.ds(start, size) for start in range(0, m, size)]


def quotients(slab_ref, pair_ref, right, rows):
    rank = right.shape[0]
    high, low = split(right)
    twice = jnp.concatenate([high, high], axis=0)
    product = dot(pair_ref[rows, :], twice) + dot(pair_ref[rows, :rank], low)
    return split(divide(slab_ref[rows, :], product))


def right_update(slab_ref, pair_ref, pair_t_ref, sums_ref, right, high_ref, low_ref):
    rank = right.shape[0]
    for rows in row_chunks(slab_ref.shape[0]):
        high, low = quotients(slab_ref, pair_ref, right, rows)
        high_ref[rows, :] = high
        low_ref[rows, :] = low
    both = dot(pair_t_ref[...], high_ref[...])
    numerator = both[:rank] + both[rank:] + dot(pair_t_ref[:rank, :], low_ref[...])
    return right * numerator / sums_ref[:, :1]


def left_numerator(slab_ref, pair_ref, right, total_ref, sums_ref, first):
    rank = right.shape[0]
    right_high, right_low = split(right)
    right_both = jnp.concatenate([right_high, right_low], axis=0)
    ones = jnp.ones((16, right.shape[1]), BF16)
    row_sums = dot_nt(ones, right_both)[:PAD]
    row_sums = row_sums[:, :rank] + row_sums[:, rank:]
    sums_ref[...] = jnp.where(first, row_sums, sums_ref[...] + row_sums)
    for rows in row_chunks(slab_ref.shape[0]):
        high, low = quotients(slab_ref, pair_ref, right, rows)
        both = dot_nt(high, right_both)
        term = both[:, :rank] + both[:, rank:] + dot_nt(low, right_high)
        total_ref[rows, :] = jnp.where(first, term, total_ref[rows, :] + term)


def write_left(total_ref, row_sums_ref, extra_ref, out_ref):
    parts, tall, rank = out_ref.shape
    height = tall - PAD
    first = lax.broadcasted_iota(jnp.int32, (PAD, rank), 0) == 0
    stats = jnp.where(first, row_sums_ref[...], extra_ref[...])
    for part in range(parts):
        out_ref[part, :height, :] = total_ref[pl.ds(part * height, height), :]
        out_ref[part, height:, :] = stats


def turn_kernel(
    slab_ref, left_ref, right_ref, extra_ref, right_out, left_out,
    pair_ref, pair_t_ref, sums_ref, high_ref, low_ref, total_ref, row_sums_ref,
):
    step = pl.program_id(0)

    @pl.when(step == 0)
    def _():
        prepare_left(left_ref, pair_ref)
        prepare_left_t(left_ref, pair_t_ref, sums_ref)

    right = right_update(
        slab_ref, pair_ref, pair_t_ref, sums_ref, right_ref[...], high_ref, low_ref
    )
    right_out[...] = right
    left_numerator(slab_ref, pair_ref, right, total_ref, row_sums_ref, step == 0)

    @pl.when(step == pl.num_programs(0) - 1)
    def _():
        write_left(total_ref, row_sums_ref, extra_ref, left_out)


def second_quotient(block, second_left, pairs):
    high, low = split(second_left)
    right_high, right_low = pairs
    product = dot(high, right_high) + (dot(low, right_high) + dot(high, right_low))
    return split(divide(block, product)), (high, low)


def right_kernel(
    slices, slab_ref, left_ref, right_ref, second_left_ref, second_right_ref, right_out, numer_out,
    pair_ref, pair_t_ref, sums_ref, high_ref, low_ref, numer_ref,
):
    step = pl.program_id(0)

    @pl.when(step == 0)
    def _():
        prepare_left(left_ref, pair_ref)
        prepare_left_t(left_ref, pair_t_ref, sums_ref)

    right = right_update(
        slab_ref, pair_ref, pair_t_ref, sums_ref, right_ref[...], high_ref, low_ref
    )
    right_out[...] = right
    rank, k = right.shape
    second_left = second_left_ref[pl.ds(step, rank, stride=slices), :]
    second_right = jnp.concatenate(
        [second_right_ref[block] for block in range(k // rank)], axis=1
    )
    (high, low), _ = second_quotient(right, second_left, split(second_right))
    left_high, left_low = split(second_left.T)
    term = dot(left_high, high) + (dot(left_low, high) + dot(left_high, low))
    numer_ref[...] = jnp.where(step == 0, term, numer_ref[...] + term)

    @pl.when(step == pl.num_programs(0) - 1)
    def _():
        for block in range(k // rank):
            numer_out[block] = numer_ref[:, pl.ds(block * rank, rank)]


def left_kernel(slab_ref, left_ref, right_ref, left_out, pair_ref, total_ref, row_sums_ref):
    step = pl.program_id(0)

    @pl.when(step == 0)
    def _():
        prepare_left(left_ref, pair_ref)

    left_numerator(slab_ref, pair_ref, right_ref[...], total_ref, row_sums_ref, step == 0)

    @pl.when(step == pl.num_programs(0) - 1)
    def _():
        write_left(total_ref, row_sums_ref, row_sums_ref, left_out)


def second_kernel(slices, right_ref, second_left_ref, second_right_ref, out_ref):
    rank = right_ref.shape[0]
    k = right_ref.shape[1] // slices
    second_right = jnp.concatenate(
        [second_right_ref[block] for block in range(k // rank)], axis=1
    )
    right_high, right_low = split(second_right)
    right_both = jnp.concatenate([right_high, right_low], axis=0)
    sums = dot_nt(jnp.ones((16, k), BF16), right_both)[:1]
    scale = 1.0 / (sums[:, :rank] + sums[:, rank:])
    for index in range(slices):
        rows = pl.ds(index, rank, stride=slices)
        second_left = second_left_ref[rows, :]
        (high, low), _ = second_quotient(
            right_ref[:, pl.ds(index * k, k)], second_left, (right_high, right_low)
        )
        both = dot_nt(high, right_both)
        numer = both[:, :rank] + both[:, rank:] + dot_nt(low, right_high)
        out_ref[rows, :] = second_left * numer * scale


def full(shape):
    return pl.BlockSpec(shape, lambda step: (0,) * len(shape))


def params():
    return pltpu.CompilerParams(
        dimension_semantics=("arbitrary",), vmem_limit_bytes=VMEM_BYTES
    )


def left_scratch(m, rank):
    return [pltpu.VMEM((m, 2 * rank), BF16)]


def right_scratch(m, rank, block):
    return [
        pltpu.VMEM((2 * rank, m), BF16),
        pltpu.VMEM((rank, rank), F32),
        pltpu.VMEM((m, block), BF16),
        pltpu.VMEM((m, block), BF16),
    ]


def total_scratch(m, rank):
    return [pltpu.VMEM((m, rank), F32), pltpu.VMEM((PAD, rank), F32)]


def cost(m, rank, columns, dots):
    return pl.CostEstimate(
        flops=6 * dots * m * rank * columns, bytes_accessed=4 * m * columns, transcendentals=0
    )


def full_turn(slab, left, right, extra, block, parts):
    (m, columns), rank = slab.shape, left.shape[1]
    columns_spec = lambda height: pl.BlockSpec((height, block), lambda step: (0, step))
    tall = m // parts + PAD
    return pl.pallas_call(
        turn_kernel,
        grid=(columns // block,),
        in_specs=[columns_spec(m), full((m, rank)), columns_spec(rank), full((PAD, rank))],
        out_specs=[columns_spec(rank), full((parts, tall, rank))],
        out_shape=[
            jax.ShapeDtypeStruct((rank, columns), F32),
            jax.ShapeDtypeStruct((parts, tall, rank), F32),
        ],
        scratch_shapes=left_scratch(m, rank)
        + right_scratch(m, rank, block)
        + total_scratch(m, rank),
        compiler_params=params(),
        cost_estimate=cost(m, rank, columns, 4),
        name="turn",
    )(slab, left, right, extra)


def right_half(slab, left, right, second_left, second_right, block):
    (m, columns), rank = slab.shape, left.shape[1]
    slices = columns // block
    columns_spec = lambda height: pl.BlockSpec((height, block), lambda step: (0, step))
    return pl.pallas_call(
        functools.partial(right_kernel, slices),
        grid=(slices,),
        in_specs=[
            columns_spec(m), full((m, rank)), columns_spec(rank),
            full(second_left.shape), full(second_right.shape),
        ],
        out_specs=[columns_spec(rank), full(second_right.shape)],
        out_shape=[
            jax.ShapeDtypeStruct((rank, columns), F32),
            jax.ShapeDtypeStruct(second_right.shape, F32),
        ],
        scratch_shapes=left_scratch(m, rank)
        + right_scratch(m, rank, block)
        + [pltpu.VMEM((rank, block), F32)],
        compiler_params=params(),
        cost_estimate=cost(m, rank, columns, 2),
        name="right_half",
    )(slab, left, right, second_left, second_right)


def left_half(slab, left, right, block, parts):
    (m, columns), rank = slab.shape, left.shape[1]
    columns_spec = lambda height: pl.BlockSpec((height, block), lambda step: (0, step))
    tall = m // parts + PAD
    return pl.pallas_call(
        left_kernel,
        grid=(columns // block,),
        in_specs=[columns_spec(m), full((m, rank)), columns_spec(rank)],
        out_specs=full((parts, tall, rank)),
        out_shape=jax.ShapeDtypeStruct((parts, tall, rank), F32),
        scratch_shapes=left_scratch(m, rank) + total_scratch(m, rank),
        compiler_params=params(),
        cost_estimate=cost(m, rank, columns, 2),
        name="left_half",
    )(slab, left, right)


def second_rows_out(right, second_left, second_right, slices):
    return pl.pallas_call(
        functools.partial(second_kernel, slices),
        out_shape=jax.ShapeDtypeStruct(second_left.shape, F32),
        compiler_params=pltpu.CompilerParams(vmem_limit_bytes=VMEM_BYTES),
        cost_estimate=cost(right.shape[0], right.shape[0], right.shape[1], 2),
        name="second_rows",
    )(right, second_left, second_right)


def body(tensor_slab, left_init, right_init, second_left_init, second_right_init):
    row_devices = lax.axis_size("row")
    col_devices = lax.axis_size("col")
    devices = row_devices * col_devices
    own_part = (lax.axis_index("row") % 2) * col_devices + lax.axis_index("col")
    parts = 2 * col_devices
    m, rank = left_init.shape
    k = second_right_init.shape[1] * col_devices
    slices = right_init.shape[1] // k
    per_owner = rank // devices
    rows_own = m // parts

    second_rows = second_left_init.shape[0] // col_devices
    own_left = lax.dynamic_slice_in_dim(
        second_left_init, lax.axis_index("col") * second_rows, second_rows, 0
    )
    col_part = jnp.broadcast_to(jnp.sum(own_left, axis=0)[None], (PAD, rank))
    own_left = own_left.reshape(per_owner, devices, slices, rank).transpose(1, 0, 2, 3)
    second_left = exchange(own_left.reshape(devices, per_owner * slices, rank))
    second_left = second_left.reshape(rank * slices, rank)
    whole = lax.all_to_all(
        jnp.broadcast_to(second_right_init[None], (col_devices,) + second_right_init.shape),
        "col", split_axis=0, concat_axis=0, tiled=True,
    )
    whole = whole.transpose(1, 0, 2).reshape(rank, k // rank, rank).transpose(1, 0, 2)

    def new_left(left, summed):
        total = reduce_parts(summed.reshape(2, col_devices, rows_own + PAD, rank))
        own = lax.dynamic_slice_in_dim(left, own_part * rows_own, rows_own, 0)
        own = own * total[:rows_own] / total[rows_own][None, :]
        return spread_parts(own).reshape(m, rank), total[rows_own + 1]

    right, summed = full_turn(tensor_slab, left_init, right_init, col_part, k, parts)
    left, col_totals = new_left(left_init, summed)
    right, numerator = right_half(tensor_slab, left, right, second_left, whole, k)
    summed = left_half(tensor_slab, left, right, k, parts)

    rows_part = k // parts
    part = reduce_parts(numerator.reshape(2, col_devices, rows_part, rank))
    init_over = (whole / col_totals[None, :, None]).reshape(k, rank)
    part = part * lax.dynamic_slice_in_dim(init_over, own_part * rows_part, rows_part, 0)
    second_right = spread_parts(part).reshape(k // rank, rank, rank)
    rows_out = second_rows_out(right, second_left, second_right, slices)
    returned = exchange(rows_out.reshape(devices, per_owner * slices, rank))
    returned = returned.reshape(devices, per_owner, slices, rank).transpose(1, 0, 2, 3)
    left_out, _ = new_left(left, summed)
    return (left_out, returned.reshape(second_rows, rank))


def solution(mesh):
    placed = (P(None, AXES), P(), P(None, AXES), P("row", None), P(None, "col"))
    return jax.shard_map(
        body, mesh=mesh, in_specs=placed, out_specs=(P(), P(AXES, None)), check_vma=False
    )
```

```python
import functools

import jax
import jax.numpy as jnp
from jax import lax
from jax.experimental import pallas as pl
from jax.experimental.pallas import tpu as pltpu
from jax.sharding import PartitionSpec as P

AXES = ("row", "col")
F32, BF16 = jnp.float32, jnp.bfloat16
PAD = 8
VMEM_BYTES = 60 * 1024 * 1024


def exchange(parts):
    return lax.all_to_all(parts, AXES, split_axis=0, concat_axis=0, tiled=True)


def send(values, row_flip, col_flip):
    rows, cols = lax.axis_size("row"), lax.axis_size("col")
    pairs = [
        (r * cols + c, (r ^ row_flip) * cols + (c ^ col_flip))
        for r in range(rows)
        for c in range(cols)
    ]
    return lax.ppermute(values, AXES, pairs)


def pick(values, index):
    return lax.dynamic_index_in_dim(values, index, 0, keepdims=False)


def tree_sum(terms):
    while len(terms) > 1:
        terms = [a + b for a, b in zip(terms[::2], terms[1::2])]
    return terms[0]


def after(values, *events):
    return lax.optimization_barrier((values,) + events)[0]


def reduce_core(parts):
    core = lax.axis_index("row") % 2
    return pick(parts, core) + send(pick(parts, 1 - core), 1, 0)


def reduce_plane(own):
    col = lax.axis_index("col")
    others = [send(pick(own, col ^ flip), 0, flip) for flip in range(1, own.shape[0])]
    return tree_sum([pick(own, col)] + others)


def reduce_z(own):
    return tree_sum([own] + [send(own, flip, 0) for flip in range(2, lax.axis_size("row"), 2)])


def spread_plane(part):
    col, cols = lax.axis_index("col"), lax.axis_size("col")
    near = jnp.stack([part] + [send(part, 0, flip) for flip in range(1, cols)])
    return jnp.stack([pick(near, index ^ col) for index in range(cols)])


def spread_core(near):
    core = lax.axis_index("row") % 2
    both = jnp.stack([near, send(near, 1, 0)])
    return jnp.stack([pick(both, core), pick(both, 1 - core)])


def split(x):
    high = x.astype(BF16)
    return high, (x - high.astype(F32)).astype(BF16)


def dot(a, b):
    return jnp.dot(a, b, preferred_element_type=F32)


def dot_nt(a, b):
    return lax.dot_general(a, b, (((1,), (1,)), ((), ())), preferred_element_type=F32)


def divide(x, y):
    return x * pl.reciprocal(y, approx=True)


def prepare_left(left_ref, pair_ref):
    rank = left_ref.shape[1]
    high, low = split(left_ref[...])
    pair_ref[:, :rank] = high
    pair_ref[:, rank : 2 * rank] = low
    pair_ref[:, 2 * rank :] = high


def prepare_left_t(left_ref, pair_t_ref, sums_ref):
    rank = left_ref.shape[1]
    turned = left_ref[...].T
    high, low = split(turned)
    pair_t_ref[:rank, :] = high
    pair_t_ref[rank:, :] = low
    sums_ref[...] = jnp.broadcast_to(jnp.sum(turned, axis=1, keepdims=True), sums_ref.shape)


def row_chunks(m):
    size = min(256, m)
    return [pl.ds(start, size) for start in range(0, m, size)]


def quotients(slab_ref, pair_ref, right, rows):
    high, low = split(right)
    product = dot(pair_ref[rows, :], jnp.concatenate([high, high, low], axis=0))
    return split(divide(slab_ref[rows, :], product))


def right_update(slab_ref, pair_ref, pair_t_ref, sums_ref, right, high_ref, low_ref):
    rank = right.shape[0]
    for rows in row_chunks(slab_ref.shape[0]):
        high, low = quotients(slab_ref, pair_ref, right, rows)
        high_ref[rows, :] = high
        low_ref[rows, :] = low
    both = dot(pair_t_ref[...], high_ref[...])
    numerator = both[:rank] + both[rank:] + dot(pair_t_ref[:rank, :], low_ref[...])
    return right * numerator / sums_ref[:, :1]


def left_numerator(slab_ref, pair_ref, right, total_ref, sums_ref, first):
    rank = right.shape[0]
    right_high, right_low = split(right)
    right_both = jnp.concatenate([right_high, right_low], axis=0)
    ones = jnp.ones((16, right.shape[1]), BF16)
    row_sums = dot_nt(ones, right_both)[:PAD]
    row_sums = row_sums[:, :rank] + row_sums[:, rank:]
    sums_ref[...] = jnp.where(first, row_sums, sums_ref[...] + row_sums)
    for rows in row_chunks(slab_ref.shape[0]):
        high, low = quotients(slab_ref, pair_ref, right, rows)
        both = dot_nt(high, right_both)
        term = both[:, :rank] + both[:, rank:] + dot_nt(low, right_high)
        total_ref[rows, :] = jnp.where(first, term, total_ref[rows, :] + term)


def write_left(total_ref, row_sums_ref, extra_ref, out_ref):
    parts, tall, rank = out_ref.shape
    height = tall - PAD
    first = lax.broadcasted_iota(jnp.int32, (PAD, rank), 0) == 0
    stats = jnp.where(first, row_sums_ref[...], extra_ref[...])
    for part in range(parts):
        out_ref[part, :height, :] = total_ref[pl.ds(part * height, height), :]
        out_ref[part, height:, :] = stats


def turn_kernel(
    slab_ref, left_ref, right_ref, extra_ref, right_out, left_out,
    pair_ref, pair_t_ref, sums_ref, high_ref, low_ref, total_ref, row_sums_ref,
):
    step = pl.program_id(0)

    @pl.when(step == 0)
    def _():
        prepare_left(left_ref, pair_ref)
        prepare_left_t(left_ref, pair_t_ref, sums_ref)

    right = right_update(
        slab_ref, pair_ref, pair_t_ref, sums_ref, right_ref[...], high_ref, low_ref
    )
    right_out[...] = right
    left_numerator(slab_ref, pair_ref, right, total_ref, row_sums_ref, step == 0)

    @pl.when(step == pl.num_programs(0) - 1)
    def _():
        write_left(total_ref, row_sums_ref, extra_ref, left_out)


def second_quotient(block, second_left, pairs):
    high, low = split(second_left)
    right_high, right_low = pairs
    product = dot(high, right_high) + (dot(low, right_high) + dot(high, right_low))
    return split(divide(block, product)), (high, low)


def right_kernel(
    slices, slab_ref, left_ref, right_ref, second_left_ref, second_right_ref, right_out, numer_out,
    pair_ref, pair_t_ref, sums_ref, high_ref, low_ref, numer_ref,
):
    step = pl.program_id(0)

    @pl.when(step == 0)
    def _():
        prepare_left(left_ref, pair_ref)
        prepare_left_t(left_ref, pair_t_ref, sums_ref)

    right = right_update(
        slab_ref, pair_ref, pair_t_ref, sums_ref, right_ref[...], high_ref, low_ref
    )
    right_out[...] = right
    rank, k = right.shape
    second_left = second_left_ref[pl.ds(step, rank, stride=slices), :]
    second_right = jnp.concatenate(
        [second_right_ref[block] for block in range(k // rank)], axis=1
    )
    (high, low), _ = second_quotient(right, second_left, split(second_right))
    left_high, left_low = split(second_left.T)
    term = dot(left_high, high) + (dot(left_low, high) + dot(left_high, low))
    numer_ref[...] = jnp.where(step == 0, term, numer_ref[...] + term)

    @pl.when(step == pl.num_programs(0) - 1)
    def _():
        for block in range(k // rank):
            numer_out[block] = numer_ref[:, pl.ds(block * rank, rank)]


def left_kernel(slab_ref, left_ref, right_ref, left_out, pair_ref, total_ref, row_sums_ref):
    step = pl.program_id(0)

    @pl.when(step == 0)
    def _():
        prepare_left(left_ref, pair_ref)

    left_numerator(slab_ref, pair_ref, right_ref[...], total_ref, row_sums_ref, step == 0)

    @pl.when(step == pl.num_programs(0) - 1)
    def _():
        write_left(total_ref, row_sums_ref, row_sums_ref, left_out)


def second_kernel(slices, right_ref, second_left_ref, second_right_ref, out_ref):
    rank = right_ref.shape[0]
    k = right_ref.shape[1] // slices
    second_right = jnp.concatenate(
        [second_right_ref[block] for block in range(k // rank)], axis=1
    )
    right_high, right_low = split(second_right)
    right_both = jnp.concatenate([right_high, right_low], axis=0)
    sums = dot_nt(jnp.ones((16, k), BF16), right_both)[:1]
    scale = 1.0 / (sums[:, :rank] + sums[:, rank:])
    for index in range(slices):
        rows = pl.ds(index, rank, stride=slices)
        second_left = second_left_ref[rows, :]
        (high, low), _ = second_quotient(
            right_ref[:, pl.ds(index * k, k)], second_left, (right_high, right_low)
        )
        both = dot_nt(high, right_both)
        numer = both[:, :rank] + both[:, rank:] + dot_nt(low, right_high)
        out_ref[rows, :] = second_left * numer * scale


def full(shape):
    return pl.BlockSpec(shape, lambda step: (0,) * len(shape))


def params():
    return pltpu.CompilerParams(
        dimension_semantics=("arbitrary",), vmem_limit_bytes=VMEM_BYTES
    )


def left_scratch(m, rank):
    return [pltpu.VMEM((m, 3 * rank), BF16)]


def right_scratch(m, rank, block):
    return [
        pltpu.VMEM((2 * rank, m), BF16),
        pltpu.VMEM((rank, rank), F32),
        pltpu.VMEM((m, block), BF16),
        pltpu.VMEM((m, block), BF16),
    ]


def total_scratch(m, rank):
    return [pltpu.VMEM((m, rank), F32), pltpu.VMEM((PAD, rank), F32)]


def cost(m, rank, columns, dots):
    return pl.CostEstimate(
        flops=6 * dots * m * rank * columns, bytes_accessed=4 * m * columns, transcendentals=0
    )


def full_turn(slab, left, right, extra, block, parts):
    (m, columns), rank = slab.shape, left.shape[1]
    columns_spec = lambda height: pl.BlockSpec((height, block), lambda step: (0, step))
    tall = m // parts + PAD
    return pl.pallas_call(
        turn_kernel,
        grid=(columns // block,),
        in_specs=[columns_spec(m), full((m, rank)), columns_spec(rank), full((PAD, rank))],
        out_specs=[columns_spec(rank), full((parts, tall, rank))],
        out_shape=[
            jax.ShapeDtypeStruct((rank, columns), F32),
            jax.ShapeDtypeStruct((parts, tall, rank), F32),
        ],
        scratch_shapes=left_scratch(m, rank)
        + right_scratch(m, rank, block)
        + total_scratch(m, rank),
        compiler_params=params(),
        cost_estimate=cost(m, rank, columns, 4),
        name="turn",
    )(slab, left, right, extra)


def right_half(slab, left, right, second_left, second_right, block):
    (m, columns), rank = slab.shape, left.shape[1]
    slices = columns // block
    columns_spec = lambda height: pl.BlockSpec((height, block), lambda step: (0, step))
    return pl.pallas_call(
        functools.partial(right_kernel, slices),
        grid=(slices,),
        in_specs=[
            columns_spec(m), full((m, rank)), columns_spec(rank),
            full(second_left.shape), full(second_right.shape),
        ],
        out_specs=[columns_spec(rank), full(second_right.shape)],
        out_shape=[
            jax.ShapeDtypeStruct((rank, columns), F32),
            jax.ShapeDtypeStruct(second_right.shape, F32),
        ],
        scratch_shapes=left_scratch(m, rank)
        + right_scratch(m, rank, block)
        + [pltpu.VMEM((rank, block), F32)],
        compiler_params=params(),
        cost_estimate=cost(m, rank, columns, 2),
        name="right_half",
    )(slab, left, right, second_left, second_right)


def left_half(slab, left, right, block, parts):
    (m, columns), rank = slab.shape, left.shape[1]
    columns_spec = lambda height: pl.BlockSpec((height, block), lambda step: (0, step))
    tall = m // parts + PAD
    return pl.pallas_call(
        left_kernel,
        grid=(columns // block,),
        in_specs=[columns_spec(m), full((m, rank)), columns_spec(rank)],
        out_specs=full((parts, tall, rank)),
        out_shape=jax.ShapeDtypeStruct((parts, tall, rank), F32),
        scratch_shapes=left_scratch(m, rank) + total_scratch(m, rank),
        compiler_params=params(),
        cost_estimate=cost(m, rank, columns, 2),
        name="left_half",
    )(slab, left, right)


def second_rows_out(right, second_left, second_right, slices):
    return pl.pallas_call(
        functools.partial(second_kernel, slices),
        out_shape=jax.ShapeDtypeStruct(second_left.shape, F32),
        compiler_params=pltpu.CompilerParams(vmem_limit_bytes=VMEM_BYTES),
        cost_estimate=cost(right.shape[0], right.shape[0], right.shape[1], 2),
        name="second_rows",
    )(right, second_left, second_right)


def body(tensor_slab, left_init, right_init, second_left_init, second_right_init):
    row_devices = lax.axis_size("row")
    col_devices = lax.axis_size("col")
    devices = row_devices * col_devices
    own_part = (lax.axis_index("row") % 2) * col_devices + lax.axis_index("col")
    parts = 2 * col_devices
    m, rank = left_init.shape
    k = second_right_init.shape[1] * col_devices
    slices = right_init.shape[1] // k
    per_owner = rank // devices
    rows_own = m // parts

    second_rows = second_left_init.shape[0] // col_devices
    own_left = lax.dynamic_slice_in_dim(
        second_left_init, lax.axis_index("col") * second_rows, second_rows, 0
    )
    col_part = jnp.broadcast_to(jnp.sum(own_left, axis=0)[None], (PAD, rank))
    own_left = own_left.reshape(per_owner, devices, slices, rank).transpose(1, 0, 2, 3)
    own_left = own_left.reshape(devices, per_owner * slices, rank)
    piece_rows = rank // row_devices
    piece = lax.dynamic_slice_in_dim(
        second_right_init, lax.axis_index("row") * piece_rows, piece_rows, 0
    ).reshape(-1, rank)
    piece = jnp.broadcast_to(piece[None], (devices,) + piece.shape)
    arrived = exchange(jnp.concatenate([own_left, piece], axis=1))

    right, summed = full_turn(tensor_slab, left_init, right_init, col_part, k, parts)
    summed, arrived = lax.optimization_barrier((summed, arrived))
    second_left = arrived[:, : per_owner * slices].reshape(rank * slices, rank)
    whole = arrived[:, per_owner * slices :].reshape(row_devices, col_devices, piece_rows, -1)
    whole = whole.transpose(0, 2, 1, 3).reshape(rank, k // rank, rank).transpose(1, 0, 2)

    def own_left_rows(left, total):
        own = lax.dynamic_slice_in_dim(left, own_part * rows_own, rows_own, 0)
        return own * total[:rows_own] / total[rows_own][None, :]

    summed = summed.reshape(2, col_devices, rows_own + PAD, rank)
    total = reduce_z(reduce_plane(reduce_core(summed)))
    left = spread_core(spread_plane(own_left_rows(left_init, total))).reshape(m, rank)
    right, numerator = right_half(tensor_slab, left, right, second_left, whole, k)
    summed = left_half(tensor_slab, left, right, k, parts)
    summed = summed.reshape(2, col_devices, rows_own + PAD, rank)

    rows_part = k // parts
    init_over = (whole / total[rows_own + 1][None, :, None]).reshape(k, rank)
    init_over = lax.dynamic_slice_in_dim(init_over, own_part * rows_part, rows_part, 0)
    plane = reduce_plane(reduce_core(numerator.reshape(2, col_devices, rows_part, rank)))
    left_core = reduce_core(after(summed, plane))
    part = init_over * reduce_z(plane)
    left_plane = reduce_plane(after(left_core, part))
    near = spread_plane(part)
    left_total = reduce_z(after(left_plane, near))
    second_right = spread_core(near).reshape(k // rank, rank, rank)
    rows_out = second_rows_out(right, second_left, second_right, slices)
    returned = exchange(rows_out.reshape(devices, per_owner * slices, rank))
    returned = returned.reshape(devices, per_owner, slices, rank).transpose(1, 0, 2, 3)
    left_part = after(own_left_rows(left, left_total), rows_out)
    left_out = spread_core(spread_plane(left_part)).reshape(m, rank)
    return (left_out, returned.reshape(second_rows, rank))


def solution(mesh):
    placed = (P(None, AXES), P(), P(None, AXES), P("row", None), P(None, "col"))
    return jax.shard_map(
        body, mesh=mesh, in_specs=placed, out_specs=(P(), P(AXES, None)), check_vma=False
    )
```

```python
import functools

import jax
import jax.numpy as jnp
from jax import lax
from jax.experimental import pallas as pl
from jax.experimental.pallas import tpu as pltpu
from jax.sharding import PartitionSpec as P

AXES = ("row", "col")
F32, BF16 = jnp.float32, jnp.bfloat16
PAD = 8
VMEM_BYTES = 54 * 1024 * 1024


def exchange(parts):
    return lax.all_to_all(parts, AXES, split_axis=0, concat_axis=0, tiled=True)


def send(values, row_flip, col_flip):
    rows, cols = lax.axis_size("row"), lax.axis_size("col")
    pairs = [
        (r * cols + c, (r ^ row_flip) * cols + (c ^ col_flip))
        for r in range(rows)
        for c in range(cols)
    ]
    return lax.ppermute(values, AXES, pairs)


def pick(values, index):
    return lax.dynamic_index_in_dim(values, index, 0, keepdims=False)


def tree_sum(terms):
    while len(terms) > 1:
        terms = [a + b for a, b in zip(terms[::2], terms[1::2])]
    return terms[0]


def after(values, *events):
    return lax.optimization_barrier((values,) + events)[0]


def reduce_core(parts):
    core = lax.axis_index("row") % 2
    return pick(parts, core) + send(pick(parts, 1 - core), 1, 0)


def reduce_plane(own):
    col = lax.axis_index("col")
    others = [send(pick(own, col ^ flip), 0, flip) for flip in range(1, own.shape[0])]
    return tree_sum([pick(own, col)] + others)


def reduce_z(own):
    return tree_sum([own] + [send(own, flip, 0) for flip in range(2, lax.axis_size("row"), 2)])


def spread_plane(part):
    col, cols = lax.axis_index("col"), lax.axis_size("col")
    near = jnp.stack([part] + [send(part, 0, flip) for flip in range(1, cols)])
    return jnp.stack([pick(near, index ^ col) for index in range(cols)])


def spread_core(near):
    core = lax.axis_index("row") % 2
    both = jnp.stack([near, send(near, 1, 0)])
    return jnp.stack([pick(both, core), pick(both, 1 - core)])


def split(x):
    high = x.astype(BF16)
    return high, (x - high.astype(F32)).astype(BF16)


def dot(a, b):
    return jnp.dot(a, b, preferred_element_type=F32)


def dot_nt(a, b):
    return lax.dot_general(a, b, (((1,), (1,)), ((), ())), preferred_element_type=F32)


def divide(x, y):
    return x * pl.reciprocal(y, approx=True)


def prepare_left(left_ref, pair_ref):
    rank = left_ref.shape[1]
    high, low = split(left_ref[...])
    pair_ref[:, :rank] = high
    pair_ref[:, rank : 2 * rank] = low
    pair_ref[:, 2 * rank :] = high


def prepare_left_t(left_ref, pair_t_ref, sums_ref):
    rank = left_ref.shape[1]
    turned = left_ref[...].T
    high, low = split(turned)
    pair_t_ref[:rank, :] = high
    pair_t_ref[rank:, :] = low
    sums_ref[...] = jnp.broadcast_to(jnp.sum(turned, axis=1, keepdims=True), sums_ref.shape)


def row_chunks(m):
    size = min(256, m)
    return [pl.ds(start, size) for start in range(0, m, size)]


def quotients(slab_ref, pair_ref, right, rows):
    high, low = split(right)
    product = dot(pair_ref[rows, :], jnp.concatenate([high, high, low], axis=0))
    return split(divide(slab_ref[rows, :], product))


def right_update(slab_ref, pair_ref, pair_t_ref, sums_ref, right, high_ref, low_ref):
    rank = right.shape[0]
    for rows in row_chunks(slab_ref.shape[0]):
        high, low = quotients(slab_ref, pair_ref, right, rows)
        high_ref[rows, :] = high
        low_ref[rows, :] = low
    both = dot(pair_t_ref[...], high_ref[...])
    numerator = both[:rank] + both[rank:] + dot(pair_t_ref[:rank, :], low_ref[...])
    return right * numerator / sums_ref[:, :1]


def left_numerator(slab_ref, pair_ref, right, total_ref, sums_ref, first):
    rank = right.shape[0]
    right_high, right_low = split(right)
    right_both = jnp.concatenate([right_high, right_low], axis=0)
    ones = jnp.ones((16, right.shape[1]), BF16)
    row_sums = dot_nt(ones, right_both)[:PAD]
    row_sums = row_sums[:, :rank] + row_sums[:, rank:]
    sums_ref[...] = jnp.where(first, row_sums, sums_ref[...] + row_sums)
    for rows in row_chunks(slab_ref.shape[0]):
        high, low = quotients(slab_ref, pair_ref, right, rows)
        both = dot_nt(high, right_both)
        term = both[:, :rank] + both[:, rank:] + dot_nt(low, right_high)
        total_ref[rows, :] = jnp.where(first, term, total_ref[rows, :] + term)


def write_left(total_ref, row_sums_ref, extra_ref, out_ref):
    parts, tall, rank = out_ref.shape
    height = tall - PAD
    first = lax.broadcasted_iota(jnp.int32, (PAD, rank), 0) == 0
    stats = jnp.where(first, row_sums_ref[...], extra_ref[...])
    for part in range(parts):
        out_ref[part, :height, :] = total_ref[pl.ds(part * height, height), :]
        out_ref[part, height:, :] = stats


def turn_kernel(
    slab_ref, left_ref, right_ref, extra_ref, right_out, left_out,
    pair_ref, pair_t_ref, sums_ref, high_ref, low_ref, total_ref, row_sums_ref,
):
    step = pl.program_id(0)

    @pl.when(step == 0)
    def _():
        prepare_left(left_ref, pair_ref)
        prepare_left_t(left_ref, pair_t_ref, sums_ref)

    right = right_update(
        slab_ref, pair_ref, pair_t_ref, sums_ref, right_ref[...], high_ref, low_ref
    )
    right_out[...] = right
    left_numerator(slab_ref, pair_ref, right, total_ref, row_sums_ref, step == 0)

    @pl.when(step == pl.num_programs(0) - 1)
    def _():
        write_left(total_ref, row_sums_ref, extra_ref, left_out)


def second_quotient(block, second_left, pairs):
    high, low = split(second_left)
    right_high, right_low = pairs
    product = dot(high, right_high) + (dot(low, right_high) + dot(high, right_low))
    return split(divide(block, product))


def numerator_kernel(slices, right_ref, second_left_ref, second_right_ref, numer_out):
    rank = right_ref.shape[0]
    k = right_ref.shape[1] // slices
    pairs = split(
        jnp.concatenate([second_right_ref[block] for block in range(k // rank)], axis=1)
    )
    total = 0.0
    for index in range(slices):
        second_left = second_left_ref[pl.ds(index, rank, stride=slices), :]
        high, low = second_quotient(right_ref[:, pl.ds(index * k, k)], second_left, pairs)
        left_high, left_low = split(second_left.T)
        total = total + (dot(left_high, high) + (dot(left_low, high) + dot(left_high, low)))
    for block in range(k // rank):
        numer_out[block] = total[:, block * rank : (block + 1) * rank]


def second_kernel(slices, right_ref, second_left_ref, second_right_ref, out_ref):
    rank = right_ref.shape[0]
    k = right_ref.shape[1] // slices
    second_right = jnp.concatenate(
        [second_right_ref[block] for block in range(k // rank)], axis=1
    )
    right_high, right_low = split(second_right)
    right_both = jnp.concatenate([right_high, right_low], axis=0)
    sums = dot_nt(jnp.ones((16, k), BF16), right_both)[:1]
    scale = 1.0 / (sums[:, :rank] + sums[:, rank:])
    for index in range(slices):
        rows = pl.ds(index, rank, stride=slices)
        second_left = second_left_ref[rows, :]
        high, low = second_quotient(
            right_ref[:, pl.ds(index * k, k)], second_left, (right_high, right_low)
        )
        both = dot_nt(high, right_both)
        numer = both[:, :rank] + both[:, rank:] + dot_nt(low, right_high)
        out_ref[rows, :] = second_left * numer * scale


def full(shape):
    return pl.BlockSpec(shape, lambda step: (0,) * len(shape))


def params():
    return pltpu.CompilerParams(
        dimension_semantics=("arbitrary",), vmem_limit_bytes=VMEM_BYTES
    )


def left_scratch(m, rank):
    return [pltpu.VMEM((m, 3 * rank), BF16)]


def right_scratch(m, rank, block):
    return [
        pltpu.VMEM((2 * rank, m), BF16),
        pltpu.VMEM((rank, rank), F32),
        pltpu.VMEM((m, block), BF16),
        pltpu.VMEM((m, block), BF16),
    ]


def total_scratch(m, rank):
    return [pltpu.VMEM((m, rank), F32), pltpu.VMEM((PAD, rank), F32)]


def cost(m, rank, columns, dots):
    return pl.CostEstimate(
        flops=6 * dots * m * rank * columns, bytes_accessed=4 * m * columns, transcendentals=0
    )


def full_turn(slab, left, right, extra, block, parts):
    (m, columns), rank = slab.shape, left.shape[1]
    columns_spec = lambda height: pl.BlockSpec((height, block), lambda step: (0, step))
    tall = m // parts + PAD
    return pl.pallas_call(
        turn_kernel,
        grid=(columns // block,),
        in_specs=[columns_spec(m), full((m, rank)), columns_spec(rank), full((PAD, rank))],
        out_specs=[columns_spec(rank), full((parts, tall, rank))],
        out_shape=[
            jax.ShapeDtypeStruct((rank, columns), F32),
            jax.ShapeDtypeStruct((parts, tall, rank), F32),
        ],
        scratch_shapes=left_scratch(m, rank)
        + right_scratch(m, rank, block)
        + total_scratch(m, rank),
        compiler_params=params(),
        cost_estimate=cost(m, rank, columns, 4),
        name="turn",
    )(slab, left, right, extra)


def second_numerator(right, second_left, second_right, slices):
    return pl.pallas_call(
        functools.partial(numerator_kernel, slices),
        out_shape=jax.ShapeDtypeStruct(second_right.shape, F32),
        compiler_params=pltpu.CompilerParams(vmem_limit_bytes=VMEM_BYTES),
        cost_estimate=cost(right.shape[0], right.shape[0], right.shape[1], 2),
        name="second_numerator",
    )(right, second_left, second_right)


def second_rows_out(right, second_left, second_right, slices):
    return pl.pallas_call(
        functools.partial(second_kernel, slices),
        out_shape=jax.ShapeDtypeStruct(second_left.shape, F32),
        compiler_params=pltpu.CompilerParams(vmem_limit_bytes=VMEM_BYTES),
        cost_estimate=cost(right.shape[0], right.shape[0], right.shape[1], 2),
        name="second_rows",
    )(right, second_left, second_right)


def body(tensor_slab, left_init, right_init, second_left_init, second_right_init):
    row_devices = lax.axis_size("row")
    col_devices = lax.axis_size("col")
    devices = row_devices * col_devices
    own_part = (lax.axis_index("row") % 2) * col_devices + lax.axis_index("col")
    parts = 2 * col_devices
    m, rank = left_init.shape
    k = second_right_init.shape[1] * col_devices
    slices = right_init.shape[1] // k
    per_owner = rank // devices
    rows_own = m // parts

    second_rows = second_left_init.shape[0] // col_devices
    own_left = lax.dynamic_slice_in_dim(
        second_left_init, lax.axis_index("col") * second_rows, second_rows, 0
    )
    col_part = jnp.broadcast_to(jnp.sum(own_left, axis=0)[None], (PAD, rank))
    own_left = own_left.reshape(per_owner, devices, slices, rank).transpose(1, 0, 2, 3)
    own_left = own_left.reshape(devices, per_owner * slices, rank)
    piece_rows = rank // row_devices
    piece = lax.dynamic_slice_in_dim(
        second_right_init, lax.axis_index("row") * piece_rows, piece_rows, 0
    ).reshape(-1, rank)
    piece = jnp.broadcast_to(piece[None], (devices,) + piece.shape)
    second_factors = jnp.concatenate([own_left, piece], axis=1)

    def own_left_rows(left, total):
        own = lax.dynamic_slice_in_dim(left, own_part * rows_own, rows_own, 0)
        return own * total[:rows_own] / total[rows_own][None, :]

    right, summed = full_turn(tensor_slab, left_init, right_init, left_init, k, parts)
    summed = summed.reshape(2, col_devices, rows_own + PAD, rank)
    total = reduce_z(reduce_plane(reduce_core(summed)))
    left = spread_core(spread_plane(own_left_rows(left_init, total))).reshape(m, rank)

    arrived = exchange(after(second_factors, left))
    right, summed = full_turn(tensor_slab, left, right, col_part, k, parts)
    arrived = after(arrived, summed)
    second_left = arrived[:, : per_owner * slices].reshape(rank * slices, rank)
    whole = arrived[:, per_owner * slices :].reshape(row_devices, col_devices, piece_rows, -1)
    whole = whole.transpose(0, 2, 1, 3).reshape(rank, k // rank, rank).transpose(1, 0, 2)
    numerator = second_numerator(right, second_left, whole, slices)

    rows_part = k // parts
    summed = summed.reshape(2, col_devices, rows_own + PAD, rank)
    numerator = numerator.reshape(2, col_devices, rows_part, rank)
    total = reduce_z(reduce_plane(reduce_core(jnp.concatenate([summed, numerator], axis=2))))
    init_over = (whole / total[rows_own + 1][None, :, None]).reshape(k, rank)
    init_over = lax.dynamic_slice_in_dim(init_over, own_part * rows_part, rows_part, 0)
    second_part = init_over * total[rows_own + PAD :]
    both = spread_core(
        spread_plane(jnp.concatenate([own_left_rows(left, total), second_part], axis=0))
    )
    left_out = both[:, :, :rows_own].reshape(m, rank)
    second_right = both[:, :, rows_own:].reshape(k // rank, rank, rank)
    rows_out = second_rows_out(right, second_left, second_right, slices)
    returned = exchange(rows_out.reshape(devices, per_owner * slices, rank))
    returned = returned.reshape(devices, per_owner, slices, rank).transpose(1, 0, 2, 3)
    return (left_out, returned.reshape(second_rows, rank))


def solution(mesh):
    placed = (P(None, AXES), P(), P(None, AXES), P("row", None), P(None, "col"))
    return jax.shard_map(
        body, mesh=mesh, in_specs=placed, out_specs=(P(), P(AXES, None)), check_vma=False
    )
```

```python
import functools

import jax
import jax.numpy as jnp
from jax import lax
from jax.experimental import pallas as pl
from jax.experimental.pallas import tpu as pltpu
from jax.sharding import PartitionSpec as P

AXES = ("row", "col")
F32, BF16 = jnp.float32, jnp.bfloat16
PAD = 8
VMEM_BYTES = 48 * 1024 * 1024


def exchange(parts):
    return lax.all_to_all(parts, AXES, split_axis=0, concat_axis=0, tiled=True)


def send(values, row_flip, col_flip):
    rows, cols = lax.axis_size("row"), lax.axis_size("col")
    pairs = [
        (r * cols + c, (r ^ row_flip) * cols + (c ^ col_flip))
        for r in range(rows)
        for c in range(cols)
    ]
    return lax.ppermute(values, AXES, pairs)


def pick(values, index):
    return lax.dynamic_index_in_dim(values, index, 0, keepdims=False)


def tree_sum(terms):
    while len(terms) > 1:
        terms = [a + b for a, b in zip(terms[::2], terms[1::2])]
    return terms[0]


def after(values, *events):
    return lax.optimization_barrier((values,) + events)[0]


def reduce_core(parts):
    core = lax.axis_index("row") % 2
    return pick(parts, core) + send(pick(parts, 1 - core), 1, 0)


def reduce_plane(own):
    col = lax.axis_index("col")
    others = [send(pick(own, col ^ flip), 0, flip) for flip in range(1, own.shape[0])]
    return tree_sum([pick(own, col)] + others)


def reduce_z(own):
    return tree_sum([own] + [send(own, flip, 0) for flip in range(2, lax.axis_size("row"), 2)])


def spread_plane(part):
    col, cols = lax.axis_index("col"), lax.axis_size("col")
    near = jnp.stack([part] + [send(part, 0, flip) for flip in range(1, cols)])
    return jnp.stack([pick(near, index ^ col) for index in range(cols)])


def spread_core(near):
    core = lax.axis_index("row") % 2
    both = jnp.stack([near, send(near, 1, 0)])
    return jnp.stack([pick(both, core), pick(both, 1 - core)])


def split(x):
    high = x.astype(BF16)
    return high, (x - high.astype(F32)).astype(BF16)


def dot(a, b):
    return jnp.dot(a, b, preferred_element_type=F32)


def dot_nt(a, b):
    return lax.dot_general(a, b, (((1,), (1,)), ((), ())), preferred_element_type=F32)


def divide(x, y):
    return x * pl.reciprocal(y, approx=True)


def prepare_left(left_ref, pair_ref):
    rank = left_ref.shape[1]
    high, low = split(left_ref[...])
    pair_ref[:, :rank] = high
    pair_ref[:, rank : 2 * rank] = low
    pair_ref[:, 2 * rank :] = high


def prepare_left_t(left_ref, pair_t_ref, sums_ref):
    rank = left_ref.shape[1]
    turned = left_ref[...].T
    high, low = split(turned)
    pair_t_ref[:rank, :] = high
    pair_t_ref[rank:, :] = low
    sums_ref[...] = jnp.broadcast_to(jnp.sum(turned, axis=1, keepdims=True), sums_ref.shape)


def chunks(extent, size):
    size = min(size, extent)
    return [pl.ds(start, size) for start in range(0, extent, size)]


def stacked(right):
    high, low = split(right)
    return jnp.concatenate([high, high, low], axis=0)


def quotients(slab_ref, pair_ref, right_stack, rows, columns):
    product = dot(pair_ref[rows, :], right_stack)
    return split(divide(slab_ref[rows, columns], product))


def right_update(
    slab_ref, pair_ref, pair_t_ref, sums_ref, right_ref, right_out, high_ref, low_ref
):
    m, block = slab_ref.shape
    rank = right_ref.shape[0]
    for columns in chunks(block, 256):
        right = right_ref[:, columns]
        stack = stacked(right)
        for rows in chunks(m, 512):
            high, low = quotients(slab_ref, pair_ref, stack, rows, columns)
            high_ref[rows, columns] = high
            low_ref[rows, columns] = low
        both = dot(pair_t_ref[...], high_ref[:, columns])
        numerator = both[:rank] + both[rank:]
        numerator = numerator + dot(pair_t_ref[:rank, :], low_ref[:, columns])
        right_out[:, columns] = right * numerator / sums_ref[:, :1]


def left_numerator(slab_ref, pair_ref, right, total_ref, sums_ref, first):
    rank = right.shape[0]
    right_high, right_low = split(right)
    right_both = jnp.concatenate([right_high, right_low], axis=0)
    ones = jnp.ones((16, right.shape[1]), BF16)
    row_sums = dot_nt(ones, right_both)[:PAD]
    row_sums = row_sums[:, :rank] + row_sums[:, rank:]
    sums_ref[...] = jnp.where(first, row_sums, sums_ref[...] + row_sums)
    stack = stacked(right)
    for rows in chunks(slab_ref.shape[0], 256):
        high, low = quotients(slab_ref, pair_ref, stack, rows, slice(None))
        both = dot_nt(high, right_both)
        term = both[:, :rank] + both[:, rank:] + dot_nt(low, right_high)
        total_ref[rows, :] = jnp.where(first, term, total_ref[rows, :] + term)


def write_left(total_ref, row_sums_ref, extra_ref, out_ref):
    parts, tall, rank = out_ref.shape
    height = tall - PAD
    first = lax.broadcasted_iota(jnp.int32, (PAD, rank), 0) == 0
    stats = jnp.where(first, row_sums_ref[...], extra_ref[:1, :])
    for part in range(parts):
        out_ref[part, :height, :] = total_ref[pl.ds(part * height, height), :]
        out_ref[part, height:, :] = stats


def turn_kernel(
    slab_ref, left_ref, right_ref, extra_ref, right_out, left_out,
    pair_ref, pair_t_ref, sums_ref, high_ref, low_ref, total_ref, row_sums_ref,
):
    step = pl.program_id(0)

    @pl.when(step == 0)
    def _():
        prepare_left(left_ref, pair_ref)
        prepare_left_t(left_ref, pair_t_ref, sums_ref)

    right_update(
        slab_ref, pair_ref, pair_t_ref, sums_ref, right_ref, right_out, high_ref, low_ref
    )
    left_numerator(slab_ref, pair_ref, right_out[...], total_ref, row_sums_ref, step == 0)

    @pl.when(step == pl.num_programs(0) - 1)
    def _():
        write_left(total_ref, row_sums_ref, extra_ref, left_out)


def second_quotient(block, second_left, pairs):
    high, low = split(second_left)
    right_high, right_low = pairs
    product = dot(high, right_high) + (dot(low, right_high) + dot(high, right_low))
    return split(divide(block, product))


def numerator_kernel(slices, right_ref, second_left_ref, second_right_ref, numer_out):
    rank = right_ref.shape[0]
    k = right_ref.shape[1] // slices
    pairs = split(
        jnp.concatenate([second_right_ref[block] for block in range(k // rank)], axis=1)
    )
    total = 0.0
    for index in range(slices):
        second_left = second_left_ref[pl.ds(index, rank, stride=slices), :]
        high, low = second_quotient(right_ref[:, pl.ds(index * k, k)], second_left, pairs)
        left_high, left_low = split(second_left.T)
        total = total + (dot(left_high, high) + (dot(left_low, high) + dot(left_high, low)))
    for block in range(k // rank):
        numer_out[block] = total[:, block * rank : (block + 1) * rank]


def second_kernel(slices, right_ref, second_left_ref, second_right_ref, out_ref):
    rank = right_ref.shape[0]
    k = right_ref.shape[1] // slices
    second_right = jnp.concatenate(
        [second_right_ref[block] for block in range(k // rank)], axis=1
    )
    right_high, right_low = split(second_right)
    right_both = jnp.concatenate([right_high, right_low], axis=0)
    sums = dot_nt(jnp.ones((16, k), BF16), right_both)[:1]
    scale = 1.0 / (sums[:, :rank] + sums[:, rank:])
    for index in range(slices):
        rows = pl.ds(index, rank, stride=slices)
        second_left = second_left_ref[rows, :]
        high, low = second_quotient(
            right_ref[:, pl.ds(index * k, k)], second_left, (right_high, right_low)
        )
        both = dot_nt(high, right_both)
        numer = both[:, :rank] + both[:, rank:] + dot_nt(low, right_high)
        out_ref[rows, :] = second_left * numer * scale


def full(shape):
    return pl.BlockSpec(shape, lambda step: (0,) * len(shape))


def params():
    return pltpu.CompilerParams(
        dimension_semantics=("arbitrary",), vmem_limit_bytes=VMEM_BYTES
    )


def left_scratch(m, rank):
    return [pltpu.VMEM((m, 3 * rank), BF16)]


def right_scratch(m, rank, block):
    return [
        pltpu.VMEM((2 * rank, m), BF16),
        pltpu.VMEM((rank, rank), F32),
        pltpu.VMEM((m, block), BF16),
        pltpu.VMEM((m, block), BF16),
    ]


def total_scratch(m, rank):
    return [pltpu.VMEM((m, rank), F32), pltpu.VMEM((PAD, rank), F32)]


def cost(m, rank, columns, dots):
    return pl.CostEstimate(
        flops=6 * dots * m * rank * columns, bytes_accessed=4 * m * columns, transcendentals=0
    )


def full_turn(slab, left, right, extra, block, parts):
    (m, columns), rank = slab.shape, left.shape[1]
    columns_spec = lambda height: pl.BlockSpec((height, block), lambda step: (0, step))
    tall = m // parts + PAD
    return pl.pallas_call(
        turn_kernel,
        grid=(columns // block,),
        in_specs=[columns_spec(m), full((m, rank)), columns_spec(rank), full((min(PAD, extra.shape[0]), rank))],
        out_specs=[columns_spec(rank), full((parts, tall, rank))],
        out_shape=[
            jax.ShapeDtypeStruct((rank, columns), F32),
            jax.ShapeDtypeStruct((parts, tall, rank), F32),
        ],
        scratch_shapes=left_scratch(m, rank)
        + right_scratch(m, rank, block)
        + total_scratch(m, rank),
        compiler_params=params(),
        cost_estimate=cost(m, rank, columns, 4),
        name="turn",
    )(slab, left, right, extra)


def second_numerator(right, second_left, second_right, slices):
    return pl.pallas_call(
        functools.partial(numerator_kernel, slices),
        out_shape=jax.ShapeDtypeStruct(second_right.shape, F32),
        compiler_params=pltpu.CompilerParams(vmem_limit_bytes=VMEM_BYTES),
        cost_estimate=cost(right.shape[0], right.shape[0], right.shape[1], 2),
        name="second_numerator",
    )(right, second_left, second_right)


def second_rows_out(right, second_left, second_right, slices):
    return pl.pallas_call(
        functools.partial(second_kernel, slices),
        out_shape=jax.ShapeDtypeStruct(second_left.shape, F32),
        compiler_params=pltpu.CompilerParams(vmem_limit_bytes=VMEM_BYTES),
        cost_estimate=cost(right.shape[0], right.shape[0], right.shape[1], 2),
        name="second_rows",
    )(right, second_left, second_right)


def body(tensor_slab, left_init, right_init, second_left_init, second_right_init):
    row_devices = lax.axis_size("row")
    col_devices = lax.axis_size("col")
    devices = row_devices * col_devices
    own_part = (lax.axis_index("row") % 2) * col_devices + lax.axis_index("col")
    parts = 2 * col_devices
    m, rank = left_init.shape
    k = second_right_init.shape[1] * col_devices
    slices = right_init.shape[1] // k
    per_owner = rank // devices
    rows_own = m // parts

    second_rows = second_left_init.shape[0] // col_devices
    own_left = lax.dynamic_slice_in_dim(
        second_left_init, lax.axis_index("col") * second_rows, second_rows, 0
    )
    col_part = jnp.sum(own_left, axis=0)[None]
    own_left = own_left.reshape(per_owner, devices, slices, rank).transpose(1, 0, 2, 3)
    own_left = own_left.reshape(devices, per_owner * slices, rank)
    piece_rows = rank // row_devices
    piece = lax.dynamic_slice_in_dim(
        second_right_init, lax.axis_index("row") * piece_rows, piece_rows, 0
    ).reshape(-1, rank)
    piece = jnp.broadcast_to(piece[None], (devices,) + piece.shape)
    second_factors = jnp.concatenate([own_left, piece], axis=1)

    def own_left_rows(left, total):
        own = lax.dynamic_slice_in_dim(left, own_part * rows_own, rows_own, 0)
        return own * total[:rows_own] / total[rows_own][None, :]

    right, summed = full_turn(tensor_slab, left_init, right_init, left_init, k, parts)
    summed = summed.reshape(2, col_devices, rows_own + PAD, rank)
    total = reduce_z(reduce_plane(reduce_core(summed)))
    left = spread_core(spread_plane(own_left_rows(left_init, total))).reshape(m, rank)

    arrived = exchange(after(second_factors, left))
    right, summed = full_turn(tensor_slab, left, right, col_part, k, parts)
    arrived = after(arrived, summed)
    second_left = arrived[:, : per_owner * slices].reshape(rank * slices, rank)
    whole = arrived[:, per_owner * slices :].reshape(row_devices, col_devices, piece_rows, -1)
    whole = whole.transpose(0, 2, 1, 3).reshape(rank, k // rank, rank).transpose(1, 0, 2)
    numerator = second_numerator(right, second_left, whole, slices)

    rows_part = k // parts
    summed = summed.reshape(2, col_devices, rows_own + PAD, rank)
    numerator = numerator.reshape(2, col_devices, rows_part, rank)
    total = reduce_z(reduce_plane(reduce_core(jnp.concatenate([summed, numerator], axis=2))))
    init_over = (whole / total[rows_own + 1][None, :, None]).reshape(k, rank)
    init_over = lax.dynamic_slice_in_dim(init_over, own_part * rows_part, rows_part, 0)
    second_part = init_over * total[rows_own + PAD :]
    both = spread_core(
        spread_plane(jnp.concatenate([own_left_rows(left, total), second_part], axis=0))
    )
    left_out = both[:, :, :rows_own].reshape(m, rank)
    second_right = both[:, :, rows_own:].reshape(k // rank, rank, rank)
    rows_out = second_rows_out(right, second_left, second_right, slices)
    returned = exchange(rows_out.reshape(devices, per_owner * slices, rank))
    returned = returned.reshape(devices, per_owner, slices, rank).transpose(1, 0, 2, 3)
    return (left_out, returned.reshape(second_rows, rank))


def solution(mesh):
    placed = (P(None, AXES), P(), P(None, AXES), P("row", None), P(None, "col"))
    return jax.shard_map(
        body, mesh=mesh, in_specs=placed, out_specs=(P(), P(AXES, None)), check_vma=False
    )
```

```python
import functools

import jax
import jax.numpy as jnp
from jax import lax
from jax.experimental import pallas as pl
from jax.experimental.pallas import tpu as pltpu
from jax.sharding import PartitionSpec as P

AXES = ("row", "col")
F32, BF16 = jnp.float32, jnp.bfloat16
PAD = 8
ROWS = 1024
MIB = 1024 * 1024
VMEM_BYTES = 48 * MIB


def exchange(parts):
    return lax.all_to_all(parts, AXES, split_axis=0, concat_axis=0, tiled=True)


def send(values, row_flip, col_flip):
    rows, cols = lax.axis_size("row"), lax.axis_size("col")
    pairs = [
        (r * cols + c, (r ^ row_flip) * cols + (c ^ col_flip))
        for r in range(rows)
        for c in range(cols)
    ]
    return lax.ppermute(values, AXES, pairs)


def pick(values, index):
    return lax.dynamic_index_in_dim(values, index, 0, keepdims=False)


def tree_sum(terms):
    while len(terms) > 1:
        terms = [a + b for a, b in zip(terms[::2], terms[1::2])]
    return terms[0]


def after(values, *events):
    return lax.optimization_barrier((values,) + events)[0]


def reduce_core(parts):
    core = lax.axis_index("row") % 2
    return pick(parts, core) + send(pick(parts, 1 - core), 1, 0)


def reduce_plane(own):
    col = lax.axis_index("col")
    others = [send(pick(own, col ^ flip), 0, flip) for flip in range(1, own.shape[0])]
    return tree_sum([pick(own, col)] + others)


def reduce_z(own):
    return tree_sum([own] + [send(own, flip, 0) for flip in range(2, lax.axis_size("row"), 2)])


def spread_plane(part):
    col, cols = lax.axis_index("col"), lax.axis_size("col")
    near = jnp.stack([part] + [send(part, 0, flip) for flip in range(1, cols)])
    return jnp.stack([pick(near, index ^ col) for index in range(cols)])


def spread_core(near):
    core = lax.axis_index("row") % 2
    both = jnp.stack([near, send(near, 1, 0)])
    return jnp.stack([pick(both, core), pick(both, 1 - core)])


def split(x):
    high = x.astype(BF16)
    return high, (x - high.astype(F32)).astype(BF16)


def dot(a, b):
    return jnp.dot(a, b, preferred_element_type=F32)


def dot_nt(a, b):
    return lax.dot_general(a, b, (((1,), (1,)), ((), ())), preferred_element_type=F32)


def divide(x, y):
    return x * pl.reciprocal(y, approx=True)


def prepare_left(left_ref, pair_ref):
    rank = left_ref.shape[1]
    high, low = split(left_ref[...])
    pair_ref[:, :rank] = high
    pair_ref[:, rank : 2 * rank] = low
    pair_ref[:, 2 * rank :] = high


def prepare_left_t(left_ref, pair_t_ref, sums_ref):
    rank = left_ref.shape[1]
    turned = left_ref[...].T
    high, low = split(turned)
    pair_t_ref[:rank, :] = high
    pair_t_ref[rank:, :] = low
    sums_ref[...] = jnp.broadcast_to(jnp.sum(turned, axis=1, keepdims=True), sums_ref.shape)


def chunks(extent, size):
    size = min(size, extent)
    return [pl.ds(start, size) for start in range(0, extent, size)]


def stacked(right):
    high, low = split(right)
    return jnp.concatenate([high, high, low], axis=0)


def quotients(slab_ref, pair_ref, right_stack, rows, columns):
    product = dot(pair_ref[rows, :], right_stack)
    return split(divide(slab_ref[rows, columns], product))


def right_update(
    slab_ref, pair_ref, pair_t_ref, sums_ref, right_ref, high_ref, low_ref, columns
):
    rank = right_ref.shape[0]
    right = right_ref[:, columns]
    stack = stacked(right)
    for rows in chunks(slab_ref.shape[0], ROWS):
        high, low = quotients(slab_ref, pair_ref, stack, rows, columns)
        high_ref[rows, columns] = high
        low_ref[rows, columns] = low
    both = dot(pair_t_ref[...], high_ref[:, columns])
    numerator = both[:rank] + both[rank:]
    numerator = numerator + dot(pair_t_ref[:rank, :], low_ref[:, columns])
    return right * numerator / sums_ref[:, :1]


def left_numerator(slab_ref, pair_ref, right, total_ref, sums_ref, high_ref, low_ref, columns, first):
    rank = right.shape[0]
    turned_high, turned_low = split(right.T)
    turned = jnp.concatenate([turned_high, turned_low], axis=1)
    row_sums = dot(jnp.ones((16, right.shape[1]), BF16), turned)[:PAD]
    row_sums = row_sums[:, :rank] + row_sums[:, rank:]
    sums_ref[...] = jnp.where(first, row_sums, sums_ref[...] + row_sums)
    stack = stacked(right)
    for rows in chunks(slab_ref.shape[0], ROWS):
        high, low = quotients(slab_ref, pair_ref, stack, rows, columns)
        high_ref[rows, columns] = high
        low_ref[rows, columns] = low
    both = dot(high_ref[:, columns], turned)
    term = both[:, :rank] + both[:, rank:] + dot(low_ref[:, columns], turned_high)
    total_ref[...] = jnp.where(first, term, total_ref[...] + term)


def write_left(total_ref, row_sums_ref, extra_ref, out_ref):
    parts, tall, rank = out_ref.shape
    height = tall - PAD
    first = lax.broadcasted_iota(jnp.int32, (PAD, rank), 0) == 0
    stats = jnp.where(first, row_sums_ref[...], extra_ref[:1, :])
    for part in range(parts):
        out_ref[part, :height, :] = total_ref[pl.ds(part * height, height), :]
        out_ref[part, height:, :] = stats


def turn_kernel(
    slab_ref, left_ref, right_ref, extra_ref, right_out, left_out,
    pair_ref, pair_t_ref, sums_ref, high_ref, low_ref, high2_ref, low2_ref, total_ref, row_sums_ref,
):
    step = pl.program_id(0)

    @pl.when(step == 0)
    def _():
        prepare_left(left_ref, pair_ref)
        prepare_left_t(left_ref, pair_t_ref, sums_ref)

    for index, columns in enumerate(chunks(slab_ref.shape[1], 256)):
        right = right_update(
            slab_ref, pair_ref, pair_t_ref, sums_ref, right_ref, high_ref, low_ref, columns
        )
        right_out[:, columns] = right
        left_numerator(
            slab_ref, pair_ref, right, total_ref, row_sums_ref, high2_ref, low2_ref, columns,
            (step == 0) if index == 0 else False,
        )

    @pl.when(step == pl.num_programs(0) - 1)
    def _():
        write_left(total_ref, row_sums_ref, extra_ref, left_out)


def second_quotient(block, second_left, pairs):
    high, low = split(second_left)
    right_high, right_low = pairs
    product = dot(high, right_high) + (dot(low, right_high) + dot(high, right_low))
    return split(divide(block, product))


def numerator_kernel(slices, right_ref, second_left_ref, second_right_ref, numer_out):
    rank = right_ref.shape[0]
    k = right_ref.shape[1] // slices
    pairs = split(
        jnp.concatenate([second_right_ref[block] for block in range(k // rank)], axis=1)
    )
    total = 0.0
    for index in range(slices):
        second_left = second_left_ref[pl.ds(index, rank, stride=slices), :]
        high, low = second_quotient(right_ref[:, pl.ds(index * k, k)], second_left, pairs)
        left_high, left_low = split(second_left.T)
        total = total + (dot(left_high, high) + (dot(left_low, high) + dot(left_high, low)))
    for block in range(k // rank):
        numer_out[block] = total[:, block * rank : (block + 1) * rank]


def second_kernel(slices, right_ref, second_left_ref, second_right_ref, out_ref):
    rank = right_ref.shape[0]
    k = right_ref.shape[1] // slices
    second_right = jnp.concatenate(
        [second_right_ref[block] for block in range(k // rank)], axis=1
    )
    right_high, right_low = split(second_right)
    right_both = jnp.concatenate([right_high, right_low], axis=0)
    sums = dot_nt(jnp.ones((16, k), BF16), right_both)[:1]
    scale = 1.0 / (sums[:, :rank] + sums[:, rank:])
    for index in range(slices):
        rows = pl.ds(index, rank, stride=slices)
        second_left = second_left_ref[rows, :]
        high, low = second_quotient(
            right_ref[:, pl.ds(index * k, k)], second_left, (right_high, right_low)
        )
        both = dot_nt(high, right_both)
        numer = both[:, :rank] + both[:, rank:] + dot_nt(low, right_high)
        out_ref[rows, :] = second_left * numer * scale


def full(shape):
    return pl.BlockSpec(shape, lambda step: (0,) * len(shape))


def params(vmem_bytes):
    return pltpu.CompilerParams(
        dimension_semantics=("arbitrary",), vmem_limit_bytes=vmem_bytes
    )


def left_scratch(m, rank):
    return [pltpu.VMEM((m, 3 * rank), BF16)]


def right_scratch(m, rank, block):
    return [
        pltpu.VMEM((2 * rank, m), BF16),
        pltpu.VMEM((rank, rank), F32),
    ] + [pltpu.VMEM((m, block), BF16)] * 4


def total_scratch(m, rank):
    return [pltpu.VMEM((m, rank), F32), pltpu.VMEM((PAD, rank), F32)]


def cost(m, rank, columns, dots):
    return pl.CostEstimate(
        flops=6 * dots * m * rank * columns, bytes_accessed=4 * m * columns, transcendentals=0
    )


def full_turn(slab, left, right, extra, block, parts, vmem_bytes):
    (m, columns), rank = slab.shape, left.shape[1]
    columns_spec = lambda height: pl.BlockSpec((height, block), lambda step: (0, step))
    tall = m // parts + PAD
    return pl.pallas_call(
        turn_kernel,
        grid=(columns // block,),
        in_specs=[columns_spec(m), full((m, rank)), columns_spec(rank), full((min(PAD, extra.shape[0]), rank))],
        out_specs=[columns_spec(rank), full((parts, tall, rank))],
        out_shape=[
            jax.ShapeDtypeStruct((rank, columns), F32),
            jax.ShapeDtypeStruct((parts, tall, rank), F32),
        ],
        scratch_shapes=left_scratch(m, rank)
        + right_scratch(m, rank, block)
        + total_scratch(m, rank),
        compiler_params=params(vmem_bytes),
        cost_estimate=cost(m, rank, columns, 4),
        name="turn",
    )(slab, left, right, extra)


def second_numerator(right, second_left, second_right, slices):
    return pl.pallas_call(
        functools.partial(numerator_kernel, slices),
        out_shape=jax.ShapeDtypeStruct(second_right.shape, F32),
        compiler_params=pltpu.CompilerParams(vmem_limit_bytes=VMEM_BYTES),
        cost_estimate=cost(right.shape[0], right.shape[0], right.shape[1], 2),
        name="second_numerator",
    )(right, second_left, second_right)


def second_rows_out(right, second_left, second_right, slices):
    return pl.pallas_call(
        functools.partial(second_kernel, slices),
        out_shape=jax.ShapeDtypeStruct(second_left.shape, F32),
        compiler_params=pltpu.CompilerParams(vmem_limit_bytes=VMEM_BYTES),
        cost_estimate=cost(right.shape[0], right.shape[0], right.shape[1], 2),
        name="second_rows",
    )(right, second_left, second_right)


def left_rows_kernel(part_ref, left_ref, total_ref, out_ref):
    height = out_ref.shape[0]
    out_ref[...] = left_ref[...] * total_ref[:height, :] / total_ref[height : height + 1, :]


def left_rows(part, left, total, height):
    rank = left.shape[1]
    return pl.pallas_call(
        left_rows_kernel,
        grid_spec=pltpu.PrefetchScalarGridSpec(
            num_scalar_prefetch=1,
            grid=(1,),
            in_specs=[
                pl.BlockSpec((height, rank), lambda step, part: (part[0], 0)),
                pl.BlockSpec(total.shape, lambda step, part: (0, 0)),
            ],
            out_specs=pl.BlockSpec((height, rank), lambda step, part: (0, 0)),
        ),
        out_shape=jax.ShapeDtypeStruct((height, rank), F32),
        cost_estimate=cost(left.shape[0], rank, 16 * rank, 1),
        name="left_rows",
    )(part.astype(jnp.int32)[None], left, total)


def body(tensor_slab, left_init, right_init, second_left_init, second_right_init):
    row_devices = lax.axis_size("row")
    col_devices = lax.axis_size("col")
    devices = row_devices * col_devices
    own_part = (lax.axis_index("row") % 2) * col_devices + lax.axis_index("col")
    parts = 2 * col_devices
    m, rank = left_init.shape
    k = second_right_init.shape[1] * col_devices
    slices = right_init.shape[1] // k
    per_owner = rank // devices
    rows_own = m // parts

    second_rows = second_left_init.shape[0] // col_devices
    own_left = lax.dynamic_slice_in_dim(
        second_left_init, lax.axis_index("col") * second_rows, second_rows, 0
    )
    col_part = jnp.sum(own_left, axis=0)[None]
    own_left = own_left.reshape(per_owner, devices, slices, rank).transpose(1, 0, 2, 3)
    own_left = own_left.reshape(devices, per_owner * slices, rank)
    piece_rows = rank // row_devices
    piece = lax.dynamic_slice_in_dim(
        second_right_init, lax.axis_index("row") * piece_rows, piece_rows, 0
    ).reshape(-1, rank)
    piece = jnp.broadcast_to(piece[None], (devices,) + piece.shape)
    second_factors = jnp.concatenate([own_left, piece], axis=1)

    def own_left_rows(left, total):
        own = lax.dynamic_slice_in_dim(left, own_part * rows_own, rows_own, 0)
        return own * total[:rows_own] / total[rows_own][None, :]

    right, summed = full_turn(
        tensor_slab, after(left_init, second_factors), right_init, left_init, k, parts, 52 * MIB
    )
    summed = summed.reshape(2, col_devices, rows_own + PAD, rank)
    total = reduce_z(reduce_plane(reduce_core(summed)))
    left = spread_core(spread_plane(own_left_rows(left_init, total))).reshape(m, rank)

    arrived = exchange(after(second_factors, left))
    right, summed = full_turn(tensor_slab, left, right, col_part, k, parts, VMEM_BYTES)
    arrived = after(arrived, summed)
    second_left = arrived[:, : per_owner * slices].reshape(rank * slices, rank)
    whole = arrived[:, per_owner * slices :].reshape(row_devices, col_devices, piece_rows, -1)
    whole = whole.transpose(0, 2, 1, 3).reshape(rank, k // rank, rank).transpose(1, 0, 2)
    numerator = second_numerator(right, second_left, whole, slices)

    rows_part = k // parts
    summed = summed.reshape(2, col_devices, rows_own + PAD, rank)
    numerator = numerator.reshape(2, col_devices, rows_part, rank)
    total = reduce_z(reduce_plane(reduce_core(jnp.concatenate([summed, numerator], axis=2))))
    init_over = (whole / total[rows_own + 1][None, :, None]).reshape(k, rank)
    init_over = lax.dynamic_slice_in_dim(init_over, own_part * rows_part, rows_part, 0)
    second_part = init_over * total[rows_own + PAD :]
    second_right = spread_core(spread_plane(second_part)).reshape(k // rank, rank, rank)
    rows_out = second_rows_out(right, second_left, second_right, slices)
    left_part = left_rows(own_part, left, after(total, rows_out), rows_own)
    left_out = spread_core(spread_plane(left_part)).reshape(m, rank)
    returned = exchange(rows_out.reshape(devices, per_owner * slices, rank))
    returned = returned.reshape(devices, per_owner, slices, rank).transpose(1, 0, 2, 3)
    return (left_out, returned.reshape(second_rows, rank))


def solution(mesh):
    placed = (P(None, AXES), P(), P(None, AXES), P("row", None), P(None, "col"))
    return jax.shard_map(
        body, mesh=mesh, in_specs=placed, out_specs=(P(), P(AXES, None)), check_vma=False
    )
```

```python
import functools

import jax
import jax.numpy as jnp
from jax import lax
from jax.experimental import pallas as pl
from jax.experimental.pallas import tpu as pltpu
from jax.sharding import PartitionSpec as P

AXES = ("row", "col")
F32, BF16 = jnp.float32, jnp.bfloat16
PAD = 8
ROWS, WIDTH = 256, 256
MIB = 1024 * 1024
VMEM_BYTES = 51 * MIB


def exchange(parts):
    return lax.all_to_all(parts, AXES, split_axis=0, concat_axis=0, tiled=True)


def send(values, row_flip, col_flip):
    rows, cols = lax.axis_size("row"), lax.axis_size("col")
    pairs = [
        (r * cols + c, (r ^ row_flip) * cols + (c ^ col_flip))
        for r in range(rows)
        for c in range(cols)
    ]
    return lax.ppermute(values, AXES, pairs)


def pick(values, index):
    return lax.dynamic_index_in_dim(values, index, 0, keepdims=False)


def tree_sum(terms):
    while len(terms) > 1:
        terms = [a + b for a, b in zip(terms[::2], terms[1::2])]
    return terms[0]


def after(values, *events):
    return lax.optimization_barrier((values,) + events)[0]


def reduce_core(parts):
    core = lax.axis_index("row") % 2
    return pick(parts, core) + send(pick(parts, 1 - core), 1, 0)


def reduce_plane(own):
    col = lax.axis_index("col")
    others = [send(pick(own, col ^ flip), 0, flip) for flip in range(1, own.shape[0])]
    return tree_sum([pick(own, col)] + others)


def reduce_z(own):
    return tree_sum([own] + [send(own, flip, 0) for flip in range(2, lax.axis_size("row"), 2)])


def spread_plane(part):
    col, cols = lax.axis_index("col"), lax.axis_size("col")
    near = jnp.stack([part] + [send(part, 0, flip) for flip in range(1, cols)])
    return jnp.stack([pick(near, index ^ col) for index in range(cols)])


def spread_core(near):
    core = lax.axis_index("row") % 2
    both = jnp.stack([near, send(near, 1, 0)])
    return jnp.stack([pick(both, core), pick(both, 1 - core)])


def split(x):
    high = x.astype(BF16)
    return high, (x - high.astype(F32)).astype(BF16)


def dot(a, b):
    return jnp.dot(a, b, preferred_element_type=F32)


def dot_nt(a, b):
    return lax.dot_general(a, b, (((1,), (1,)), ((), ())), preferred_element_type=F32)


def divide(x, y):
    return x * pl.reciprocal(y, approx=True)


def prepare_left(left_ref, pair_ref):
    rank = left_ref.shape[1]
    high, low = split(left_ref[...])
    pair_ref[:, :rank] = high
    pair_ref[:, rank : 2 * rank] = low
    pair_ref[:, 2 * rank :] = high


def prepare_left_t(left_ref, pair_t_ref, sums_ref):
    rank = left_ref.shape[1]
    turned = left_ref[...].T
    high, low = split(turned)
    pair_t_ref[:rank, :] = high
    pair_t_ref[rank:, :] = low
    sums_ref[...] = jnp.broadcast_to(jnp.sum(turned, axis=1, keepdims=True), sums_ref.shape)


def chunks(extent, size):
    size = min(size, extent)
    return [pl.ds(start, size) for start in range(0, extent, size)]


def stacked(right):
    high, low = split(right)
    return jnp.concatenate([high, high, low], axis=0)


def quotients(slab_ref, pair_ref, right_stack, rows, columns):
    product = dot(pair_ref[rows, :], right_stack)
    return split(divide(slab_ref[rows, columns], product))


def right_update(
    slab_ref, pair_ref, pair_t_ref, sums_ref, right_ref, right_out, high_ref, low_ref, start, arrive
):
    block = high_ref.shape[1]
    rank = right_ref.shape[0]
    for index, half in enumerate(chunks(block, WIDTH)):
        columns = pl.ds(start + half.start, half.size)
        right = right_ref[:, columns]
        stack = stacked(right)
        for piece, rows in enumerate(chunks(slab_ref.shape[0], ROWS)):
            if index == 0:
                arrive(piece)
            high, low = quotients(slab_ref, pair_ref, stack, rows, columns)
            high_ref[rows, half] = high
            low_ref[rows, half] = low
        both = dot(pair_t_ref[...], high_ref[:, half])
        numerator = both[:rank] + both[rank:]
        numerator = numerator + dot(pair_t_ref[:rank, :], low_ref[:, half])
        right_out[:, columns] = right * numerator / sums_ref[:, :1]


def left_numerator(slab_ref, pair_ref, right_ref, total_ref, sums_ref, high_ref, low_ref, start, first):
    block = high_ref.shape[1]
    rank = right_ref.shape[0]
    right = right_ref[:, pl.ds(start, block)]
    stack = stacked(right)
    right_high, right_low = stack[:rank], stack[2 * rank :]
    right_both = jnp.concatenate([right_high, right_low], axis=0)
    row_sums = dot_nt(jnp.ones((16, block), BF16), right_both)[:PAD]
    row_sums = row_sums[:, :rank] + row_sums[:, rank:]
    sums_ref[...] = jnp.where(first, row_sums, sums_ref[...] + row_sums)
    for rows in chunks(slab_ref.shape[0], ROWS):
        for half in chunks(block, WIDTH):
            columns = pl.ds(start + half.start, half.size)
            part = stack[:, half.start : half.start + half.size]
            high, low = quotients(slab_ref, pair_ref, part, rows, columns)
            high_ref[rows, half] = high
            low_ref[rows, half] = low
        both = dot_nt(high_ref[rows, :], right_both)
        term = both[:, :rank] + both[:, rank:] + dot_nt(low_ref[rows, :], right_high)
        total_ref[rows, :] = jnp.where(first, term, total_ref[rows, :] + term)


def write_left(total_ref, row_sums_ref, extra_ref, out_ref):
    parts, tall, rank = out_ref.shape
    height = tall - PAD
    first = lax.broadcasted_iota(jnp.int32, (PAD, rank), 0) == 0
    stats = jnp.where(first, row_sums_ref[...], extra_ref[:1, :])
    for part in range(parts):
        out_ref[part, :height, :] = total_ref[pl.ds(part * height, height), :]
        out_ref[part, height:, :] = stats


def turn_kernel(
    block, slab_hbm, left_ref, right_ref, extra_ref, right_out, left_out, slab_ref,
    pair_ref, pair_t_ref, sums_ref, high_ref, low_ref, total_ref, row_sums_ref, arrivals,
):
    m, width = slab_ref.shape
    steps = width // block
    pieces = chunks(m, ROWS)

    def copy(step, piece):
        where = (pieces[piece], pl.ds(pl.multiple_of(step * block, block), block))
        return pltpu.make_async_copy(
            slab_hbm.at[where], slab_ref.at[where], arrivals.at[step, piece]
        )

    for step in range(steps):
        for piece in range(len(pieces)):
            copy(step, piece).start()
    prepare_left(left_ref, pair_ref)
    prepare_left_t(left_ref, pair_t_ref, sums_ref)

    def one(step, carry):
        start = pl.multiple_of(step * block, block)
        right_update(
            slab_ref, pair_ref, pair_t_ref, sums_ref, right_ref, right_out, high_ref, low_ref,
            start, lambda piece: copy(step, piece).wait(),
        )
        left_numerator(
            slab_ref, pair_ref, right_out, total_ref, row_sums_ref, high_ref, low_ref,
            start, step == 0,
        )
        return carry

    lax.fori_loop(0, steps, one, 0)
    write_left(total_ref, row_sums_ref, extra_ref, left_out)


def second_quotient(block, second_left, pairs):
    high, low = split(second_left)
    right_high, right_low = pairs
    product = dot(high, right_high) + (dot(low, right_high) + dot(high, right_low))
    return split(divide(block, product))


def numerator_kernel(slices, right_ref, second_left_ref, second_right_ref, numer_out):
    rank = right_ref.shape[0]
    k = right_ref.shape[1] // slices
    pairs = split(
        jnp.concatenate([second_right_ref[block] for block in range(k // rank)], axis=1)
    )
    total = 0.0
    for index in range(slices):
        second_left = second_left_ref[pl.ds(index, rank, stride=slices), :]
        high, low = second_quotient(right_ref[:, pl.ds(index * k, k)], second_left, pairs)
        left_high, left_low = split(second_left.T)
        total = total + (dot(left_high, high) + (dot(left_low, high) + dot(left_high, low)))
    for block in range(k // rank):
        numer_out[block] = total[:, block * rank : (block + 1) * rank]


def second_kernel(slices, right_ref, second_left_ref, second_right_ref, out_ref):
    rank = right_ref.shape[0]
    k = right_ref.shape[1] // slices
    second_right = jnp.concatenate(
        [second_right_ref[block] for block in range(k // rank)], axis=1
    )
    right_high, right_low = split(second_right)
    right_both = jnp.concatenate([right_high, right_low], axis=0)
    sums = dot_nt(jnp.ones((16, k), BF16), right_both)[:1]
    scale = 1.0 / (sums[:, :rank] + sums[:, rank:])
    for index in range(slices):
        rows = pl.ds(index, rank, stride=slices)
        second_left = second_left_ref[rows, :]
        high, low = second_quotient(
            right_ref[:, pl.ds(index * k, k)], second_left, (right_high, right_low)
        )
        both = dot_nt(high, right_both)
        numer = both[:, :rank] + both[:, rank:] + dot_nt(low, right_high)
        out_ref[rows, :] = second_left * numer * scale


def full(shape):
    return pl.BlockSpec(shape, lambda step: (0,) * len(shape))


def params(vmem_bytes):
    return pltpu.CompilerParams(
        dimension_semantics=("arbitrary",), vmem_limit_bytes=vmem_bytes
    )


def left_scratch(m, rank):
    return [pltpu.VMEM((m, 3 * rank), BF16)]


def right_scratch(m, rank, block):
    return [
        pltpu.VMEM((2 * rank, m), BF16),
        pltpu.VMEM((rank, rank), F32),
        pltpu.VMEM((m, block), BF16),
        pltpu.VMEM((m, block), BF16),
    ]


def total_scratch(m, rank):
    return [pltpu.VMEM((m, rank), F32), pltpu.VMEM((PAD, rank), F32)]


def cost(m, rank, columns, dots):
    return pl.CostEstimate(
        flops=6 * dots * m * rank * columns, bytes_accessed=4 * m * columns, transcendentals=0
    )


def full_turn(slab, left, right, extra, block, parts, vmem_bytes):
    (m, columns), rank = slab.shape, left.shape[1]
    tall = m // parts + PAD
    return pl.pallas_call(
        functools.partial(turn_kernel, block),
        grid=(1,),
        in_specs=[
            pl.BlockSpec(memory_space=pl.ANY),
            full((m, rank)),
            full((rank, columns)),
            full((min(PAD, extra.shape[0]), rank)),
        ],
        out_specs=[full((rank, columns)), full((parts, tall, rank))],
        out_shape=[
            jax.ShapeDtypeStruct((rank, columns), F32),
            jax.ShapeDtypeStruct((parts, tall, rank), F32),
        ],
        scratch_shapes=[pltpu.VMEM((m, columns), F32)]
        + left_scratch(m, rank)
        + right_scratch(m, rank, block)
        + total_scratch(m, rank)
        + [pltpu.SemaphoreType.DMA((columns // block, max(1, m // ROWS)))],
        compiler_params=params(vmem_bytes),
        cost_estimate=cost(m, rank, columns, 4),
        name="turn",
    )(slab, left, right, extra)


def second_numerator(right, second_left, second_right, slices):
    return pl.pallas_call(
        functools.partial(numerator_kernel, slices),
        out_shape=jax.ShapeDtypeStruct(second_right.shape, F32),
        compiler_params=pltpu.CompilerParams(vmem_limit_bytes=VMEM_BYTES),
        cost_estimate=cost(right.shape[0], right.shape[0], right.shape[1], 2),
        name="second_numerator",
    )(right, second_left, second_right)


def second_rows_out(right, second_left, second_right, slices):
    return pl.pallas_call(
        functools.partial(second_kernel, slices),
        out_shape=jax.ShapeDtypeStruct(second_left.shape, F32),
        compiler_params=pltpu.CompilerParams(vmem_limit_bytes=VMEM_BYTES),
        cost_estimate=cost(right.shape[0], right.shape[0], right.shape[1], 2),
        name="second_rows",
    )(right, second_left, second_right)


def body(tensor_slab, left_init, right_init, second_left_init, second_right_init):
    row_devices = lax.axis_size("row")
    col_devices = lax.axis_size("col")
    devices = row_devices * col_devices
    own_part = (lax.axis_index("row") % 2) * col_devices + lax.axis_index("col")
    parts = 2 * col_devices
    m, rank = left_init.shape
    k = second_right_init.shape[1] * col_devices
    slices = right_init.shape[1] // k
    per_owner = rank // devices
    rows_own = m // parts

    second_rows = second_left_init.shape[0] // col_devices
    own_left = lax.dynamic_slice_in_dim(
        second_left_init, lax.axis_index("col") * second_rows, second_rows, 0
    )
    col_part = jnp.sum(own_left, axis=0)[None]
    own_left = own_left.reshape(per_owner, devices, slices, rank).transpose(1, 0, 2, 3)
    own_left = own_left.reshape(devices, per_owner * slices, rank)
    piece_rows = rank // row_devices
    piece = lax.dynamic_slice_in_dim(
        second_right_init, lax.axis_index("row") * piece_rows, piece_rows, 0
    ).reshape(-1, rank)
    piece = jnp.broadcast_to(piece[None], (devices,) + piece.shape)
    second_factors = jnp.concatenate([own_left, piece], axis=1)

    def own_left_rows(left, total):
        own = lax.dynamic_slice_in_dim(left, own_part * rows_own, rows_own, 0)
        return own * total[:rows_own] / total[rows_own][None, :]

    right, summed = full_turn(
        tensor_slab, after(left_init, second_factors), right_init, left_init, k, parts, 52 * MIB
    )
    summed = summed.reshape(2, col_devices, rows_own + PAD, rank)
    total = reduce_z(reduce_plane(reduce_core(summed)))
    left = spread_core(spread_plane(own_left_rows(left_init, total))).reshape(m, rank)

    arrived = exchange(after(second_factors, left))
    right, summed = full_turn(tensor_slab, left, right, col_part, k, parts, VMEM_BYTES)
    arrived = after(arrived, summed)
    second_left = arrived[:, : per_owner * slices].reshape(rank * slices, rank)
    whole = arrived[:, per_owner * slices :].reshape(row_devices, col_devices, piece_rows, -1)
    whole = whole.transpose(0, 2, 1, 3).reshape(rank, k // rank, rank).transpose(1, 0, 2)
    numerator = second_numerator(right, second_left, whole, slices)

    rows_part = k // parts
    summed = summed.reshape(2, col_devices, rows_own + PAD, rank)
    numerator = numerator.reshape(2, col_devices, rows_part, rank)
    total = reduce_z(reduce_plane(reduce_core(jnp.concatenate([summed, numerator], axis=2))))
    init_over = (whole / total[rows_own + 1][None, :, None]).reshape(k, rank)
    init_over = lax.dynamic_slice_in_dim(init_over, own_part * rows_part, rows_part, 0)
    second_part = init_over * total[rows_own + PAD :]
    both = spread_core(
        spread_plane(jnp.concatenate([own_left_rows(left, total), second_part], axis=0))
    )
    left_out = both[:, :, :rows_own].reshape(m, rank)
    second_right = both[:, :, rows_own:].reshape(k // rank, rank, rank)
    rows_out = second_rows_out(right, second_left, second_right, slices)
    returned = exchange(rows_out.reshape(devices, per_owner * slices, rank))
    returned = returned.reshape(devices, per_owner, slices, rank).transpose(1, 0, 2, 3)
    return (left_out, returned.reshape(second_rows, rank))


def solution(mesh):
    placed = (P(None, AXES), P(), P(None, AXES), P("row", None), P(None, "col"))
    return jax.shard_map(
        body, mesh=mesh, in_specs=placed, out_specs=(P(), P(AXES, None)), check_vma=False
    )
```

```python
import functools

import jax
import jax.numpy as jnp
from jax import lax
from jax.experimental import pallas as pl
from jax.experimental.pallas import tpu as pltpu
from jax.sharding import PartitionSpec as P

AXES = ("row", "col")
F32, BF16 = jnp.float32, jnp.bfloat16
PAD = 8
ROWS = 256
MIB = 1024 * 1024
VMEM_BYTES = 51 * MIB


def exchange(parts):
    return lax.all_to_all(parts, AXES, split_axis=0, concat_axis=0, tiled=True)


def send(values, row_flip, col_flip):
    rows, cols = lax.axis_size("row"), lax.axis_size("col")
    pairs = [
        (r * cols + c, (r ^ row_flip) * cols + (c ^ col_flip))
        for r in range(rows)
        for c in range(cols)
    ]
    return lax.ppermute(values, AXES, pairs)


def pick(values, index):
    return lax.dynamic_index_in_dim(values, index, 0, keepdims=False)


def tree_sum(terms):
    while len(terms) > 1:
        terms = [a + b for a, b in zip(terms[::2], terms[1::2])]
    return terms[0]


def after(values, *events):
    return lax.optimization_barrier((values,) + events)[0]


def reduce_core(parts):
    core = lax.axis_index("row") % 2
    return pick(parts, core) + send(pick(parts, 1 - core), 1, 0)


def reduce_plane(own):
    col = lax.axis_index("col")
    others = [send(pick(own, col ^ flip), 0, flip) for flip in range(1, own.shape[0])]
    return tree_sum([pick(own, col)] + others)


def reduce_z(own):
    return tree_sum([own] + [send(own, flip, 0) for flip in range(2, lax.axis_size("row"), 2)])


def spread_plane(part):
    col, cols = lax.axis_index("col"), lax.axis_size("col")
    near = jnp.stack([part] + [send(part, 0, flip) for flip in range(1, cols)])
    return jnp.stack([pick(near, index ^ col) for index in range(cols)])


def spread_core(near):
    core = lax.axis_index("row") % 2
    both = jnp.stack([near, send(near, 1, 0)])
    return jnp.stack([pick(both, core), pick(both, 1 - core)])


def split(x):
    high = x.astype(BF16)
    return high, (x - high.astype(F32)).astype(BF16)


def dot(a, b):
    return jnp.dot(a, b, preferred_element_type=F32)


def dot_nt(a, b):
    return lax.dot_general(a, b, (((1,), (1,)), ((), ())), preferred_element_type=F32)


def divide(x, y):
    return x * pl.reciprocal(y, approx=True)


def prepare_left(left_ref, pair_ref):
    rank = left_ref.shape[1]
    high, low = split(left_ref[...])
    pair_ref[:, :rank] = high
    pair_ref[:, rank : 2 * rank] = low
    pair_ref[:, 2 * rank :] = high


def prepare_left_t(left_ref, pair_t_ref, sums_ref):
    rank = left_ref.shape[1]
    turned = left_ref[...].T
    high, low = split(turned)
    pair_t_ref[:rank, :] = high
    pair_t_ref[rank:, :] = low
    sums_ref[...] = jnp.broadcast_to(jnp.sum(turned, axis=1, keepdims=True), sums_ref.shape)


def chunks(extent, size):
    size = min(size, extent)
    return [pl.ds(start, size) for start in range(0, extent, size)]


def stacked(right):
    high, low = split(right)
    return jnp.concatenate([high, high, low], axis=0)


def quotients(slab_ref, pair_ref, right_stack, rows):
    product = dot(pair_ref[rows, :], right_stack)
    return split(divide(slab_ref[rows, :], product))


def right_update(slab_ref, pair_ref, pair_t_ref, sums_ref, right):
    rank = right.shape[0]
    stack = stacked(right)
    parts = [quotients(slab_ref, pair_ref, stack, rows) for rows in chunks(slab_ref.shape[0], ROWS)]
    both = dot(pair_t_ref[...], jnp.concatenate([high for high, _ in parts], axis=0))
    numerator = both[:rank] + both[rank:]
    numerator = numerator + dot(
        pair_t_ref[:rank, :], jnp.concatenate([low for _, low in parts], axis=0)
    )
    return right * numerator / sums_ref[:, :1]


def left_numerator(slab_ref, pair_ref, right, total_ref, sums_ref, first):
    rank = right.shape[0]
    stack = stacked(right)
    right_high, right_low = stack[:rank], stack[2 * rank :]
    right_both = jnp.concatenate([right_high, right_low], axis=0)
    row_sums = dot_nt(jnp.ones((16, right.shape[1]), BF16), right_both)[:PAD]
    row_sums = row_sums[:, :rank] + row_sums[:, rank:]
    sums_ref[...] = jnp.where(first, row_sums, sums_ref[...] + row_sums)
    for rows in chunks(slab_ref.shape[0], ROWS):
        high, low = quotients(slab_ref, pair_ref, stack, rows)
        both = dot_nt(high, right_both)
        term = both[:, :rank] + both[:, rank:] + dot_nt(low, right_high)
        total_ref[rows, :] = jnp.where(first, term, total_ref[rows, :] + term)


def write_left(total_ref, row_sums_ref, extra_ref, out_ref):
    parts, tall, rank = out_ref.shape
    height = tall - PAD
    first = lax.broadcasted_iota(jnp.int32, (PAD, rank), 0) == 0
    stats = jnp.where(first, row_sums_ref[...], extra_ref[:1, :])
    for part in range(parts):
        out_ref[part, :height, :] = total_ref[pl.ds(part * height, height), :]
        out_ref[part, height:, :] = stats


def turn_kernel(
    slab_ref, left_ref, right_ref, extra_ref, right_out, left_out,
    pair_ref, pair_t_ref, sums_ref, total_ref, row_sums_ref,
):
    step = pl.program_id(0)

    @pl.when(step == 0)
    def _():
        prepare_left(left_ref, pair_ref)
        prepare_left_t(left_ref, pair_t_ref, sums_ref)

    right = right_update(slab_ref, pair_ref, pair_t_ref, sums_ref, right_ref[...])
    right_out[...] = right
    left_numerator(slab_ref, pair_ref, right, total_ref, row_sums_ref, step == 0)

    @pl.when(step == pl.num_programs(0) - 1)
    def _():
        write_left(total_ref, row_sums_ref, extra_ref, left_out)


def second_quotient(block, second_left, pairs):
    high, low = split(second_left)
    right_high, right_low = pairs
    product = dot(high, right_high) + (dot(low, right_high) + dot(high, right_low))
    return split(divide(block, product))


def numerator_kernel(slices, right_ref, second_left_ref, second_right_ref, numer_out):
    rank = right_ref.shape[0]
    k = right_ref.shape[1] // slices
    pairs = split(
        jnp.concatenate([second_right_ref[block] for block in range(k // rank)], axis=1)
    )
    total = 0.0
    for index in range(slices):
        second_left = second_left_ref[pl.ds(index, rank, stride=slices), :]
        high, low = second_quotient(right_ref[:, pl.ds(index * k, k)], second_left, pairs)
        left_high, left_low = split(second_left.T)
        total = total + (dot(left_high, high) + (dot(left_low, high) + dot(left_high, low)))
    for block in range(k // rank):
        numer_out[block] = total[:, block * rank : (block + 1) * rank]


def second_kernel(slices, right_ref, second_left_ref, second_right_ref, out_ref):
    rank = right_ref.shape[0]
    k = right_ref.shape[1] // slices
    second_right = jnp.concatenate(
        [second_right_ref[block] for block in range(k // rank)], axis=1
    )
    right_high, right_low = split(second_right)
    right_both = jnp.concatenate([right_high, right_low], axis=0)
    sums = dot_nt(jnp.ones((16, k), BF16), right_both)[:1]
    scale = 1.0 / (sums[:, :rank] + sums[:, rank:])
    for index in range(slices):
        rows = pl.ds(index, rank, stride=slices)
        second_left = second_left_ref[rows, :]
        high, low = second_quotient(
            right_ref[:, pl.ds(index * k, k)], second_left, (right_high, right_low)
        )
        both = dot_nt(high, right_both)
        numer = both[:, :rank] + both[:, rank:] + dot_nt(low, right_high)
        out_ref[rows, :] = second_left * numer * scale


def full(shape):
    return pl.BlockSpec(shape, lambda step: (0,) * len(shape))


def params(vmem_bytes):
    return pltpu.CompilerParams(
        dimension_semantics=("arbitrary",), vmem_limit_bytes=vmem_bytes
    )


def left_scratch(m, rank):
    return [pltpu.VMEM((m, 3 * rank), BF16)]


def right_scratch(m, rank):
    return [pltpu.VMEM((2 * rank, m), BF16), pltpu.VMEM((rank, rank), F32)]


def total_scratch(m, rank):
    return [pltpu.VMEM((m, rank), F32), pltpu.VMEM((PAD, rank), F32)]


def cost(m, rank, columns, dots):
    return pl.CostEstimate(
        flops=6 * dots * m * rank * columns, bytes_accessed=4 * m * columns, transcendentals=0
    )


def full_turn(slab, left, right, extra, block, parts, vmem_bytes):
    (m, columns), rank = slab.shape, left.shape[1]
    columns_spec = lambda height: pl.BlockSpec((height, block), lambda step: (0, step))
    tall = m // parts + PAD
    return pl.pallas_call(
        turn_kernel,
        grid=(columns // block,),
        in_specs=[columns_spec(m), full((m, rank)), columns_spec(rank), full((min(PAD, extra.shape[0]), rank))],
        out_specs=[columns_spec(rank), full((parts, tall, rank))],
        out_shape=[
            jax.ShapeDtypeStruct((rank, columns), F32),
            jax.ShapeDtypeStruct((parts, tall, rank), F32),
        ],
        scratch_shapes=left_scratch(m, rank)
        + right_scratch(m, rank)
        + total_scratch(m, rank),
        compiler_params=params(vmem_bytes),
        cost_estimate=cost(m, rank, columns, 4),
        name="turn",
    )(slab, left, right, extra)


def second_numerator(right, second_left, second_right, slices):
    return pl.pallas_call(
        functools.partial(numerator_kernel, slices),
        out_shape=jax.ShapeDtypeStruct(second_right.shape, F32),
        compiler_params=pltpu.CompilerParams(vmem_limit_bytes=VMEM_BYTES),
        cost_estimate=cost(right.shape[0], right.shape[0], right.shape[1], 2),
        name="second_numerator",
    )(right, second_left, second_right)


def second_rows_out(right, second_left, second_right, slices):
    return pl.pallas_call(
        functools.partial(second_kernel, slices),
        out_shape=jax.ShapeDtypeStruct(second_left.shape, F32),
        compiler_params=pltpu.CompilerParams(vmem_limit_bytes=VMEM_BYTES),
        cost_estimate=cost(right.shape[0], right.shape[0], right.shape[1], 2),
        name="second_rows",
    )(right, second_left, second_right)


def body(tensor_slab, left_init, right_init, second_left_init, second_right_init):
    row_devices = lax.axis_size("row")
    col_devices = lax.axis_size("col")
    devices = row_devices * col_devices
    own_part = (lax.axis_index("row") % 2) * col_devices + lax.axis_index("col")
    parts = 2 * col_devices
    m, rank = left_init.shape
    k = second_right_init.shape[1] * col_devices
    slices = right_init.shape[1] // k
    per_owner = rank // devices
    rows_own = m // parts

    second_rows = second_left_init.shape[0] // col_devices
    own_left = lax.dynamic_slice_in_dim(
        second_left_init, lax.axis_index("col") * second_rows, second_rows, 0
    )
    col_part = jnp.sum(own_left, axis=0)[None]
    own_left = own_left.reshape(per_owner, devices, slices, rank).transpose(1, 0, 2, 3)
    own_left = own_left.reshape(devices, per_owner * slices, rank)
    piece_rows = rank // row_devices
    piece = lax.dynamic_slice_in_dim(
        second_right_init, lax.axis_index("row") * piece_rows, piece_rows, 0
    ).reshape(-1, rank)
    piece = jnp.broadcast_to(piece[None], (devices,) + piece.shape)
    second_factors = jnp.concatenate([own_left, piece], axis=1)

    def own_left_rows(left, total):
        own = lax.dynamic_slice_in_dim(left, own_part * rows_own, rows_own, 0)
        return own * total[:rows_own] / total[rows_own][None, :]

    right, summed = full_turn(
        tensor_slab, after(left_init, second_factors), right_init, left_init, k, parts, 52 * MIB
    )
    summed = summed.reshape(2, col_devices, rows_own + PAD, rank)
    total = reduce_z(reduce_plane(reduce_core(summed)))
    left = spread_core(spread_plane(own_left_rows(left_init, total))).reshape(m, rank)

    arrived = exchange(after(second_factors, left))
    right, summed = full_turn(tensor_slab, left, right, col_part, k, parts, VMEM_BYTES)
    arrived = after(arrived, summed)
    second_left = arrived[:, : per_owner * slices].reshape(rank * slices, rank)
    whole = arrived[:, per_owner * slices :].reshape(row_devices, col_devices, piece_rows, -1)
    whole = whole.transpose(0, 2, 1, 3).reshape(rank, k // rank, rank).transpose(1, 0, 2)
    numerator = second_numerator(right, second_left, whole, slices)

    rows_part = k // parts
    summed = summed.reshape(2, col_devices, rows_own + PAD, rank)
    numerator = numerator.reshape(2, col_devices, rows_part, rank)
    total = reduce_z(reduce_plane(reduce_core(jnp.concatenate([summed, numerator], axis=2))))
    init_over = (whole / total[rows_own + 1][None, :, None]).reshape(k, rank)
    init_over = lax.dynamic_slice_in_dim(init_over, own_part * rows_part, rows_part, 0)
    second_part = init_over * total[rows_own + PAD :]
    both = spread_core(
        spread_plane(jnp.concatenate([own_left_rows(left, total), second_part], axis=0))
    )
    left_out = both[:, :, :rows_own].reshape(m, rank)
    second_right = both[:, :, rows_own:].reshape(k // rank, rank, rank)
    rows_out = second_rows_out(right, second_left, second_right, slices)
    returned = exchange(rows_out.reshape(devices, per_owner * slices, rank))
    returned = returned.reshape(devices, per_owner, slices, rank).transpose(1, 0, 2, 3)
    return (left_out, returned.reshape(second_rows, rank))


def solution(mesh):
    placed = (P(None, AXES), P(), P(None, AXES), P("row", None), P(None, "col"))
    return jax.shard_map(
        body, mesh=mesh, in_specs=placed, out_specs=(P(), P(AXES, None)), check_vma=False
    )
```

```python
import functools

import jax
import jax.numpy as jnp
from jax import lax
from jax.experimental import pallas as pl
from jax.experimental.pallas import tpu as pltpu
from jax.sharding import PartitionSpec as P

AXES = ("row", "col")
F32, BF16 = jnp.float32, jnp.bfloat16
PAD = 8
ROWS = 128
MIB = 1024 * 1024
T1_MIB = 52
VMEM_BYTES = 51 * MIB


def exchange(parts):
    return lax.all_to_all(parts, AXES, split_axis=0, concat_axis=0, tiled=True)


def send(values, row_flip, col_flip):
    rows, cols = lax.axis_size("row"), lax.axis_size("col")
    pairs = [
        (r * cols + c, (r ^ row_flip) * cols + (c ^ col_flip))
        for r in range(rows)
        for c in range(cols)
    ]
    return lax.ppermute(values, AXES, pairs)


def pick(values, index):
    return lax.dynamic_index_in_dim(values, index, 0, keepdims=False)


def tree_sum(terms):
    while len(terms) > 1:
        terms = [a + b for a, b in zip(terms[::2], terms[1::2])]
    return terms[0]


def after(values, *events):
    return lax.optimization_barrier((values,) + events)[0]


def reduce_core(parts):
    core = lax.axis_index("row") % 2
    return pick(parts, core) + send(pick(parts, 1 - core), 1, 0)


def reduce_plane(own):
    col = lax.axis_index("col")
    others = [send(pick(own, col ^ flip), 0, flip) for flip in range(1, own.shape[0])]
    return tree_sum([pick(own, col)] + others)


def reduce_z(own):
    return tree_sum([own] + [send(own, flip, 0) for flip in range(2, lax.axis_size("row"), 2)])


def spread_plane(part):
    col, cols = lax.axis_index("col"), lax.axis_size("col")
    near = jnp.stack([part] + [send(part, 0, flip) for flip in range(1, cols)])
    return jnp.stack([pick(near, index ^ col) for index in range(cols)])


def spread_core(near):
    core = lax.axis_index("row") % 2
    both = jnp.stack([near, send(near, 1, 0)])
    return jnp.stack([pick(both, core), pick(both, 1 - core)])


def split(x):
    high = x.astype(BF16)
    return high, (x - high.astype(F32)).astype(BF16)


def dot(a, b):
    return jnp.dot(a, b, preferred_element_type=F32)


def dot_nt(a, b):
    return lax.dot_general(a, b, (((1,), (1,)), ((), ())), preferred_element_type=F32)


def divide(x, y):
    return x * pl.reciprocal(y, approx=True)


def prepare_left(left_ref, pair_ref):
    rank = left_ref.shape[1]
    high, low = split(left_ref[...])
    pair_ref[:, :rank] = high
    pair_ref[:, rank : 2 * rank] = low
    pair_ref[:, 2 * rank :] = high


def prepare_left_t(left_ref, pair_t_ref, sums_ref):
    rank = left_ref.shape[1]
    turned = left_ref[...].T
    high, low = split(turned)
    pair_t_ref[:rank, :] = high
    pair_t_ref[rank:, :] = low
    sums_ref[...] = jnp.broadcast_to(jnp.sum(turned, axis=1, keepdims=True), sums_ref.shape)


def chunks(extent, size):
    size = min(size, extent)
    return [pl.ds(start, size) for start in range(0, extent, size)]


def stacked(right):
    high, low = split(right)
    return jnp.concatenate([high, high, low], axis=0)


def quotients(slab_ref, pair_ref, right_stack, rows):
    product = dot(pair_ref[rows, :], right_stack)
    return split(divide(slab_ref[rows, :], product))


def right_update(slab_ref, pair_ref, pair_t_ref, sums_ref, right):
    rank = right.shape[0]
    stack = stacked(right)
    parts = [quotients(slab_ref, pair_ref, stack, rows) for rows in chunks(slab_ref.shape[0], ROWS)]
    both = dot(pair_t_ref[...], jnp.concatenate([high for high, _ in parts], axis=0))
    numerator = both[:rank] + both[rank:]
    numerator = numerator + dot(
        pair_t_ref[:rank, :], jnp.concatenate([low for _, low in parts], axis=0)
    )
    return right * numerator / sums_ref[:, :1]


def left_numerator(slab_ref, pair_ref, right, total_ref, sums_ref, first):
    rank = right.shape[0]
    stack = stacked(right)
    right_high, right_low = stack[:rank], stack[2 * rank :]
    right_both = jnp.concatenate([right_high, right_low], axis=0)
    row_sums = dot_nt(jnp.ones((16, right.shape[1]), BF16), right_both)[:PAD]
    row_sums = row_sums[:, :rank] + row_sums[:, rank:]
    sums_ref[...] = jnp.where(first, row_sums, sums_ref[...] + row_sums)
    for rows in chunks(slab_ref.shape[0], ROWS):
        high, low = quotients(slab_ref, pair_ref, stack, rows)
        both = dot_nt(high, right_both)
        term = both[:, :rank] + both[:, rank:] + dot_nt(low, right_high)
        total_ref[rows, :] = jnp.where(first, term, total_ref[rows, :] + term)


def write_left(total_ref, row_sums_ref, extra_ref, out_ref):
    parts, tall, rank = out_ref.shape
    height = tall - PAD
    first = lax.broadcasted_iota(jnp.int32, (PAD, rank), 0) == 0
    stats = jnp.where(first, row_sums_ref[...], extra_ref[:1, :])
    for part in range(parts):
        out_ref[part, :height, :] = total_ref[pl.ds(part * height, height), :]
        out_ref[part, height:, :] = stats


def turn_kernel(
    slab_ref, left_ref, right_ref, extra_ref, right_out, left_out,
    pair_ref, pair_t_ref, sums_ref, total_ref, row_sums_ref,
):
    step = pl.program_id(0)

    @pl.when(step == 0)
    def _():
        prepare_left(left_ref, pair_ref)
        prepare_left_t(left_ref, pair_t_ref, sums_ref)

    right = right_update(slab_ref, pair_ref, pair_t_ref, sums_ref, right_ref[...])
    right_out[...] = right
    left_numerator(slab_ref, pair_ref, right, total_ref, row_sums_ref, step == 0)

    @pl.when(step == pl.num_programs(0) - 1)
    def _():
        write_left(total_ref, row_sums_ref, extra_ref, left_out)


def second_quotient(block, second_left, pairs):
    high, low = split(second_left)
    right_high, right_low = pairs
    product = dot(high, right_high) + (dot(low, right_high) + dot(high, right_low))
    return split(divide(block, product))


def numerator_kernel(slices, right_ref, second_left_ref, second_right_ref, numer_out):
    rank = right_ref.shape[0]
    k = right_ref.shape[1] // slices
    pairs = split(
        jnp.concatenate([second_right_ref[block] for block in range(k // rank)], axis=1)
    )
    total = 0.0
    for index in range(slices):
        second_left = second_left_ref[pl.ds(index, rank, stride=slices), :]
        high, low = second_quotient(right_ref[:, pl.ds(index * k, k)], second_left, pairs)
        left_high, left_low = split(second_left.T)
        total = total + (dot(left_high, high) + (dot(left_low, high) + dot(left_high, low)))
    for block in range(k // rank):
        numer_out[block] = total[:, block * rank : (block + 1) * rank]


def second_kernel(slices, right_ref, second_left_ref, second_right_ref, out_ref):
    rank = right_ref.shape[0]
    k = right_ref.shape[1] // slices
    second_right = jnp.concatenate(
        [second_right_ref[block] for block in range(k // rank)], axis=1
    )
    right_high, right_low = split(second_right)
    right_both = jnp.concatenate([right_high, right_low], axis=0)
    sums = dot_nt(jnp.ones((16, k), BF16), right_both)[:1]
    scale = 1.0 / (sums[:, :rank] + sums[:, rank:])
    for index in range(slices):
        rows = pl.ds(index, rank, stride=slices)
        second_left = second_left_ref[rows, :]
        high, low = second_quotient(
            right_ref[:, pl.ds(index * k, k)], second_left, (right_high, right_low)
        )
        both = dot_nt(high, right_both)
        numer = both[:, :rank] + both[:, rank:] + dot_nt(low, right_high)
        out_ref[rows, :] = second_left * numer * scale


def full(shape):
    return pl.BlockSpec(shape, lambda step: (0,) * len(shape))


def params(vmem_bytes):
    return pltpu.CompilerParams(
        dimension_semantics=("arbitrary",), vmem_limit_bytes=vmem_bytes
    )


def left_scratch(m, rank):
    return [pltpu.VMEM((m, 3 * rank), BF16)]


def right_scratch(m, rank):
    return [pltpu.VMEM((2 * rank, m), BF16), pltpu.VMEM((rank, rank), F32)]


def total_scratch(m, rank):
    return [pltpu.VMEM((m, rank), F32), pltpu.VMEM((PAD, rank), F32)]


def cost(m, rank, columns, dots):
    return pl.CostEstimate(
        flops=6 * dots * m * rank * columns, bytes_accessed=4 * m * columns, transcendentals=0
    )


def full_turn(slab, left, right, extra, block, parts, vmem_bytes):
    (m, columns), rank = slab.shape, left.shape[1]
    columns_spec = lambda height: pl.BlockSpec((height, block), lambda step: (0, step))
    tall = m // parts + PAD
    return pl.pallas_call(
        turn_kernel,
        grid=(columns // block,),
        in_specs=[columns_spec(m), full((m, rank)), columns_spec(rank), full((min(PAD, extra.shape[0]), rank))],
        out_specs=[columns_spec(rank), full((parts, tall, rank))],
        out_shape=[
            jax.ShapeDtypeStruct((rank, columns), F32),
            jax.ShapeDtypeStruct((parts, tall, rank), F32),
        ],
        scratch_shapes=left_scratch(m, rank)
        + right_scratch(m, rank)
        + total_scratch(m, rank),
        compiler_params=params(vmem_bytes),
        cost_estimate=cost(m, rank, columns, 4),
        name="turn",
    )(slab, left, right, extra)


def second_numerator(right, second_left, second_right, slices):
    return pl.pallas_call(
        functools.partial(numerator_kernel, slices),
        out_shape=jax.ShapeDtypeStruct(second_right.shape, F32),
        compiler_params=pltpu.CompilerParams(vmem_limit_bytes=VMEM_BYTES),
        cost_estimate=cost(right.shape[0], right.shape[0], right.shape[1], 2),
        name="second_numerator",
    )(right, second_left, second_right)


def second_rows_out(right, second_left, second_right, slices):
    return pl.pallas_call(
        functools.partial(second_kernel, slices),
        out_shape=jax.ShapeDtypeStruct(second_left.shape, F32),
        compiler_params=pltpu.CompilerParams(vmem_limit_bytes=VMEM_BYTES),
        cost_estimate=cost(right.shape[0], right.shape[0], right.shape[1], 2),
        name="second_rows",
    )(right, second_left, second_right)


def body(tensor_slab, left_init, right_init, second_left_init, second_right_init):
    row_devices = lax.axis_size("row")
    col_devices = lax.axis_size("col")
    devices = row_devices * col_devices
    own_part = (lax.axis_index("row") % 2) * col_devices + lax.axis_index("col")
    parts = 2 * col_devices
    m, rank = left_init.shape
    k = second_right_init.shape[1] * col_devices
    slices = right_init.shape[1] // k
    per_owner = rank // devices
    rows_own = m // parts

    second_rows = second_left_init.shape[0] // col_devices
    own_left = lax.dynamic_slice_in_dim(
        second_left_init, lax.axis_index("col") * second_rows, second_rows, 0
    )
    col_part = jnp.sum(own_left, axis=0)[None]
    own_left = own_left.reshape(per_owner, devices, slices, rank)
    piece_rows = rank // row_devices
    piece = lax.dynamic_slice_in_dim(
        second_right_init, lax.axis_index("row") * piece_rows, piece_rows, 0
    ).reshape(-1, rank)
    piece = jnp.broadcast_to(piece[None], (devices,) + piece.shape)
    second_factors = [own_left[index] for index in range(per_owner)] + [piece]
    arrived = exchange(jnp.concatenate(second_factors, axis=1))

    def own_rows(left):
        return lax.dynamic_slice_in_dim(left, own_part * rows_own, rows_own, 0)

    def own_left_rows(own, total):
        return own * total[:rows_own] / total[rows_own][None, :]

    own_init = own_rows(left_init)
    right, summed = full_turn(
        tensor_slab, after(left_init, own_init), right_init, left_init, k, parts, T1_MIB * MIB
    )
    summed, arrived = lax.optimization_barrier((summed, arrived))
    summed = summed.reshape(2, col_devices, rows_own + PAD, rank)
    total = reduce_z(reduce_plane(reduce_core(summed)))
    left = spread_core(spread_plane(own_left_rows(own_init, total))).reshape(m, rank)
    right, summed = full_turn(tensor_slab, left, right, col_part, k, parts, VMEM_BYTES)
    second_left = arrived[:, : per_owner * slices].reshape(rank * slices, rank)
    whole = arrived[:, per_owner * slices :].reshape(row_devices, col_devices, piece_rows, -1)
    whole = whole.transpose(0, 2, 1, 3).reshape(rank, k // rank, rank).transpose(1, 0, 2)
    numerator = second_numerator(right, second_left, whole, slices)

    rows_part = k // parts
    summed = summed.reshape(2, col_devices, rows_own + PAD, rank)
    numerator = numerator.reshape(2, col_devices, rows_part, rank)
    total = reduce_z(reduce_plane(reduce_core(jnp.concatenate([summed, numerator], axis=2))))
    init_over = (whole / total[rows_own + 1][None, :, None]).reshape(k, rank)
    init_over = lax.dynamic_slice_in_dim(init_over, own_part * rows_part, rows_part, 0)
    second_part = init_over * total[rows_own + PAD :]
    both = spread_core(
        spread_plane(jnp.concatenate([own_left_rows(own_rows(left), total), second_part], axis=0))
    )
    left_out = both[:, :, :rows_own].reshape(m, rank)
    second_right = both[:, :, rows_own:].reshape(k // rank, rank, rank)
    rows_out = second_rows_out(right, second_left, second_right, slices)
    returned = exchange(rows_out.reshape(devices, per_owner * slices, rank))
    returned = returned.reshape(devices, per_owner, slices, rank).transpose(1, 0, 2, 3)
    return (left_out, returned.reshape(second_rows, rank))


def solution(mesh):
    placed = (P(None, AXES), P(), P(None, AXES), P("row", None), P(None, "col"))
    return jax.shard_map(
        body, mesh=mesh, in_specs=placed, out_specs=(P(), P(AXES, None)), check_vma=False
    )
```

```python
import functools

import jax
import jax.numpy as jnp
from jax import lax
from jax.experimental import pallas as pl
from jax.experimental.pallas import tpu as pltpu
from jax.sharding import PartitionSpec as P

AXES = ("row", "col")
F32, BF16 = jnp.float32, jnp.bfloat16
PAD = 8
ROWS = 512
MIB = 1024 * 1024
T1_MIB = 52
PREP_KIB = 54528
VMEM_BYTES = 51 * MIB


def exchange(parts):
    return lax.all_to_all(parts, AXES, split_axis=0, concat_axis=0, tiled=True)


def send(values, row_flip, col_flip):
    rows, cols = lax.axis_size("row"), lax.axis_size("col")
    pairs = [
        (r * cols + c, (r ^ row_flip) * cols + (c ^ col_flip))
        for r in range(rows)
        for c in range(cols)
    ]
    return lax.ppermute(values, AXES, pairs)


def pick(values, index):
    return lax.dynamic_index_in_dim(values, index, 0, keepdims=False)


def tree_sum(terms):
    while len(terms) > 1:
        terms = [a + b for a, b in zip(terms[::2], terms[1::2])]
    return terms[0]


def after(values, *events):
    return lax.optimization_barrier((values,) + events)[0]


def reduce_core(parts):
    core = lax.axis_index("row") % 2
    return pick(parts, core) + send(pick(parts, 1 - core), 1, 0)


def reduce_plane(own):
    col = lax.axis_index("col")
    others = [send(pick(own, col ^ flip), 0, flip) for flip in range(1, own.shape[0])]
    return tree_sum([pick(own, col)] + others)


def reduce_z(own):
    return tree_sum([own] + [send(own, flip, 0) for flip in range(2, lax.axis_size("row"), 2)])


def spread_plane(part):
    col, cols = lax.axis_index("col"), lax.axis_size("col")
    near = jnp.stack([part] + [send(part, 0, flip) for flip in range(1, cols)])
    return jnp.stack([pick(near, index ^ col) for index in range(cols)])


def spread_core(near):
    core = lax.axis_index("row") % 2
    both = jnp.stack([near, send(near, 1, 0)])
    return jnp.stack([pick(both, core), pick(both, 1 - core)])


def split(x):
    high = x.astype(BF16)
    return high, (x - high.astype(F32)).astype(BF16)


def dot(a, b):
    return jnp.dot(a, b, preferred_element_type=F32)


def dot_nt(a, b):
    return lax.dot_general(a, b, (((1,), (1,)), ((), ())), preferred_element_type=F32)


def divide(x, y):
    return x * pl.reciprocal(y, approx=True)


def prepare_left(left_ref, pair_ref):
    rank = left_ref.shape[1]
    high, low = split(left_ref[...])
    pair_ref[:, :rank] = high
    pair_ref[:, rank : 2 * rank] = low
    pair_ref[:, 2 * rank :] = high


def prepare_left_t(left_ref, pair_t_ref, sums_ref):
    rank = left_ref.shape[1]
    turned = left_ref[...].T
    high, low = split(turned)
    pair_t_ref[:rank, :] = high
    pair_t_ref[rank:, :] = low
    sums_ref[...] = jnp.broadcast_to(jnp.sum(turned, axis=1, keepdims=True), sums_ref.shape)


def chunks(extent, size):
    size = min(size, extent)
    return [pl.ds(start, size) for start in range(0, extent, size)]


def stacked(right):
    high, low = split(right)
    return jnp.concatenate([high, high, low], axis=0)


def quotients(slab_ref, pair_ref, right_stack, rows):
    product = dot(pair_ref[rows, :], right_stack)
    return split(divide(slab_ref[rows, :], product))


def right_update(slab_ref, pair_ref, pair_t_ref, sums_ref, right):
    rank = right.shape[0]
    stack = stacked(right)
    parts = [quotients(slab_ref, pair_ref, stack, rows) for rows in chunks(slab_ref.shape[0], ROWS)]
    both = dot(pair_t_ref[...], jnp.concatenate([high for high, _ in parts], axis=0))
    numerator = both[:rank] + both[rank:]
    numerator = numerator + dot(
        pair_t_ref[:rank, :], jnp.concatenate([low for _, low in parts], axis=0)
    )
    return right * numerator / sums_ref[:, :1]


def left_numerator(slab_ref, pair_ref, right, total_ref, sums_ref, first):
    rank = right.shape[0]
    stack = stacked(right)
    right_high, right_low = stack[:rank], stack[2 * rank :]
    right_both = jnp.concatenate([right_high, right_low], axis=0)
    row_sums = dot_nt(jnp.ones((16, right.shape[1]), BF16), right_both)[:PAD]
    row_sums = row_sums[:, :rank] + row_sums[:, rank:]
    sums_ref[...] = jnp.where(first, row_sums, sums_ref[...] + row_sums)
    for rows in chunks(slab_ref.shape[0], ROWS):
        high, low = quotients(slab_ref, pair_ref, stack, rows)
        both = dot_nt(high, right_both)
        term = both[:, :rank] + both[:, rank:] + dot_nt(low, right_high)
        total_ref[rows, :] = jnp.where(first, term, total_ref[rows, :] + term)


def write_left(total_ref, row_sums_ref, extra_ref, out_ref):
    parts, tall, rank = out_ref.shape
    height = tall - PAD
    first = lax.broadcasted_iota(jnp.int32, (PAD, rank), 0) == 0
    stats = jnp.where(first, row_sums_ref[...], extra_ref[:1, :])
    for part in range(parts):
        out_ref[part, :height, :] = total_ref[pl.ds(part * height, height), :]
        out_ref[part, height:, :] = stats


def turn_kernel(
    slab_ref, left_ref, right_ref, extra_ref, right_out, left_out,
    pair_ref, pair_t_ref, sums_ref, total_ref, row_sums_ref,
):
    step = pl.program_id(0)

    @pl.when(step == 0)
    def _():
        prepare_left(left_ref, pair_ref)
        prepare_left_t(left_ref, pair_t_ref, sums_ref)

    right = right_update(slab_ref, pair_ref, pair_t_ref, sums_ref, right_ref[...])
    right_out[...] = right
    left_numerator(slab_ref, pair_ref, right, total_ref, row_sums_ref, step == 0)

    @pl.when(step == pl.num_programs(0) - 1)
    def _():
        write_left(total_ref, row_sums_ref, extra_ref, left_out)


def second_quotient(block, second_left, pairs):
    high, low = split(second_left)
    right_high, right_low = pairs
    product = dot(high, right_high) + (dot(low, right_high) + dot(high, right_low))
    return split(divide(block, product))


def numerator_kernel(slices, right_ref, second_left_ref, second_right_ref, numer_out):
    rank = right_ref.shape[0]
    k = right_ref.shape[1] // slices
    pairs = split(
        jnp.concatenate([second_right_ref[block] for block in range(k // rank)], axis=1)
    )
    total = 0.0
    for index in range(slices):
        second_left = second_left_ref[pl.ds(index, rank, stride=slices), :]
        high, low = second_quotient(right_ref[:, pl.ds(index * k, k)], second_left, pairs)
        left_high, left_low = split(second_left.T)
        total = total + (dot(left_high, high) + (dot(left_low, high) + dot(left_high, low)))
    for block in range(k // rank):
        numer_out[block] = total[:, block * rank : (block + 1) * rank]


def second_kernel(slices, right_ref, second_left_ref, second_right_ref, out_ref):
    rank = right_ref.shape[0]
    k = right_ref.shape[1] // slices
    second_right = jnp.concatenate(
        [second_right_ref[block] for block in range(k // rank)], axis=1
    )
    right_high, right_low = split(second_right)
    right_both = jnp.concatenate([right_high, right_low], axis=0)
    sums = dot_nt(jnp.ones((16, k), BF16), right_both)[:1]
    scale = 1.0 / (sums[:, :rank] + sums[:, rank:])
    for index in range(slices):
        rows = pl.ds(index, rank, stride=slices)
        second_left = second_left_ref[rows, :]
        high, low = second_quotient(
            right_ref[:, pl.ds(index * k, k)], second_left, (right_high, right_low)
        )
        both = dot_nt(high, right_both)
        numer = both[:, :rank] + both[:, rank:] + dot_nt(low, right_high)
        out_ref[rows, :] = second_left * numer * scale


def full(shape):
    return pl.BlockSpec(shape, lambda step: (0,) * len(shape))


def params(vmem_bytes):
    return pltpu.CompilerParams(
        dimension_semantics=("arbitrary",), vmem_limit_bytes=vmem_bytes
    )


def left_scratch(m, rank):
    return [pltpu.VMEM((m, 3 * rank), BF16)]


def right_scratch(m, rank):
    return [pltpu.VMEM((2 * rank, m), BF16), pltpu.VMEM((rank, rank), F32)]


def total_scratch(m, rank):
    return [pltpu.VMEM((m, rank), F32), pltpu.VMEM((PAD, rank), F32)]


def cost(m, rank, columns, dots):
    return pl.CostEstimate(
        flops=6 * dots * m * rank * columns, bytes_accessed=4 * m * columns, transcendentals=0
    )


def full_turn(slab, left, right, extra, block, parts, vmem_bytes):
    (m, columns), rank = slab.shape, left.shape[1]
    columns_spec = lambda height: pl.BlockSpec((height, block), lambda step: (0, step))
    tall = m // parts + PAD
    return pl.pallas_call(
        turn_kernel,
        grid=(columns // block,),
        in_specs=[columns_spec(m), full((m, rank)), columns_spec(rank), full((min(PAD, extra.shape[0]), rank))],
        out_specs=[columns_spec(rank), full((parts, tall, rank))],
        out_shape=[
            jax.ShapeDtypeStruct((rank, columns), F32),
            jax.ShapeDtypeStruct((parts, tall, rank), F32),
        ],
        scratch_shapes=left_scratch(m, rank)
        + right_scratch(m, rank)
        + total_scratch(m, rank),
        compiler_params=params(vmem_bytes),
        cost_estimate=cost(m, rank, columns, 4),
        name="turn",
    )(slab, left, right, extra)


def second_numerator(right, second_left, second_right, slices):
    return pl.pallas_call(
        functools.partial(numerator_kernel, slices),
        out_shape=jax.ShapeDtypeStruct(second_right.shape, F32),
        compiler_params=pltpu.CompilerParams(vmem_limit_bytes=VMEM_BYTES),
        cost_estimate=cost(right.shape[0], right.shape[0], right.shape[1], 2),
        name="second_numerator",
    )(right, second_left, second_right)


def second_rows_out(right, second_left, second_right, slices):
    return pl.pallas_call(
        functools.partial(second_kernel, slices),
        out_shape=jax.ShapeDtypeStruct(second_left.shape, F32),
        compiler_params=pltpu.CompilerParams(vmem_limit_bytes=VMEM_BYTES),
        cost_estimate=cost(right.shape[0], right.shape[0], right.shape[1], 2),
        name="second_rows",
    )(right, second_left, second_right)


def prepare_kernel(slices, place_ref, second_left_ref, second_right_ref, left_ref, out_ref, sums_out, left_out):
    devices, tall, rank = out_ref.shape
    second_left = second_left_ref[...]
    sums_out[...] = jnp.sum(second_left, axis=0, keepdims=True)
    left_out[...] = left_ref[...]
    per_owner = second_left.shape[0] // (devices * slices)
    for index in range(per_owner):
        for device in range(devices):
            start = (index * devices + device) * slices
            out_ref[device, index * slices : (index + 1) * slices, :] = second_left[
                start : start + slices
            ]
    rows = tall - per_owner * slices
    piece = second_right_ref[...]
    piece = jnp.concatenate(
        [piece[start : start + rows] for start in range(0, piece.shape[0], rows)], axis=1
    )
    for device in range(devices):
        out_ref[device, per_owner * slices :, :] = piece


def prepare(place, second_left, second_right, left, sizes):
    devices, slices, second_rows, piece_rows, rows_own = sizes
    rank, width = left.shape[1], second_right.shape[1]
    tall = second_rows // devices + piece_rows * width // rank
    block = lambda shape, which: pl.BlockSpec(shape, lambda step, place: (place[which], 0))
    fixed = lambda shape: pl.BlockSpec(shape, lambda step, place: (0,) * len(shape))
    return pl.pallas_call(
        functools.partial(prepare_kernel, slices),
        grid_spec=pltpu.PrefetchScalarGridSpec(
            num_scalar_prefetch=1,
            grid=(1,),
            in_specs=[
                block((second_rows, rank), 0),
                block((piece_rows, width), 1),
                block((rows_own, rank), 2),
            ],
            out_specs=[fixed((devices, tall, rank)), fixed((1, rank)), fixed((rows_own, rank))],
        ),
        out_shape=[
            jax.ShapeDtypeStruct((devices, tall, rank), F32),
            jax.ShapeDtypeStruct((1, rank), F32),
            jax.ShapeDtypeStruct((rows_own, rank), F32),
        ],
        compiler_params=params(PREP_KIB * 1024),
        cost_estimate=pl.CostEstimate(
            flops=second_rows * rank, bytes_accessed=12 * second_rows * rank, transcendentals=0
        ),
        name="prepare",
    )(place, second_left, second_right, left)


def body(tensor_slab, left_init, right_init, second_left_init, second_right_init):
    row_devices = lax.axis_size("row")
    col_devices = lax.axis_size("col")
    devices = row_devices * col_devices
    own_part = (lax.axis_index("row") % 2) * col_devices + lax.axis_index("col")
    parts = 2 * col_devices
    m, rank = left_init.shape
    k = second_right_init.shape[1] * col_devices
    slices = right_init.shape[1] // k
    per_owner = rank // devices
    rows_own = m // parts

    second_rows = second_left_init.shape[0] // col_devices
    piece_rows = rank // row_devices
    groups = rank // second_right_init.shape[1]
    place = jnp.stack([lax.axis_index("col"), lax.axis_index("row"), own_part]).astype(jnp.int32)
    second_factors, col_part, own_init = prepare(
        place, second_left_init, second_right_init, left_init,
        (devices, slices, second_rows, piece_rows, rows_own),
    )
    arrived = exchange(second_factors)

    def own_rows(left):
        return lax.dynamic_slice_in_dim(left, own_part * rows_own, rows_own, 0)

    def own_left_rows(own, total):
        return own * total[:rows_own] / total[rows_own][None, :]

    right, summed = full_turn(
        tensor_slab, left_init, right_init, left_init, k, parts, T1_MIB * MIB
    )
    summed, arrived = lax.optimization_barrier((summed, arrived))
    summed = summed.reshape(2, col_devices, rows_own + PAD, rank)
    total = reduce_z(reduce_plane(reduce_core(summed)))
    left = spread_core(spread_plane(own_left_rows(own_init, total))).reshape(m, rank)
    right, summed = full_turn(tensor_slab, left, right, col_part, k, parts, VMEM_BYTES)
    second_left = arrived[:, : per_owner * slices].reshape(rank * slices, rank)
    whole = arrived[:, per_owner * slices :].reshape(
        row_devices, col_devices, piece_rows // groups, groups, -1
    )
    whole = whole.transpose(0, 3, 2, 1, 4).reshape(rank, k // rank, rank).transpose(1, 0, 2)
    numerator = second_numerator(right, second_left, whole, slices)

    rows_part = k // parts
    summed = summed.reshape(2, col_devices, rows_own + PAD, rank)
    numerator = numerator.reshape(2, col_devices, rows_part, rank)
    total = reduce_z(reduce_plane(reduce_core(jnp.concatenate([summed, numerator], axis=2))))
    init_over = (whole / total[rows_own + 1][None, :, None]).reshape(k, rank)
    init_over = lax.dynamic_slice_in_dim(init_over, own_part * rows_part, rows_part, 0)
    second_part = init_over * total[rows_own + PAD :]
    both = spread_core(
        spread_plane(jnp.concatenate([own_left_rows(own_rows(left), total), second_part], axis=0))
    )
    left_out = both[:, :, :rows_own].reshape(m, rank)
    second_right = both[:, :, rows_own:].reshape(k // rank, rank, rank)
    rows_out = second_rows_out(right, second_left, second_right, slices)
    returned = exchange(rows_out.reshape(devices, per_owner * slices, rank))
    returned = returned.reshape(devices, per_owner, slices, rank).transpose(1, 0, 2, 3)
    return (left_out, returned.reshape(second_rows, rank))


def solution(mesh):
    placed = (P(None, AXES), P(), P(None, AXES), P("row", None), P(None, "col"))
    return jax.shard_map(
        body, mesh=mesh, in_specs=placed, out_specs=(P(), P(AXES, None)), check_vma=False
    )
```

```python
import functools

import jax
import jax.numpy as jnp
from jax import lax
from jax.experimental import pallas as pl
from jax.experimental.pallas import tpu as pltpu
from jax.sharding import PartitionSpec as P

AXES = ("row", "col")
F32, BF16 = jnp.float32, jnp.bfloat16
PAD = 8
ROWS = 1024
MIB = 1024 * 1024
T1_MIB = 52
PREP_KIB = 54528
VMEM_BYTES = 51 * MIB


def exchange(parts):
    return lax.all_to_all(parts, AXES, split_axis=0, concat_axis=0, tiled=True)


def send(values, row_flip, col_flip):
    rows, cols = lax.axis_size("row"), lax.axis_size("col")
    pairs = [
        (r * cols + c, (r ^ row_flip) * cols + (c ^ col_flip))
        for r in range(rows)
        for c in range(cols)
    ]
    return lax.ppermute(values, AXES, pairs)


def pick(values, index):
    return lax.dynamic_index_in_dim(values, index, 0, keepdims=False)


def tree_sum(terms):
    while len(terms) > 1:
        terms = [a + b for a, b in zip(terms[::2], terms[1::2])]
    return terms[0]


def after(values, *events):
    return lax.optimization_barrier((values,) + events)[0]


def reduce_core(parts):
    core = lax.axis_index("row") % 2
    return pick(parts, core) + send(pick(parts, 1 - core), 1, 0)


def reduce_plane(own):
    col = lax.axis_index("col")
    others = [send(pick(own, col ^ flip), 0, flip) for flip in range(1, own.shape[0])]
    return tree_sum([pick(own, col)] + others)


def reduce_z(own):
    return tree_sum([own] + [send(own, flip, 0) for flip in range(2, lax.axis_size("row"), 2)])


def spread_plane(part):
    col, cols = lax.axis_index("col"), lax.axis_size("col")
    near = jnp.stack([part] + [send(part, 0, flip) for flip in range(1, cols)])
    return jnp.stack([pick(near, index ^ col) for index in range(cols)])


def spread_core(near):
    core = lax.axis_index("row") % 2
    both = jnp.stack([near, send(near, 1, 0)])
    return jnp.stack([pick(both, core), pick(both, 1 - core)])


def split(x):
    high = x.astype(BF16)
    return high, (x - high.astype(F32)).astype(BF16)


def dot(a, b):
    return jnp.dot(a, b, preferred_element_type=F32)


def dot_nt(a, b):
    return lax.dot_general(a, b, (((1,), (1,)), ((), ())), preferred_element_type=F32)


def divide(x, y):
    return x * pl.reciprocal(y, approx=True)


def prepare_left(left_ref, pair_ref):
    rank = left_ref.shape[1]
    high, low = split(left_ref[...])
    pair_ref[:, :rank] = high
    pair_ref[:, rank : 2 * rank] = low
    pair_ref[:, 2 * rank :] = high


def prepare_left_t(left_ref, pair_t_ref, sums_ref):
    rank = left_ref.shape[1]
    turned = left_ref[...].T
    high, low = split(turned)
    pair_t_ref[:rank, :] = high
    pair_t_ref[rank:, :] = low
    sums_ref[...] = jnp.broadcast_to(jnp.sum(turned, axis=1, keepdims=True), sums_ref.shape)


def chunks(extent, size):
    size = min(size, extent)
    return [pl.ds(start, size) for start in range(0, extent, size)]


def stacked(right):
    high, low = split(right)
    return jnp.concatenate([high, high, low], axis=0)


def quotients(slab_ref, pair_ref, right_stack, rows):
    product = dot(pair_ref[rows, :], right_stack)
    return split(divide(slab_ref[rows, :], product))


def right_update(slab_ref, pair_ref, pair_t_ref, sums_ref, right):
    rank = right.shape[0]
    stack = stacked(right)
    parts = [quotients(slab_ref, pair_ref, stack, rows) for rows in chunks(slab_ref.shape[0], ROWS)]
    both = dot(pair_t_ref[...], jnp.concatenate([high for high, _ in parts], axis=0))
    numerator = both[:rank] + both[rank:]
    numerator = numerator + dot(
        pair_t_ref[:rank, :], jnp.concatenate([low for _, low in parts], axis=0)
    )
    return right * numerator / sums_ref[:, :1]


def left_numerator(slab_ref, pair_ref, right, total_ref, sums_ref, first):
    rank = right.shape[0]
    stack = stacked(right)
    right_high, right_low = stack[:rank], stack[2 * rank :]
    right_both = jnp.concatenate([right_high, right_low], axis=0)
    row_sums = dot_nt(jnp.ones((16, right.shape[1]), BF16), right_both)[:PAD]
    row_sums = row_sums[:, :rank] + row_sums[:, rank:]
    sums_ref[...] = jnp.where(first, row_sums, sums_ref[...] + row_sums)
    for rows in chunks(slab_ref.shape[0], ROWS):
        high, low = quotients(slab_ref, pair_ref, stack, rows)
        both = dot_nt(high, right_both)
        term = both[:, :rank] + both[:, rank:] + dot_nt(low, right_high)
        total_ref[rows, :] = jnp.where(first, term, total_ref[rows, :] + term)


def write_left(total_ref, row_sums_ref, extra_ref, out_ref):
    parts, tall, rank = out_ref.shape
    height = tall - PAD
    first = lax.broadcasted_iota(jnp.int32, (PAD, rank), 0) == 0
    stats = jnp.where(first, row_sums_ref[...], extra_ref[:1, :])
    for part in range(parts):
        out_ref[part, :height, :] = total_ref[pl.ds(part * height, height), :]
        out_ref[part, height:, :] = stats


def turn_kernel(
    slab_ref, left_ref, right_ref, extra_ref, right_out, left_out,
    pair_ref, pair_t_ref, sums_ref, total_ref, row_sums_ref,
):
    step = pl.program_id(0)

    @pl.when(step == 0)
    def _():
        prepare_left(left_ref, pair_ref)
        prepare_left_t(left_ref, pair_t_ref, sums_ref)

    right = right_update(slab_ref, pair_ref, pair_t_ref, sums_ref, right_ref[...])
    right_out[...] = right
    left_numerator(slab_ref, pair_ref, right, total_ref, row_sums_ref, step == 0)

    @pl.when(step == pl.num_programs(0) - 1)
    def _():
        write_left(total_ref, row_sums_ref, extra_ref, left_out)


def second_quotient(block, second_left, pairs):
    high, low = split(second_left)
    right_high, right_low = pairs
    product = dot(high, right_high) + (dot(low, right_high) + dot(high, right_low))
    return split(divide(block, product))


def numerator_kernel(slices, right_ref, second_left_ref, second_right_ref, numer_out):
    rank = right_ref.shape[0]
    k = right_ref.shape[1] // slices
    pairs = split(
        jnp.concatenate([second_right_ref[block] for block in range(k // rank)], axis=1)
    )
    total = 0.0
    for index in range(slices):
        second_left = second_left_ref[pl.ds(index, rank, stride=slices), :]
        high, low = second_quotient(right_ref[:, pl.ds(index * k, k)], second_left, pairs)
        left_high, left_low = split(second_left.T)
        total = total + (dot(left_high, high) + (dot(left_low, high) + dot(left_high, low)))
    for block in range(k // rank):
        numer_out[block] = total[:, block * rank : (block + 1) * rank]


def second_kernel(slices, right_ref, second_left_ref, second_right_ref, out_ref):
    rank = right_ref.shape[0]
    k = right_ref.shape[1] // slices
    second_right = jnp.concatenate(
        [second_right_ref[block] for block in range(k // rank)], axis=1
    )
    right_high, right_low = split(second_right)
    right_both = jnp.concatenate([right_high, right_low], axis=0)
    sums = dot_nt(jnp.ones((16, k), BF16), right_both)[:1]
    scale = 1.0 / (sums[:, :rank] + sums[:, rank:])
    for index in range(slices):
        rows = pl.ds(index, rank, stride=slices)
        second_left = second_left_ref[rows, :]
        high, low = second_quotient(
            right_ref[:, pl.ds(index * k, k)], second_left, (right_high, right_low)
        )
        both = dot_nt(high, right_both)
        numer = both[:, :rank] + both[:, rank:] + dot_nt(low, right_high)
        out_ref[rows, :] = second_left * numer * scale


def full(shape):
    return pl.BlockSpec(shape, lambda step: (0,) * len(shape))


def params(vmem_bytes):
    return pltpu.CompilerParams(
        dimension_semantics=("arbitrary",), vmem_limit_bytes=vmem_bytes
    )


def left_scratch(m, rank):
    return [pltpu.VMEM((m, 3 * rank), BF16)]


def right_scratch(m, rank):
    return [pltpu.VMEM((2 * rank, m), BF16), pltpu.VMEM((rank, rank), F32)]


def total_scratch(m, rank):
    return [pltpu.VMEM((m, rank), F32), pltpu.VMEM((PAD, rank), F32)]


def cost(m, rank, columns, dots):
    return pl.CostEstimate(
        flops=6 * dots * m * rank * columns, bytes_accessed=4 * m * columns, transcendentals=0
    )


def full_turn(slab, left, right, extra, block, parts, vmem_bytes):
    (m, columns), rank = slab.shape, left.shape[1]
    columns_spec = lambda height: pl.BlockSpec((height, block), lambda step: (0, step))
    tall = m // parts + PAD
    return pl.pallas_call(
        turn_kernel,
        grid=(columns // block,),
        in_specs=[columns_spec(m), full((m, rank)), columns_spec(rank), full((1, rank))],
        out_specs=[columns_spec(rank), full((parts, tall, rank))],
        out_shape=[
            jax.ShapeDtypeStruct((rank, columns), F32),
            jax.ShapeDtypeStruct((parts, tall, rank), F32),
        ],
        scratch_shapes=left_scratch(m, rank)
        + right_scratch(m, rank)
        + total_scratch(m, rank),
        compiler_params=params(vmem_bytes),
        cost_estimate=cost(m, rank, columns, 4),
        name="turn",
    )(slab, left, right, extra)


def second_numerator(right, second_left, second_right, slices):
    return pl.pallas_call(
        functools.partial(numerator_kernel, slices),
        out_shape=jax.ShapeDtypeStruct(second_right.shape, F32),
        compiler_params=pltpu.CompilerParams(vmem_limit_bytes=VMEM_BYTES),
        cost_estimate=cost(right.shape[0], right.shape[0], right.shape[1], 2),
        name="second_numerator",
    )(right, second_left, second_right)


def second_rows_out(right, second_left, second_right, slices):
    return pl.pallas_call(
        functools.partial(second_kernel, slices),
        out_shape=jax.ShapeDtypeStruct(second_left.shape, F32),
        compiler_params=pltpu.CompilerParams(vmem_limit_bytes=VMEM_BYTES),
        cost_estimate=cost(right.shape[0], right.shape[0], right.shape[1], 2),
        name="second_rows",
    )(right, second_left, second_right)


def prepare_kernel(slices, place_ref, second_left_ref, second_right_ref, left_ref, out_ref, sums_out, left_out):
    devices, tall, rank = out_ref.shape
    second_left = second_left_ref[...]
    sums_out[...] = jnp.sum(second_left, axis=0, keepdims=True)
    left_out[...] = left_ref[...]
    per_owner = second_left.shape[0] // (devices * slices)
    for index in range(per_owner):
        for device in range(devices):
            start = (index * devices + device) * slices
            out_ref[device, index * slices : (index + 1) * slices, :] = second_left[
                start : start + slices
            ]
    rows = tall - per_owner * slices
    piece = second_right_ref[...]
    piece = jnp.concatenate(
        [piece[start : start + rows] for start in range(0, piece.shape[0], rows)], axis=1
    )
    for device in range(devices):
        out_ref[device, per_owner * slices :, :] = piece


def prepare(place, second_left, second_right, left, sizes):
    devices, slices, second_rows, piece_rows, rows_own = sizes
    rank, width = left.shape[1], second_right.shape[1]
    tall = second_rows // devices + piece_rows * width // rank
    block = lambda shape, which: pl.BlockSpec(shape, lambda step, place: (place[which], 0))
    fixed = lambda shape: pl.BlockSpec(shape, lambda step, place: (0,) * len(shape))
    return pl.pallas_call(
        functools.partial(prepare_kernel, slices),
        grid_spec=pltpu.PrefetchScalarGridSpec(
            num_scalar_prefetch=1,
            grid=(1,),
            in_specs=[
                block((second_rows, rank), 0),
                block((piece_rows, width), 1),
                block((rows_own, rank), 2),
            ],
            out_specs=[fixed((devices, tall, rank)), fixed((1, rank)), fixed((rows_own, rank))],
        ),
        out_shape=[
            jax.ShapeDtypeStruct((devices, tall, rank), F32),
            jax.ShapeDtypeStruct((1, rank), F32),
            jax.ShapeDtypeStruct((rows_own, rank), F32),
        ],
        compiler_params=params(PREP_KIB * 1024),
        cost_estimate=pl.CostEstimate(
            flops=second_rows * rank, bytes_accessed=12 * second_rows * rank, transcendentals=0
        ),
        name="prepare",
    )(place, second_left, second_right, left)


def body(tensor_slab, left_init, right_init, second_left_init, second_right_init):
    row_devices = lax.axis_size("row")
    col_devices = lax.axis_size("col")
    devices = row_devices * col_devices
    own_part = (lax.axis_index("row") % 2) * col_devices + lax.axis_index("col")
    parts = 2 * col_devices
    m, rank = left_init.shape
    k = second_right_init.shape[1] * col_devices
    slices = right_init.shape[1] // k
    per_owner = rank // devices
    rows_own = m // parts

    second_rows = second_left_init.shape[0] // col_devices
    piece_rows = rank // row_devices
    groups = rank // second_right_init.shape[1]
    place = jnp.stack([lax.axis_index("col"), lax.axis_index("row"), own_part]).astype(jnp.int32)
    second_factors, col_part, own_init = prepare(
        place, second_left_init, second_right_init, left_init,
        (devices, slices, second_rows, piece_rows, rows_own),
    )
    arrived = exchange(second_factors)

    def own_rows(left):
        return lax.dynamic_slice_in_dim(left, own_part * rows_own, rows_own, 0)

    def own_left_rows(own, total):
        return own * total[:rows_own] / total[rows_own][None, :]

    right, summed = full_turn(
        tensor_slab, left_init, right_init, col_part, k, parts, T1_MIB * MIB
    )
    summed, arrived = lax.optimization_barrier((summed, arrived))
    summed = summed.reshape(2, col_devices, rows_own + PAD, rank)
    total = reduce_z(reduce_plane(reduce_core(summed)))
    left = spread_core(spread_plane(own_left_rows(own_init, total))).reshape(m, rank)
    right, summed = full_turn(tensor_slab, left, right, col_part, k, parts, VMEM_BYTES)
    second_left = arrived[:, : per_owner * slices].reshape(rank * slices, rank)
    whole = arrived[:, per_owner * slices :].reshape(
        row_devices, col_devices, piece_rows // groups, groups, -1
    )
    whole = whole.transpose(0, 3, 2, 1, 4).reshape(rank, k // rank, rank).transpose(1, 0, 2)
    numerator = second_numerator(right, second_left, whole, slices)

    rows_part = k // parts
    summed = summed.reshape(2, col_devices, rows_own + PAD, rank)
    numerator = numerator.reshape(2, col_devices, rows_part, rank)
    total = reduce_z(reduce_plane(reduce_core(jnp.concatenate([summed, numerator], axis=2))))
    init_over = (whole / total[rows_own + 1][None, :, None]).reshape(k, rank)
    init_over = lax.dynamic_slice_in_dim(init_over, own_part * rows_part, rows_part, 0)
    second_part = init_over * total[rows_own + PAD :]
    both = spread_core(
        spread_plane(jnp.concatenate([own_left_rows(own_rows(left), total), second_part], axis=0))
    )
    left_out = both[:, :, :rows_own].reshape(m, rank)
    second_right = both[:, :, rows_own:].reshape(k // rank, rank, rank)
    rows_out = second_rows_out(right, second_left, second_right, slices)
    returned = exchange(rows_out.reshape(devices, per_owner * slices, rank))
    returned = returned.reshape(devices, per_owner, slices, rank).transpose(1, 0, 2, 3)
    return (left_out, returned.reshape(second_rows, rank))


def solution(mesh):
    placed = (P(None, AXES), P(), P(None, AXES), P("row", None), P(None, "col"))
    return jax.shard_map(
        body, mesh=mesh, in_specs=placed, out_specs=(P(), P(AXES, None)), check_vma=False
    )
```

```python
import functools

import jax
import jax.numpy as jnp
from jax import lax
from jax.experimental import pallas as pl
from jax.experimental.pallas import tpu as pltpu
from jax.sharding import PartitionSpec as P

AXES = ("row", "col")
F32, BF16 = jnp.float32, jnp.bfloat16
PAD = 8
ROWS = 1024
MIB = 1024 * 1024
T1_MIB = 51
T2_MIB = 42
PREP_KIB = 54528
VMEM_BYTES = 51 * MIB


def exchange(parts):
    return lax.all_to_all(parts, AXES, split_axis=0, concat_axis=0, tiled=True)


def send(values, row_flip, col_flip):
    rows, cols = lax.axis_size("row"), lax.axis_size("col")
    pairs = [
        (r * cols + c, (r ^ row_flip) * cols + (c ^ col_flip))
        for r in range(rows)
        for c in range(cols)
    ]
    return lax.ppermute(values, AXES, pairs)


def pick(values, index):
    return lax.dynamic_index_in_dim(values, index, 0, keepdims=False)


def tree_sum(terms):
    while len(terms) > 1:
        terms = [a + b for a, b in zip(terms[::2], terms[1::2])]
    return terms[0]


def after(values, *events):
    return lax.optimization_barrier((values,) + events)[0]


def reduce_core(parts):
    core = lax.axis_index("row") % 2
    return pick(parts, core) + send(pick(parts, 1 - core), 1, 0)


def reduce_plane(own):
    col = lax.axis_index("col")
    others = [send(pick(own, col ^ flip), 0, flip) for flip in range(1, own.shape[0])]
    return tree_sum([pick(own, col)] + others)


def reduce_z(own):
    return tree_sum([own] + [send(own, flip, 0) for flip in range(2, lax.axis_size("row"), 2)])


def spread_plane(part):
    col, cols = lax.axis_index("col"), lax.axis_size("col")
    near = jnp.stack([part] + [send(part, 0, flip) for flip in range(1, cols)])
    return jnp.stack([pick(near, index ^ col) for index in range(cols)])


def spread_core(near):
    core = lax.axis_index("row") % 2
    both = jnp.stack([near, send(near, 1, 0)])
    return jnp.stack([pick(both, core), pick(both, 1 - core)])


def split(x):
    high = x.astype(BF16)
    return high, (x - high.astype(F32)).astype(BF16)


def dot(a, b):
    return jnp.dot(a, b, preferred_element_type=F32)


def dot_nt(a, b):
    return lax.dot_general(a, b, (((1,), (1,)), ((), ())), preferred_element_type=F32)


def divide(x, y):
    return x * pl.reciprocal(y, approx=True)


def prepare_left(left_ref, pair_ref):
    rank = left_ref.shape[1]
    high, low = split(left_ref[...])
    pair_ref[:, :rank] = high
    pair_ref[:, rank : 2 * rank] = low
    pair_ref[:, 2 * rank :] = high


def prepare_left_t(left_ref, pair_t_ref, sums_ref):
    rank = left_ref.shape[1]
    turned = left_ref[...].T
    high, low = split(turned)
    pair_t_ref[:rank, :] = high
    pair_t_ref[rank:, :] = low
    sums_ref[...] = jnp.broadcast_to(jnp.sum(turned, axis=1, keepdims=True), sums_ref.shape)


def chunks(extent, size):
    size = min(size, extent)
    return [pl.ds(start, size) for start in range(0, extent, size)]


def stacked(right):
    high, low = split(right)
    return jnp.concatenate([high, high, low], axis=0)


def quotients(slab_ref, pair_ref, right_stack, rows):
    product = dot(pair_ref[rows, :], right_stack)
    return split(divide(slab_ref[rows, :], product))


def right_update(slab_ref, pair_ref, pair_t_ref, sums_ref, right):
    rank = right.shape[0]
    stack = stacked(right)
    parts = [quotients(slab_ref, pair_ref, stack, rows) for rows in chunks(slab_ref.shape[0], ROWS)]
    both = dot(pair_t_ref[...], jnp.concatenate([high for high, _ in parts], axis=0))
    numerator = both[:rank] + both[rank:]
    numerator = numerator + dot(
        pair_t_ref[:rank, :], jnp.concatenate([low for _, low in parts], axis=0)
    )
    return right * numerator / sums_ref[:, :1]


def left_numerator(slab_ref, pair_ref, right, total_ref, sums_ref, first):
    rank = right.shape[0]
    stack = stacked(right)
    right_high, right_low = stack[:rank], stack[2 * rank :]
    right_both = jnp.concatenate([right_high, right_low], axis=0)
    row_sums = dot_nt(jnp.ones((16, right.shape[1]), BF16), right_both)[:PAD]
    row_sums = row_sums[:, :rank] + row_sums[:, rank:]
    sums_ref[...] = jnp.where(first, row_sums, sums_ref[...] + row_sums)
    for rows in chunks(slab_ref.shape[0], ROWS):
        high, low = quotients(slab_ref, pair_ref, stack, rows)
        both = dot_nt(high, right_both)
        term = both[:, :rank] + both[:, rank:] + dot_nt(low, right_high)
        total_ref[rows, :] = jnp.where(first, term, total_ref[rows, :] + term)


def write_left(total_ref, row_sums_ref, extra_ref, out_ref):
    parts, tall, rank = out_ref.shape
    height = tall - PAD
    first = lax.broadcasted_iota(jnp.int32, (PAD, rank), 0) == 0
    stats = jnp.where(first, row_sums_ref[...], extra_ref[:1, :])
    for part in range(parts):
        out_ref[part, :height, :] = total_ref[pl.ds(part * height, height), :]
        out_ref[part, height:, :] = stats


def second_quotient(block, second_left, pairs):
    high, low = split(second_left)
    right_high, right_low = pairs
    product = dot(high, right_high) + (dot(low, right_high) + dot(high, right_low))
    return split(divide(block, product))


def turn_body(
    slab_ref, left_ref, right_ref, extra_ref, right_out, left_out,
    pair_ref, pair_t_ref, sums_ref, total_ref, row_sums_ref,
):
    step = pl.program_id(0)

    @pl.when(step == 0)
    def _():
        prepare_left(left_ref, pair_ref)
        prepare_left_t(left_ref, pair_t_ref, sums_ref)

    right = right_update(slab_ref, pair_ref, pair_t_ref, sums_ref, right_ref[...])
    right_out[...] = right
    left_numerator(slab_ref, pair_ref, right, total_ref, row_sums_ref, step == 0)

    @pl.when(step == pl.num_programs(0) - 1)
    def _():
        write_left(total_ref, row_sums_ref, extra_ref, left_out)

    return step, right


def turn_kernel(*refs):
    turn_body(*refs)


def last_turn_kernel(
    slab_ref, left_ref, right_ref, extra_ref, second_left_ref, second_right_ref,
    right_out, left_out, numer_out, *scratch,
):
    step, right = turn_body(
        slab_ref, left_ref, right_ref, extra_ref, right_out, left_out, *scratch
    )
    rank, k = right.shape
    slices = pl.num_programs(0)
    second_left = second_left_ref[pl.ds(step, rank, stride=slices), :]
    second_right = jnp.concatenate(
        [second_right_ref[block] for block in range(k // rank)], axis=1
    )
    high, low = second_quotient(right, second_left, split(second_right))
    left_high, left_low = split(second_left.T)
    term = dot(left_high, high) + (dot(left_low, high) + dot(left_high, low))
    for block in range(k // rank):
        part = term[:, block * rank : (block + 1) * rank]
        numer_out[block] = jnp.where(step == 0, part, numer_out[block] + part)


def second_kernel(slices, right_ref, second_left_ref, second_right_ref, out_ref):
    rank = right_ref.shape[0]
    k = right_ref.shape[1] // slices
    second_right = jnp.concatenate(
        [second_right_ref[block] for block in range(k // rank)], axis=1
    )
    right_high, right_low = split(second_right)
    right_both = jnp.concatenate([right_high, right_low], axis=0)
    sums = dot_nt(jnp.ones((16, k), BF16), right_both)[:1]
    scale = 1.0 / (sums[:, :rank] + sums[:, rank:])
    for index in range(slices):
        rows = pl.ds(index, rank, stride=slices)
        second_left = second_left_ref[rows, :]
        high, low = second_quotient(
            right_ref[:, pl.ds(index * k, k)], second_left, (right_high, right_low)
        )
        both = dot_nt(high, right_both)
        numer = both[:, :rank] + both[:, rank:] + dot_nt(low, right_high)
        out_ref[rows, :] = second_left * numer * scale


def full(shape):
    return pl.BlockSpec(shape, lambda step: (0,) * len(shape))


def params(vmem_bytes):
    return pltpu.CompilerParams(
        dimension_semantics=("arbitrary",), vmem_limit_bytes=vmem_bytes
    )


def left_scratch(m, rank):
    return [pltpu.VMEM((m, 3 * rank), BF16)]


def right_scratch(m, rank):
    return [pltpu.VMEM((2 * rank, m), BF16), pltpu.VMEM((rank, rank), F32)]


def total_scratch(m, rank):
    return [pltpu.VMEM((m, rank), F32), pltpu.VMEM((PAD, rank), F32)]


def cost(m, rank, columns, dots):
    return pl.CostEstimate(
        flops=6 * dots * m * rank * columns, bytes_accessed=4 * m * columns, transcendentals=0
    )


def full_turn(slab, left, right, extra, block, parts, vmem_bytes, second=()):
    (m, columns), rank = slab.shape, left.shape[1]
    columns_spec = lambda height: pl.BlockSpec((height, block), lambda step: (0, step))
    tall = m // parts + PAD
    out_shapes = [(rank, columns), (parts, tall, rank)] + [factor.shape for factor in second[1:]]
    kernel = last_turn_kernel if second else turn_kernel
    return pl.pallas_call(
        kernel,
        grid=(columns // block,),
        in_specs=[columns_spec(m), full((m, rank)), columns_spec(rank), full((1, rank))]
        + [full(factor.shape) for factor in second],
        out_specs=[columns_spec(rank)] + [full(shape) for shape in out_shapes[1:]],
        out_shape=[jax.ShapeDtypeStruct(shape, F32) for shape in out_shapes],
        scratch_shapes=left_scratch(m, rank)
        + right_scratch(m, rank)
        + total_scratch(m, rank),
        compiler_params=params(vmem_bytes),
        cost_estimate=cost(m, rank, columns, 4),
        name="turn",
    )(slab, left, right, extra, *second)


def second_rows_out(right, second_left, second_right, slices):
    return pl.pallas_call(
        functools.partial(second_kernel, slices),
        out_shape=jax.ShapeDtypeStruct(second_left.shape, F32),
        compiler_params=pltpu.CompilerParams(vmem_limit_bytes=VMEM_BYTES),
        cost_estimate=cost(right.shape[0], right.shape[0], right.shape[1], 2),
        name="second_rows",
    )(right, second_left, second_right)


def prepare_kernel(slices, place_ref, second_left_ref, second_right_ref, left_ref, out_ref, sums_out, left_out):
    devices, tall, rank = out_ref.shape
    second_left = second_left_ref[...]
    sums_out[...] = jnp.sum(second_left, axis=0, keepdims=True)
    left_out[...] = left_ref[...]
    per_owner = second_left.shape[0] // (devices * slices)
    for index in range(per_owner):
        for device in range(devices):
            start = (index * devices + device) * slices
            out_ref[device, index * slices : (index + 1) * slices, :] = second_left[
                start : start + slices
            ]
    rows = tall - per_owner * slices
    piece = second_right_ref[...]
    piece = jnp.concatenate(
        [piece[start : start + rows] for start in range(0, piece.shape[0], rows)], axis=1
    )
    for device in range(devices):
        out_ref[device, per_owner * slices :, :] = piece


def prepare(place, second_left, second_right, left, sizes):
    devices, slices, second_rows, piece_rows, rows_own = sizes
    rank, width = left.shape[1], second_right.shape[1]
    tall = second_rows // devices + piece_rows * width // rank
    block = lambda shape, which: pl.BlockSpec(shape, lambda step, place: (place[which], 0))
    fixed = lambda shape: pl.BlockSpec(shape, lambda step, place: (0,) * len(shape))
    return pl.pallas_call(
        functools.partial(prepare_kernel, slices),
        grid_spec=pltpu.PrefetchScalarGridSpec(
            num_scalar_prefetch=1,
            grid=(1,),
            in_specs=[
                block((second_rows, rank), 0),
                block((piece_rows, width), 1),
                block((rows_own, rank), 2),
            ],
            out_specs=[fixed((devices, tall, rank)), fixed((1, rank)), fixed((rows_own, rank))],
        ),
        out_shape=[
            jax.ShapeDtypeStruct((devices, tall, rank), F32),
            jax.ShapeDtypeStruct((1, rank), F32),
            jax.ShapeDtypeStruct((rows_own, rank), F32),
        ],
        compiler_params=params(PREP_KIB * 1024),
        cost_estimate=pl.CostEstimate(
            flops=second_rows * rank, bytes_accessed=12 * second_rows * rank, transcendentals=0
        ),
        name="prepare",
    )(place, second_left, second_right, left)


def body(tensor_slab, left_init, right_init, second_left_init, second_right_init):
    row_devices = lax.axis_size("row")
    col_devices = lax.axis_size("col")
    devices = row_devices * col_devices
    own_part = (lax.axis_index("row") % 2) * col_devices + lax.axis_index("col")
    parts = 2 * col_devices
    m, rank = left_init.shape
    k = second_right_init.shape[1] * col_devices
    slices = right_init.shape[1] // k
    per_owner = rank // devices
    rows_own = m // parts

    second_rows = second_left_init.shape[0] // col_devices
    piece_rows = rank // row_devices
    groups = rank // second_right_init.shape[1]
    place = jnp.stack([lax.axis_index("col"), lax.axis_index("row"), own_part]).astype(jnp.int32)
    second_factors, col_part, own_init = prepare(
        place, second_left_init, second_right_init, left_init,
        (devices, slices, second_rows, piece_rows, rows_own),
    )
    arrived = exchange(second_factors)

    def own_rows(left):
        return lax.dynamic_slice_in_dim(left, own_part * rows_own, rows_own, 0)

    def own_left_rows(own, total):
        return own * total[:rows_own] / total[rows_own][None, :]

    right, summed = full_turn(
        tensor_slab, left_init, right_init, col_part, k, parts, T1_MIB * MIB
    )
    summed, arrived = lax.optimization_barrier((summed, arrived))
    summed = summed.reshape(2, col_devices, rows_own + PAD, rank)
    total = reduce_z(reduce_plane(reduce_core(summed)))
    left = spread_core(spread_plane(own_left_rows(own_init, total))).reshape(m, rank)
    second_left = arrived[:, : per_owner * slices].reshape(rank * slices, rank)
    whole = arrived[:, per_owner * slices :].reshape(
        row_devices, col_devices, piece_rows // groups, groups, -1
    )
    whole = whole.transpose(0, 3, 2, 1, 4).reshape(rank, k // rank, rank).transpose(1, 0, 2)
    right, summed, numerator = full_turn(
        tensor_slab, left, right, col_part, k, parts, T2_MIB * MIB, (second_left, whole)
    )

    rows_part = k // parts
    summed = summed.reshape(2, col_devices, rows_own + PAD, rank)
    numerator = numerator.reshape(2, col_devices, rows_part, rank)
    total = reduce_z(reduce_plane(reduce_core(jnp.concatenate([summed, numerator], axis=2))))
    init_over = (whole / total[rows_own + 1][None, :, None]).reshape(k, rank)
    init_over = lax.dynamic_slice_in_dim(init_over, own_part * rows_part, rows_part, 0)
    second_part = init_over * total[rows_own + PAD :]
    both = spread_core(
        spread_plane(jnp.concatenate([own_left_rows(own_rows(left), total), second_part], axis=0))
    )
    left_out = both[:, :, :rows_own].reshape(m, rank)
    second_right = both[:, :, rows_own:].reshape(k // rank, rank, rank)
    rows_out = second_rows_out(right, second_left, second_right, slices)
    returned = exchange(rows_out.reshape(devices, per_owner * slices, rank))
    returned = returned.reshape(devices, per_owner, slices, rank).transpose(1, 0, 2, 3)
    return (left_out, returned.reshape(second_rows, rank))


def solution(mesh):
    placed = (P(None, AXES), P(), P(None, AXES), P("row", None), P(None, "col"))
    return jax.shard_map(
        body, mesh=mesh, in_specs=placed, out_specs=(P(), P(AXES, None)), check_vma=False
    )
```

```python
import functools

import jax
import jax.numpy as jnp
from jax import lax
from jax.experimental import pallas as pl
from jax.experimental.pallas import tpu as pltpu
from jax.sharding import PartitionSpec as P

AXES = ("row", "col")
F32, BF16 = jnp.float32, jnp.bfloat16
PAD = 8
ROWS = 1024
MIB = 1024 * 1024
T1_MIB = 52
PREP_KIB = 54528
VMEM_BYTES = 51 * MIB


def exchange(parts):
    return lax.all_to_all(parts, AXES, split_axis=0, concat_axis=0, tiled=True)


def send(values, row_flip, col_flip):
    rows, cols = lax.axis_size("row"), lax.axis_size("col")
    pairs = [
        (r * cols + c, (r ^ row_flip) * cols + (c ^ col_flip))
        for r in range(rows)
        for c in range(cols)
    ]
    return lax.ppermute(values, AXES, pairs)


def pick(values, index):
    return lax.dynamic_index_in_dim(values, index, 0, keepdims=False)


def tree_sum(terms):
    while len(terms) > 1:
        terms = [a + b for a, b in zip(terms[::2], terms[1::2])]
    return terms[0]


def after(values, *events):
    return lax.optimization_barrier((values,) + events)[0]


def reduce_core(parts):
    core = lax.axis_index("row") % 2
    return pick(parts, core) + send(pick(parts, 1 - core), 1, 0)


def reduce_plane(own):
    col = lax.axis_index("col")
    others = [send(pick(own, col ^ flip), 0, flip) for flip in range(1, own.shape[0])]
    return tree_sum([pick(own, col)] + others)


def reduce_plane_with(own, rider):
    col, (cols, height, _) = lax.axis_index("col"), own.shape
    others = [
        send(jnp.concatenate([pick(own, col ^ flip), rider], axis=0), 0, flip)
        for flip in range(1, cols)
    ]
    total = tree_sum([pick(own, col)] + [other[:height] for other in others])
    riders = jnp.stack([rider] + [other[height:] for other in others])
    return total, jnp.stack([pick(riders, index ^ col) for index in range(cols)])


def reduce_z(own):
    return tree_sum([own] + [send(own, flip, 0) for flip in range(2, lax.axis_size("row"), 2)])


def spread_plane(part):
    col, cols = lax.axis_index("col"), lax.axis_size("col")
    near = jnp.stack([part] + [send(part, 0, flip) for flip in range(1, cols)])
    return jnp.stack([pick(near, index ^ col) for index in range(cols)])


def spread_core(near):
    core = lax.axis_index("row") % 2
    both = jnp.stack([near, send(near, 1, 0)])
    return jnp.stack([pick(both, core), pick(both, 1 - core)])


def split(x):
    high = x.astype(BF16)
    return high, (x - high.astype(F32)).astype(BF16)


def dot(a, b):
    return jnp.dot(a, b, preferred_element_type=F32)


def dot_nt(a, b):
    return lax.dot_general(a, b, (((1,), (1,)), ((), ())), preferred_element_type=F32)


def divide(x, y):
    return x * pl.reciprocal(y, approx=True)


def prepare_left(left_ref, pair_ref):
    rank = left_ref.shape[1]
    high, low = split(left_ref[...])
    pair_ref[:, :rank] = high
    pair_ref[:, rank : 2 * rank] = low
    pair_ref[:, 2 * rank :] = high


def prepare_left_t(left_ref, pair_t_ref, sums_ref):
    rank = left_ref.shape[1]
    turned = left_ref[...].T
    high, low = split(turned)
    pair_t_ref[:rank, :] = high
    pair_t_ref[rank:, :] = low
    sums_ref[...] = jnp.broadcast_to(jnp.sum(turned, axis=1, keepdims=True), sums_ref.shape)


def chunks(extent, size):
    size = min(size, extent)
    return [pl.ds(start, size) for start in range(0, extent, size)]


def stacked(right):
    high, low = split(right)
    return jnp.concatenate([high, high, low], axis=0)


def quotients(slab_ref, pair_ref, right_stack, rows, columns=slice(None)):
    product = dot(pair_ref[rows, :], right_stack)
    return split(divide(slab_ref[rows, columns], product))


def right_update(slab_ref, pair_ref, pair_t_ref, sums_ref, right):
    rank, block = right.shape
    stack = stacked(right)
    rows = pl.ds(0, slab_ref.shape[0])
    halves = [slice(start, start + block // 2) for start in (0, block // 2)]
    parts = [quotients(slab_ref, pair_ref, stack[:, half], rows, half) for half in halves]
    numerators = []
    for high, low in parts:
        both = dot(pair_t_ref[...], high)
        numerators.append(both[:rank] + both[rank:] + dot(pair_t_ref[:rank, :], low))
    return right * jnp.concatenate(numerators, axis=1) / sums_ref[:, :1]


def left_numerator(slab_ref, pair_ref, right, total_ref, sums_ref, first):
    rank = right.shape[0]
    stack = stacked(right)
    right_high, right_low = stack[:rank], stack[2 * rank :]
    right_both = jnp.concatenate([right_high, right_low], axis=0)
    row_sums = dot_nt(jnp.ones((16, right.shape[1]), BF16), right_both)[:PAD]
    row_sums = row_sums[:, :rank] + row_sums[:, rank:]
    sums_ref[...] = jnp.where(first, row_sums, sums_ref[...] + row_sums)
    for rows in chunks(slab_ref.shape[0], ROWS):
        high, low = quotients(slab_ref, pair_ref, stack, rows)
        both = dot_nt(high, right_both)
        term = both[:, :rank] + both[:, rank:] + dot_nt(low, right_high)
        total_ref[rows, :] = jnp.where(first, term, total_ref[rows, :] + term)


def write_left(total_ref, row_sums_ref, extra_ref, out_ref):
    parts, tall, rank = out_ref.shape
    height = tall - PAD
    first = lax.broadcasted_iota(jnp.int32, (PAD, rank), 0) == 0
    stats = jnp.where(first, row_sums_ref[...], extra_ref[:1, :])
    for part in range(parts):
        out_ref[part, :height, :] = total_ref[pl.ds(part * height, height), :]
        out_ref[part, height:, :] = stats


def turn_kernel(
    slab_ref, left_ref, right_ref, extra_ref, right_out, left_out,
    pair_ref, pair_t_ref, sums_ref, total_ref, row_sums_ref,
):
    step = pl.program_id(0)

    @pl.when(step == 0)
    def _():
        prepare_left(left_ref, pair_ref)
        prepare_left_t(left_ref, pair_t_ref, sums_ref)

    right = right_update(slab_ref, pair_ref, pair_t_ref, sums_ref, right_ref[...])
    right_out[...] = right
    left_numerator(slab_ref, pair_ref, right, total_ref, row_sums_ref, step == 0)

    @pl.when(step == pl.num_programs(0) - 1)
    def _():
        write_left(total_ref, row_sums_ref, extra_ref, left_out)


def second_quotient(block, second_left, pairs):
    high, low = split(second_left)
    right_high, right_low = pairs
    product = dot(high, right_high) + (dot(low, right_high) + dot(high, right_low))
    return split(divide(block, product))


def numerator_kernel(slices, right_ref, second_left_ref, second_right_ref, numer_out):
    rank = right_ref.shape[0]
    k = right_ref.shape[1] // slices
    pairs = split(
        jnp.concatenate([second_right_ref[block] for block in range(k // rank)], axis=1)
    )
    total = 0.0
    for index in range(slices):
        second_left = second_left_ref[pl.ds(index, rank, stride=slices), :]
        high, low = second_quotient(right_ref[:, pl.ds(index * k, k)], second_left, pairs)
        left_high, left_low = split(second_left.T)
        total = total + (dot(left_high, high) + (dot(left_low, high) + dot(left_high, low)))
    for block in range(k // rank):
        numer_out[block] = total[:, block * rank : (block + 1) * rank]


def second_kernel(slices, right_ref, second_left_ref, second_right_ref, out_ref):
    rank = right_ref.shape[0]
    k = right_ref.shape[1] // slices
    second_right = jnp.concatenate(
        [second_right_ref[block] for block in range(k // rank)], axis=1
    )
    right_high, right_low = split(second_right)
    right_both = jnp.concatenate([right_high, right_low], axis=0)
    sums = dot_nt(jnp.ones((16, k), BF16), right_both)[:1]
    scale = 1.0 / (sums[:, :rank] + sums[:, rank:])
    for index in range(slices):
        rows = pl.ds(index, rank, stride=slices)
        second_left = second_left_ref[rows, :]
        high, low = second_quotient(
            right_ref[:, pl.ds(index * k, k)], second_left, (right_high, right_low)
        )
        both = dot_nt(high, right_both)
        numer = both[:, :rank] + both[:, rank:] + dot_nt(low, right_high)
        out_ref[rows, :] = second_left * numer * scale


def full(shape):
    return pl.BlockSpec(shape, lambda step: (0,) * len(shape))


def params(vmem_bytes):
    return pltpu.CompilerParams(
        dimension_semantics=("arbitrary",), vmem_limit_bytes=vmem_bytes
    )


def left_scratch(m, rank):
    return [pltpu.VMEM((m, 3 * rank), BF16)]


def right_scratch(m, rank):
    return [pltpu.VMEM((2 * rank, m), BF16), pltpu.VMEM((rank, rank), F32)]


def total_scratch(m, rank):
    return [pltpu.VMEM((m, rank), F32), pltpu.VMEM((PAD, rank), F32)]


def cost(m, rank, columns, dots):
    return pl.CostEstimate(
        flops=6 * dots * m * rank * columns, bytes_accessed=4 * m * columns, transcendentals=0
    )


def full_turn(slab, left, right, extra, block, parts, vmem_bytes):
    (m, columns), rank = slab.shape, left.shape[1]
    columns_spec = lambda height: pl.BlockSpec((height, block), lambda step: (0, step))
    tall = m // parts + PAD
    return pl.pallas_call(
        turn_kernel,
        grid=(columns // block,),
        in_specs=[columns_spec(m), full((m, rank)), columns_spec(rank), full((min(PAD, extra.shape[0]), rank))],
        out_specs=[columns_spec(rank), full((parts, tall, rank))],
        out_shape=[
            jax.ShapeDtypeStruct((rank, columns), F32),
            jax.ShapeDtypeStruct((parts, tall, rank), F32),
        ],
        scratch_shapes=left_scratch(m, rank)
        + right_scratch(m, rank)
        + total_scratch(m, rank),
        compiler_params=params(vmem_bytes),
        cost_estimate=cost(m, rank, columns, 4),
        name="turn",
    )(slab, left, right, extra)


def second_numerator(right, second_left, second_right, slices):
    return pl.pallas_call(
        functools.partial(numerator_kernel, slices),
        out_shape=jax.ShapeDtypeStruct(second_right.shape, F32),
        compiler_params=pltpu.CompilerParams(vmem_limit_bytes=VMEM_BYTES),
        cost_estimate=cost(right.shape[0], right.shape[0], right.shape[1], 2),
        name="second_numerator",
    )(right, second_left, second_right)


def second_rows_out(right, second_left, second_right, slices):
    return pl.pallas_call(
        functools.partial(second_kernel, slices),
        out_shape=jax.ShapeDtypeStruct(second_left.shape, F32),
        compiler_params=pltpu.CompilerParams(vmem_limit_bytes=VMEM_BYTES),
        cost_estimate=cost(right.shape[0], right.shape[0], right.shape[1], 2),
        name="second_rows",
    )(right, second_left, second_right)


def prepare_kernel(slices, place_ref, second_left_ref, out_ref, sums_out):
    devices, tall, rank = out_ref.shape
    second_left = second_left_ref[...]
    sums_out[...] = jnp.sum(second_left, axis=0, keepdims=True)
    for index in range(tall // slices):
        for device in range(devices):
            start = (index * devices + device) * slices
            out_ref[device, index * slices : (index + 1) * slices, :] = second_left[
                start : start + slices
            ]


def prepare(place, second_left, devices, slices, second_rows):
    rank = second_left.shape[1]
    shapes = [(devices, second_rows // devices, rank), (1, rank)]
    return pl.pallas_call(
        functools.partial(prepare_kernel, slices),
        grid_spec=pltpu.PrefetchScalarGridSpec(
            num_scalar_prefetch=1,
            grid=(1,),
            in_specs=[pl.BlockSpec((second_rows, rank), lambda step, place: (place[0], 0))],
            out_specs=[
                pl.BlockSpec(shapes[0], lambda step, place: (0, 0, 0)),
                pl.BlockSpec(shapes[1], lambda step, place: (0, 0)),
            ],
        ),
        out_shape=[jax.ShapeDtypeStruct(shape, F32) for shape in shapes],
        compiler_params=params(PREP_KIB * 1024),
        cost_estimate=pl.CostEstimate(
            flops=second_rows * rank, bytes_accessed=8 * second_rows * rank, transcendentals=0
        ),
        name="prepare",
    )(place, second_left)


def body(tensor_slab, left_init, right_init, second_left_init, second_right_init):
    row_devices = lax.axis_size("row")
    col_devices = lax.axis_size("col")
    devices = row_devices * col_devices
    own_part = (lax.axis_index("row") % 2) * col_devices + lax.axis_index("col")
    parts = 2 * col_devices
    m, rank = left_init.shape
    k = second_right_init.shape[1] * col_devices
    slices = right_init.shape[1] // k
    per_owner = rank // devices
    rows_own = m // parts

    def own_rows(left):
        return lax.dynamic_slice_in_dim(left, own_part * rows_own, rows_own, 0)

    def own_left_rows(own, total):
        return own * total[:rows_own] / total[rows_own][None, :]

    right, summed = full_turn(
        tensor_slab, left_init, right_init, left_init, k, parts, T1_MIB * MIB
    )
    second_left = after(second_left_init, summed)
    summed = summed.reshape(2, col_devices, rows_own + PAD, rank)
    core_sum = reduce_core(summed)
    own_init = after(own_rows(left_init), core_sum)

    half = rank // 2
    groups = rank // second_right_init.shape[1]
    rider = lax.dynamic_slice_in_dim(second_right_init, lax.axis_index("row") % 2 * half, half, 0)
    rider = jnp.concatenate(jnp.split(rider, groups, axis=0), axis=1)
    plane, riders = reduce_plane_with(core_sum, rider)
    total = reduce_z(plane)
    near = spread_plane(own_left_rows(own_init, total))
    both = spread_core(jnp.concatenate([near, riders], axis=1))
    left = both[:, :, :rows_own].reshape(m, rank)
    whole = both[:, :, rows_own:].reshape(2, col_devices, half // groups, groups, -1)
    whole = whole.transpose(0, 3, 2, 1, 4).reshape(rank, k // rank, rank).transpose(1, 0, 2)

    second_rows = second_left_init.shape[0] // col_devices
    place = lax.axis_index("col").astype(jnp.int32)[None]
    second_left, col_part = prepare(place, second_left, devices, slices, second_rows)
    arrived = exchange(after(second_left, left))
    right, summed = full_turn(tensor_slab, left, right, col_part, k, parts, VMEM_BYTES)
    arrived = after(arrived, summed)
    second_left = arrived.reshape(rank * slices, rank)
    numerator = second_numerator(right, second_left, whole, slices)

    rows_part = k // parts
    summed = summed.reshape(2, col_devices, rows_own + PAD, rank)
    numerator = numerator.reshape(2, col_devices, rows_part, rank)
    total = reduce_z(reduce_plane(reduce_core(jnp.concatenate([summed, numerator], axis=2))))
    init_over = (whole / total[rows_own + 1][None, :, None]).reshape(k, rank)
    init_over = lax.dynamic_slice_in_dim(init_over, own_part * rows_part, rows_part, 0)
    second_part = init_over * total[rows_own + PAD :]
    both = spread_core(
        spread_plane(jnp.concatenate([own_left_rows(own_rows(left), total), second_part], axis=0))
    )
    left_out = both[:, :, :rows_own].reshape(m, rank)
    second_right = both[:, :, rows_own:].reshape(k // rank, rank, rank)
    rows_out = second_rows_out(right, second_left, second_right, slices)
    returned = exchange(rows_out.reshape(devices, per_owner * slices, rank))
    returned = returned.reshape(devices, per_owner, slices, rank).transpose(1, 0, 2, 3)
    return (left_out, returned.reshape(second_rows, rank))


def solution(mesh):
    placed = (P(None, AXES), P(), P(None, AXES), P("row", None), P(None, "col"))
    return jax.shard_map(
        body, mesh=mesh, in_specs=placed, out_specs=(P(), P(AXES, None)), check_vma=False
    )
```

```python
import functools

import jax
import jax.numpy as jnp
from jax import lax
from jax.experimental import pallas as pl
from jax.experimental.pallas import tpu as pltpu
from jax.sharding import PartitionSpec as P

AXES = ("row", "col")
F32, BF16 = jnp.float32, jnp.bfloat16
PAD = 8
ROWS = 1024
MIB = 1024 * 1024
T1_MIB = 52
PREP_KIB = 54528
VMEM_BYTES = 51 * MIB


def exchange(parts):
    return lax.all_to_all(parts, AXES, split_axis=0, concat_axis=0, tiled=True)


def send(values, row_flip, col_flip):
    rows, cols = lax.axis_size("row"), lax.axis_size("col")
    pairs = [
        (r * cols + c, (r ^ row_flip) * cols + (c ^ col_flip))
        for r in range(rows)
        for c in range(cols)
    ]
    return lax.ppermute(values, AXES, pairs)


def pick(values, index):
    return lax.dynamic_index_in_dim(values, index, 0, keepdims=False)


def tree_sum(terms):
    while len(terms) > 1:
        terms = [a + b for a, b in zip(terms[::2], terms[1::2])]
    return terms[0]


def after(values, *events):
    return lax.optimization_barrier((values,) + events)[0]


def reduce_core(parts):
    core = lax.axis_index("row") % 2
    return pick(parts, core) + send(pick(parts, 1 - core), 1, 0)


def reduce_plane(own):
    col = lax.axis_index("col")
    others = [send(pick(own, col ^ flip), 0, flip) for flip in range(1, own.shape[0])]
    return tree_sum([pick(own, col)] + others)


def reduce_plane_with(own, rider):
    col, (cols, height, _) = lax.axis_index("col"), own.shape
    others = [
        send(jnp.concatenate([pick(own, col ^ flip), rider], axis=0), 0, flip)
        for flip in range(1, cols)
    ]
    total = tree_sum([pick(own, col)] + [other[:height] for other in others])
    riders = jnp.stack([rider] + [other[height:] for other in others])
    return total, jnp.stack([pick(riders, index ^ col) for index in range(cols)])


def reduce_z(own):
    return tree_sum([own] + [send(own, flip, 0) for flip in range(2, lax.axis_size("row"), 2)])


def spread_plane(part):
    col, cols = lax.axis_index("col"), lax.axis_size("col")
    near = jnp.stack([part] + [send(part, 0, flip) for flip in range(1, cols)])
    return jnp.stack([pick(near, index ^ col) for index in range(cols)])


def spread_core(near):
    core = lax.axis_index("row") % 2
    both = jnp.stack([near, send(near, 1, 0)])
    return jnp.stack([pick(both, core), pick(both, 1 - core)])


def split(x):
    high = x.astype(BF16)
    return high, (x - high.astype(F32)).astype(BF16)


def dot(a, b):
    return jnp.dot(a, b, preferred_element_type=F32)


def divide(x, y):
    return x * pl.reciprocal(y, approx=True)


def prepare_left(left_ref, pair_ref):
    rank = left_ref.shape[1]
    high, low = split(left_ref[...])
    pair_ref[:, :rank] = high
    pair_ref[:, rank : 2 * rank] = low
    pair_ref[:, 2 * rank :] = high


def prepare_left_t(left_ref, pair_t_ref, sums_ref):
    rank = left_ref.shape[1]
    turned = left_ref[...].T
    high, low = split(turned)
    pair_t_ref[:rank, :] = high
    pair_t_ref[rank:, :] = low
    sums_ref[...] = jnp.broadcast_to(jnp.sum(turned, axis=1, keepdims=True), sums_ref.shape)


def chunks(extent, size):
    size = min(size, extent)
    return [pl.ds(start, size) for start in range(0, extent, size)]


def stacked(right):
    high, low = split(right)
    return jnp.concatenate([high, high, low], axis=0)


def quotients(slab_ref, pair_ref, right_stack, rows, columns=slice(None)):
    product = dot(pair_ref[rows, :], right_stack)
    return split(divide(slab_ref[rows, columns], product))


def right_update(slab_ref, pair_ref, pair_t_ref, sums_ref, right):
    rank, block = right.shape
    stack = stacked(right)
    rows = pl.ds(0, slab_ref.shape[0])
    halves = [slice(start, start + block // 2) for start in (0, block // 2)]
    parts = [quotients(slab_ref, pair_ref, stack[:, half], rows, half) for half in halves]
    numerators = []
    for high, low in parts:
        both = dot(pair_t_ref[...], high)
        numerators.append(both[:rank] + both[rank:] + dot(pair_t_ref[:rank, :], low))
    return right * jnp.concatenate(numerators, axis=1) / sums_ref[:, :1]


def left_numerator(slab_ref, pair_ref, right, total_ref, sums_ref, first):
    rank = right.shape[0]
    stack = stacked(right)
    right_high, right_low = split(right.T)
    right_both = jnp.concatenate([right_high, right_low], axis=1)
    row_sums = dot(jnp.ones((16, right.shape[1]), BF16), right_both)[:PAD]
    row_sums = row_sums[:, :rank] + row_sums[:, rank:]
    sums_ref[...] = jnp.where(first, row_sums, sums_ref[...] + row_sums)
    for rows in chunks(slab_ref.shape[0], ROWS):
        high, low = quotients(slab_ref, pair_ref, stack, rows)
        both = dot(high, right_both)
        term = both[:, :rank] + both[:, rank:] + dot(low, right_high)
        total_ref[rows, :] = jnp.where(first, term, total_ref[rows, :] + term)


def write_left(total_ref, row_sums_ref, extra_ref, out_ref):
    parts, tall, rank = out_ref.shape
    height = tall - PAD
    first = lax.broadcasted_iota(jnp.int32, (PAD, rank), 0) == 0
    stats = jnp.where(first, row_sums_ref[...], extra_ref[:1, :])
    for part in range(parts):
        out_ref[part, :height, :] = total_ref[pl.ds(part * height, height), :]
        out_ref[part, height:, :] = stats


def turn_kernel(
    slab_ref, left_ref, right_ref, extra_ref, right_out, left_out,
    pair_ref, pair_t_ref, sums_ref, total_ref, row_sums_ref,
):
    step = pl.program_id(0)

    @pl.when(step == 0)
    def _():
        prepare_left(left_ref, pair_ref)
        prepare_left_t(left_ref, pair_t_ref, sums_ref)

    right = right_update(slab_ref, pair_ref, pair_t_ref, sums_ref, right_ref[...])
    right_out[...] = right
    left_numerator(slab_ref, pair_ref, right, total_ref, row_sums_ref, step == 0)

    @pl.when(step == pl.num_programs(0) - 1)
    def _():
        write_left(total_ref, row_sums_ref, extra_ref, left_out)


def second_parts(slices, right_ref, second_left_ref, second_right_ref):
    rank = right_ref.shape[0]
    k = right_ref.shape[1] // slices
    second_left = jnp.concatenate(
        [second_left_ref[pl.ds(index, rank, stride=slices), :] for index in range(slices)], axis=0
    )
    second_right = jnp.concatenate(
        [second_right_ref[block] for block in range(k // rank)], axis=1
    )
    high, low = split(second_left)
    product = dot(jnp.concatenate([high, low, high], axis=1), stacked(second_right))
    block = jnp.concatenate(
        [right_ref[:, index * k : (index + 1) * k] for index in range(slices)], axis=0
    )
    return second_left, second_right, split(divide(block, product))


def numerator_kernel(slices, right_ref, second_left_ref, second_right_ref, numer_out):
    second_left, _, (high, low) = second_parts(
        slices, right_ref, second_left_ref, second_right_ref
    )
    rank = second_left.shape[1]
    left_both = jnp.concatenate(split(second_left.T), axis=0)
    both = dot(left_both, high)
    total = both[:rank] + both[rank:] + dot(left_both[:rank], low)
    for block in range(total.shape[1] // rank):
        numer_out[block] = total[:, block * rank : (block + 1) * rank]


def second_kernel(slices, right_ref, second_left_ref, second_right_ref, out_ref):
    second_left, second_right, (high, low) = second_parts(
        slices, right_ref, second_left_ref, second_right_ref
    )
    rank = second_left.shape[1]
    right_high, right_low = split(second_right.T)
    right_both = jnp.concatenate([right_high, right_low], axis=1)
    sums = dot(jnp.ones((16, right_both.shape[0]), BF16), right_both)[:1]
    both = dot(high, right_both)
    numer = both[:, :rank] + both[:, rank:] + dot(low, right_high)
    rows = second_left * numer * (1.0 / (sums[:, :rank] + sums[:, rank:]))
    for index in range(slices):
        out_ref[pl.ds(index, rank, stride=slices), :] = rows[index * rank : (index + 1) * rank]


def full(shape):
    return pl.BlockSpec(shape, lambda step: (0,) * len(shape))


def params(vmem_bytes):
    return pltpu.CompilerParams(
        dimension_semantics=("arbitrary",), vmem_limit_bytes=vmem_bytes
    )


def left_scratch(m, rank):
    return [pltpu.VMEM((m, 3 * rank), BF16)]


def right_scratch(m, rank):
    return [pltpu.VMEM((2 * rank, m), BF16), pltpu.VMEM((rank, rank), F32)]


def total_scratch(m, rank):
    return [pltpu.VMEM((m, rank), F32), pltpu.VMEM((PAD, rank), F32)]


def cost(m, rank, columns, dots):
    return pl.CostEstimate(
        flops=6 * dots * m * rank * columns, bytes_accessed=4 * m * columns, transcendentals=0
    )


def full_turn(slab, left, right, extra, block, parts, vmem_bytes):
    (m, columns), rank = slab.shape, left.shape[1]
    columns_spec = lambda height: pl.BlockSpec((height, block), lambda step: (0, step))
    tall = m // parts + PAD
    return pl.pallas_call(
        turn_kernel,
        grid=(columns // block,),
        in_specs=[columns_spec(m), full((m, rank)), columns_spec(rank), full((min(PAD, extra.shape[0]), rank))],
        out_specs=[columns_spec(rank), full((parts, tall, rank))],
        out_shape=[
            jax.ShapeDtypeStruct((rank, columns), F32),
            jax.ShapeDtypeStruct((parts, tall, rank), F32),
        ],
        scratch_shapes=left_scratch(m, rank)
        + right_scratch(m, rank)
        + total_scratch(m, rank),
        compiler_params=params(vmem_bytes),
        cost_estimate=cost(m, rank, columns, 4),
        name="turn",
    )(slab, left, right, extra)


def second_numerator(right, second_left, second_right, slices):
    return pl.pallas_call(
        functools.partial(numerator_kernel, slices),
        out_shape=jax.ShapeDtypeStruct(second_right.shape, F32),
        compiler_params=pltpu.CompilerParams(vmem_limit_bytes=VMEM_BYTES),
        cost_estimate=cost(right.shape[0], right.shape[0], right.shape[1], 2),
        name="second_numerator",
    )(right, second_left, second_right)


def second_rows_out(right, second_left, second_right, slices):
    return pl.pallas_call(
        functools.partial(second_kernel, slices),
        out_shape=jax.ShapeDtypeStruct(second_left.shape, F32),
        compiler_params=pltpu.CompilerParams(vmem_limit_bytes=VMEM_BYTES),
        cost_estimate=cost(right.shape[0], right.shape[0], right.shape[1], 2),
        name="second_rows",
    )(right, second_left, second_right)


def prepare_kernel(slices, place_ref, second_left_ref, out_ref, sums_out):
    devices, tall, rank = out_ref.shape
    second_left = second_left_ref[...]
    sums_out[...] = jnp.sum(second_left, axis=0, keepdims=True)
    for index in range(tall // slices):
        for device in range(devices):
            start = (index * devices + device) * slices
            out_ref[device, index * slices : (index + 1) * slices, :] = second_left[
                start : start + slices
            ]


def prepare(place, second_left, devices, slices, second_rows):
    rank = second_left.shape[1]
    shapes = [(devices, second_rows // devices, rank), (1, rank)]
    return pl.pallas_call(
        functools.partial(prepare_kernel, slices),
        grid_spec=pltpu.PrefetchScalarGridSpec(
            num_scalar_prefetch=1,
            grid=(1,),
            in_specs=[pl.BlockSpec((second_rows, rank), lambda step, place: (place[0], 0))],
            out_specs=[
                pl.BlockSpec(shapes[0], lambda step, place: (0, 0, 0)),
                pl.BlockSpec(shapes[1], lambda step, place: (0, 0)),
            ],
        ),
        out_shape=[jax.ShapeDtypeStruct(shape, F32) for shape in shapes],
        compiler_params=params(PREP_KIB * 1024),
        cost_estimate=pl.CostEstimate(
            flops=second_rows * rank, bytes_accessed=8 * second_rows * rank, transcendentals=0
        ),
        name="prepare",
    )(place, second_left)


def body(tensor_slab, left_init, right_init, second_left_init, second_right_init):
    row_devices = lax.axis_size("row")
    col_devices = lax.axis_size("col")
    devices = row_devices * col_devices
    own_part = (lax.axis_index("row") % 2) * col_devices + lax.axis_index("col")
    parts = 2 * col_devices
    m, rank = left_init.shape
    k = second_right_init.shape[1] * col_devices
    slices = right_init.shape[1] // k
    per_owner = rank // devices
    rows_own = m // parts

    def own_rows(left):
        return lax.dynamic_slice_in_dim(left, own_part * rows_own, rows_own, 0)

    def own_left_rows(own, total):
        return own * total[:rows_own] / total[rows_own][None, :]

    right, summed = full_turn(
        tensor_slab, left_init, right_init, left_init, k, parts, T1_MIB * MIB
    )
    second_left = after(second_left_init, summed)
    summed = summed.reshape(2, col_devices, rows_own + PAD, rank)
    core_sum = reduce_core(summed)
    own_init = after(own_rows(left_init), core_sum)

    half = rank // 2
    groups = rank // second_right_init.shape[1]
    rider = lax.dynamic_slice_in_dim(second_right_init, lax.axis_index("row") % 2 * half, half, 0)
    rider = jnp.concatenate(jnp.split(rider, groups, axis=0), axis=1)
    plane, riders = reduce_plane_with(core_sum, rider)
    total = reduce_z(plane)
    near = spread_plane(own_left_rows(own_init, total))
    both = spread_core(jnp.concatenate([near, riders], axis=1))
    left = both[:, :, :rows_own].reshape(m, rank)
    whole = both[:, :, rows_own:].reshape(2, col_devices, half // groups, groups, -1)
    whole = whole.transpose(0, 3, 2, 1, 4).reshape(rank, k // rank, rank).transpose(1, 0, 2)

    second_rows = second_left_init.shape[0] // col_devices
    place = lax.axis_index("col").astype(jnp.int32)[None]
    second_left, col_part = prepare(place, second_left, devices, slices, second_rows)
    arrived = exchange(after(second_left, left))
    right, summed = full_turn(tensor_slab, left, right, col_part, k, parts, VMEM_BYTES)
    arrived = after(arrived, summed)
    second_left = arrived.reshape(rank * slices, rank)
    numerator = second_numerator(right, second_left, whole, slices)

    rows_part = k // parts
    summed = summed.reshape(2, col_devices, rows_own + PAD, rank)
    numerator = numerator.reshape(2, col_devices, rows_part, rank)
    total = reduce_z(reduce_plane(reduce_core(jnp.concatenate([summed, numerator], axis=2))))
    init_over = (whole / total[rows_own + 1][None, :, None]).reshape(k, rank)
    init_over = lax.dynamic_slice_in_dim(init_over, own_part * rows_part, rows_part, 0)
    second_part = init_over * total[rows_own + PAD :]
    both = spread_core(
        spread_plane(jnp.concatenate([own_left_rows(own_rows(left), total), second_part], axis=0))
    )
    left_out = both[:, :, :rows_own].reshape(m, rank)
    second_right = both[:, :, rows_own:].reshape(k // rank, rank, rank)
    rows_out = second_rows_out(right, second_left, second_right, slices)
    returned = exchange(rows_out.reshape(devices, per_owner * slices, rank))
    returned = returned.reshape(devices, per_owner, slices, rank).transpose(1, 0, 2, 3)
    return (left_out, returned.reshape(second_rows, rank))


def solution(mesh):
    placed = (P(None, AXES), P(), P(None, AXES), P("row", None), P(None, "col"))
    return jax.shard_map(
        body, mesh=mesh, in_specs=placed, out_specs=(P(), P(AXES, None)), check_vma=False
    )
```

```python
import functools

import jax
import jax.numpy as jnp
from jax import lax
from jax.experimental import pallas as pl
from jax.experimental.pallas import tpu as pltpu
from jax.sharding import PartitionSpec as P

AXES = ("row", "col")
F32, BF16 = jnp.float32, jnp.bfloat16
PAD = 8
MIB = 1024 * 1024
T1_MIB = 52
PREP_KIB = 54528
VMEM_BYTES = 51 * MIB


def exchange(parts):
    return lax.all_to_all(parts, AXES, split_axis=0, concat_axis=0, tiled=True)


def send(values, row_flip, col_flip):
    rows, cols = lax.axis_size("row"), lax.axis_size("col")
    pairs = [
        (r * cols + c, (r ^ row_flip) * cols + (c ^ col_flip))
        for r in range(rows)
        for c in range(cols)
    ]
    return lax.ppermute(values, AXES, pairs)


def pick(values, index):
    return lax.dynamic_index_in_dim(values, index, 0, keepdims=False)


def tree_sum(terms):
    while len(terms) > 1:
        terms = [a + b for a, b in zip(terms[::2], terms[1::2])]
    return terms[0]


def after(values, *events):
    return lax.optimization_barrier((values,) + events)[0]


def reduce_core(parts):
    core = lax.axis_index("row") % 2
    return pick(parts, core) + send(pick(parts, 1 - core), 1, 0)


def reduce_plane(own):
    col = lax.axis_index("col")
    others = [send(pick(own, col ^ flip), 0, flip) for flip in range(1, own.shape[0])]
    return tree_sum([pick(own, col)] + others)


def reduce_plane_with(own, rider):
    col, (cols, height, _) = lax.axis_index("col"), own.shape
    others = [
        send(jnp.concatenate([pick(own, col ^ flip), rider], axis=0), 0, flip)
        for flip in range(1, cols)
    ]
    total = tree_sum([pick(own, col)] + [other[:height] for other in others])
    riders = jnp.stack([rider] + [other[height:] for other in others])
    return total, jnp.stack([pick(riders, index ^ col) for index in range(cols)])


def reduce_z(own):
    return tree_sum([own] + [send(own, flip, 0) for flip in range(2, lax.axis_size("row"), 2)])


def spread_plane(part):
    col, cols = lax.axis_index("col"), lax.axis_size("col")
    near = jnp.stack([part] + [send(part, 0, flip) for flip in range(1, cols)])
    return jnp.stack([pick(near, index ^ col) for index in range(cols)])


def spread_core(near):
    core = lax.axis_index("row") % 2
    both = jnp.stack([near, send(near, 1, 0)])
    return jnp.stack([pick(both, core), pick(both, 1 - core)])


def split(x):
    high = x.astype(BF16)
    return high, (x - high.astype(F32)).astype(BF16)


def dot(a, b):
    return jnp.dot(a, b, preferred_element_type=F32)


def divide(x, y):
    return x * pl.reciprocal(y, approx=True)


def prepare_left(left_ref, pair_ref):
    rank = left_ref.shape[1]
    high, low = split(left_ref[...])
    pair_ref[:, :rank] = high
    pair_ref[:, rank : 2 * rank] = low
    pair_ref[:, 2 * rank :] = high


def prepare_left_t(left_ref, pair_t_ref, sums_ref):
    rank = left_ref.shape[1]
    turned = left_ref[...].T
    high, low = split(turned)
    pair_t_ref[:rank, :] = high
    pair_t_ref[rank:, :] = low
    sums_ref[...] = jnp.broadcast_to(jnp.sum(turned, axis=1, keepdims=True), sums_ref.shape)


def stacked(right):
    high, low = split(right)
    return jnp.concatenate([high, high, low], axis=0)


def quotients(slab_ref, pair_ref, right_stack, rows):
    product = dot(pair_ref[rows, :], right_stack)
    return split(divide(slab_ref[rows, :], product))


def right_update(slab_ref, pair_ref, pair_t_ref, sums_ref, right):
    rank = right.shape[0]
    high, low = quotients(slab_ref, pair_ref, stacked(right), pl.ds(0, slab_ref.shape[0]))
    both = dot(pair_t_ref[...], high)
    numerator = both[:rank] + both[rank:] + dot(pair_t_ref[:rank, :], low)
    return right * numerator / sums_ref[:, :1]


def left_numerator(slab_ref, pair_ref, right):
    rank = right.shape[0]
    right_high, right_low = split(right.T)
    right_both = jnp.concatenate([right_high, right_low], axis=1)
    row_sums = dot(jnp.ones((16, right.shape[1]), BF16), right_both)[:PAD]
    high, low = quotients(slab_ref, pair_ref, stacked(right), pl.ds(0, slab_ref.shape[0]))
    both = dot(high, right_both)
    term = both[:, :rank] + both[:, rank:] + dot(low, right_high)
    return term, row_sums[:, :rank] + row_sums[:, rank:]


def write_left(total, row_sums, extra_ref, out_ref):
    parts, tall, rank = out_ref.shape
    height = tall - PAD
    first = lax.broadcasted_iota(jnp.int32, (PAD, rank), 0) == 0
    stats = jnp.where(first, row_sums, extra_ref[:1, :])
    for part in range(parts):
        out_ref[part, :height, :] = total[part * height : (part + 1) * height]
        out_ref[part, height:, :] = stats


def turn_kernel(
    block, slab_hbm, left_ref, right_ref, extra_ref, right_out, left_out,
    slab_ref, pair_ref, pair_t_ref, sums_ref, arrivals,
):
    blocks = [pl.ds(start, block) for start in range(0, slab_ref.shape[1], block)]
    copies = [
        pltpu.make_async_copy(
            slab_hbm.at[:, columns], slab_ref.at[:, columns], arrivals.at[index]
        )
        for index, columns in enumerate(blocks)
    ]
    for copy in copies:
        copy.start()
    prepare_left(left_ref, pair_ref)
    prepare_left_t(left_ref, pair_t_ref, sums_ref)
    total = row_sums = 0.0
    for copy, columns in zip(copies, blocks):
        copy.wait()
        part_ref = slab_ref.at[:, columns]
        right = right_update(part_ref, pair_ref, pair_t_ref, sums_ref, right_ref[:, columns])
        right_out[:, columns] = right
        term, sums = left_numerator(part_ref, pair_ref, right)
        total, row_sums = total + term, row_sums + sums
    write_left(total, row_sums, extra_ref, left_out)


def second_parts(slices, right_ref, second_left_ref, second_right_ref):
    rank = right_ref.shape[0]
    k = right_ref.shape[1] // slices
    second_left = jnp.concatenate(
        [second_left_ref[pl.ds(index, rank, stride=slices), :] for index in range(slices)], axis=0
    )
    second_right = jnp.concatenate(
        [second_right_ref[block] for block in range(k // rank)], axis=1
    )
    high, low = split(second_left)
    product = dot(jnp.concatenate([high, low, high], axis=1), stacked(second_right))
    block = jnp.concatenate(
        [right_ref[:, index * k : (index + 1) * k] for index in range(slices)], axis=0
    )
    return second_left, second_right, split(divide(block, product))


def numerator_kernel(slices, right_ref, second_left_ref, second_right_ref, numer_out):
    second_left, _, (high, low) = second_parts(
        slices, right_ref, second_left_ref, second_right_ref
    )
    rank = second_left.shape[1]
    left_both = jnp.concatenate(split(second_left.T), axis=0)
    both = dot(left_both, high)
    total = both[:rank] + both[rank:] + dot(left_both[:rank], low)
    for block in range(total.shape[1] // rank):
        numer_out[block] = total[:, block * rank : (block + 1) * rank]


def second_kernel(slices, right_ref, second_left_ref, second_right_ref, out_ref):
    second_left, second_right, (high, low) = second_parts(
        slices, right_ref, second_left_ref, second_right_ref
    )
    rank = second_left.shape[1]
    right_high, right_low = split(second_right.T)
    right_both = jnp.concatenate([right_high, right_low], axis=1)
    sums = dot(jnp.ones((16, right_both.shape[0]), BF16), right_both)[:1]
    both = dot(high, right_both)
    numer = both[:, :rank] + both[:, rank:] + dot(low, right_high)
    rows = second_left * numer * (1.0 / (sums[:, :rank] + sums[:, rank:]))
    for index in range(slices):
        out_ref[pl.ds(index, rank, stride=slices), :] = rows[index * rank : (index + 1) * rank]


def full(shape):
    return pl.BlockSpec(shape, lambda step: (0,) * len(shape))


def params(vmem_bytes):
    return pltpu.CompilerParams(
        dimension_semantics=("arbitrary",), vmem_limit_bytes=vmem_bytes
    )


def left_scratch(m, rank):
    return [pltpu.VMEM((m, 3 * rank), BF16)]


def right_scratch(m, rank):
    return [pltpu.VMEM((2 * rank, m), BF16), pltpu.VMEM((rank, rank), F32)]


def cost(m, rank, columns, dots):
    return pl.CostEstimate(
        flops=6 * dots * m * rank * columns, bytes_accessed=4 * m * columns, transcendentals=0
    )


def full_turn(slab, left, right, extra, block, parts, vmem_bytes):
    (m, columns), rank = slab.shape, left.shape[1]
    tall = m // parts + PAD
    return pl.pallas_call(
        functools.partial(turn_kernel, block),
        grid=(1,),
        in_specs=[
            pl.BlockSpec(memory_space=pl.ANY),
            full((m, rank)),
            full((rank, columns)),
            full((min(PAD, extra.shape[0]), rank)),
        ],
        out_specs=[full((rank, columns)), full((parts, tall, rank))],
        out_shape=[
            jax.ShapeDtypeStruct((rank, columns), F32),
            jax.ShapeDtypeStruct((parts, tall, rank), F32),
        ],
        scratch_shapes=[pltpu.VMEM((m, columns), F32)]
        + left_scratch(m, rank)
        + right_scratch(m, rank)
        + [pltpu.SemaphoreType.DMA((columns // block,))],
        compiler_params=params(vmem_bytes),
        cost_estimate=cost(m, rank, columns, 4),
        name="turn",
    )(slab, left, right, extra)


def second_numerator(right, second_left, second_right, slices):
    return pl.pallas_call(
        functools.partial(numerator_kernel, slices),
        out_shape=jax.ShapeDtypeStruct(second_right.shape, F32),
        compiler_params=pltpu.CompilerParams(vmem_limit_bytes=VMEM_BYTES),
        cost_estimate=cost(right.shape[0], right.shape[0], right.shape[1], 2),
        name="second_numerator",
    )(right, second_left, second_right)


def second_rows_out(right, second_left, second_right, slices):
    return pl.pallas_call(
        functools.partial(second_kernel, slices),
        out_shape=jax.ShapeDtypeStruct(second_left.shape, F32),
        compiler_params=pltpu.CompilerParams(vmem_limit_bytes=VMEM_BYTES),
        cost_estimate=cost(right.shape[0], right.shape[0], right.shape[1], 2),
        name="second_rows",
    )(right, second_left, second_right)


def prepare_kernel(slices, place_ref, second_left_ref, out_ref, sums_out):
    devices, tall, rank = out_ref.shape
    second_left = second_left_ref[...]
    sums_out[...] = jnp.sum(second_left, axis=0, keepdims=True)
    for index in range(tall // slices):
        for device in range(devices):
            start = (index * devices + device) * slices
            out_ref[device, index * slices : (index + 1) * slices, :] = second_left[
                start : start + slices
            ]


def prepare(place, second_left, devices, slices, second_rows):
    rank = second_left.shape[1]
    shapes = [(devices, second_rows // devices, rank), (1, rank)]
    return pl.pallas_call(
        functools.partial(prepare_kernel, slices),
        grid_spec=pltpu.PrefetchScalarGridSpec(
            num_scalar_prefetch=1,
            grid=(1,),
            in_specs=[pl.BlockSpec((second_rows, rank), lambda step, place: (place[0], 0))],
            out_specs=[
                pl.BlockSpec(shapes[0], lambda step, place: (0, 0, 0)),
                pl.BlockSpec(shapes[1], lambda step, place: (0, 0)),
            ],
        ),
        out_shape=[jax.ShapeDtypeStruct(shape, F32) for shape in shapes],
        compiler_params=params(PREP_KIB * 1024),
        cost_estimate=pl.CostEstimate(
            flops=second_rows * rank, bytes_accessed=8 * second_rows * rank, transcendentals=0
        ),
        name="prepare",
    )(place, second_left)


def body(tensor_slab, left_init, right_init, second_left_init, second_right_init):
    row_devices = lax.axis_size("row")
    col_devices = lax.axis_size("col")
    devices = row_devices * col_devices
    own_part = (lax.axis_index("row") % 2) * col_devices + lax.axis_index("col")
    parts = 2 * col_devices
    m, rank = left_init.shape
    k = second_right_init.shape[1] * col_devices
    slices = right_init.shape[1] // k
    per_owner = rank // devices
    rows_own = m // parts

    def own_rows(left):
        return lax.dynamic_slice_in_dim(left, own_part * rows_own, rows_own, 0)

    def own_left_rows(own, total):
        return own * total[:rows_own] / total[rows_own][None, :]

    right, summed = full_turn(
        tensor_slab, left_init, right_init, left_init, k, parts, T1_MIB * MIB
    )
    second_left = after(second_left_init, summed)
    summed = summed.reshape(2, col_devices, rows_own + PAD, rank)
    core_sum = reduce_core(summed)
    own_init = after(own_rows(left_init), core_sum)

    half = rank // 2
    groups = rank // second_right_init.shape[1]
    rider = lax.dynamic_slice_in_dim(second_right_init, lax.axis_index("row") % 2 * half, half, 0)
    rider = jnp.concatenate(jnp.split(rider, groups, axis=0), axis=1)
    plane, riders = reduce_plane_with(core_sum, rider)
    total = reduce_z(plane)
    near = spread_plane(own_left_rows(own_init, total))
    both = spread_core(jnp.concatenate([near, riders], axis=1))
    left = both[:, :, :rows_own].reshape(m, rank)
    whole = both[:, :, rows_own:].reshape(2, col_devices, half // groups, groups, -1)
    whole = whole.transpose(0, 3, 2, 1, 4).reshape(rank, k // rank, rank).transpose(1, 0, 2)

    second_rows = second_left_init.shape[0] // col_devices
    place = lax.axis_index("col").astype(jnp.int32)[None]
    second_left, col_part = prepare(place, second_left, devices, slices, second_rows)
    arrived = exchange(after(second_left, left))
    right, summed = full_turn(tensor_slab, left, right, col_part, k, parts, VMEM_BYTES)
    arrived = after(arrived, summed)
    second_left = arrived.reshape(rank * slices, rank)
    numerator = second_numerator(right, second_left, whole, slices)

    rows_part = k // parts
    summed = summed.reshape(2, col_devices, rows_own + PAD, rank)
    numerator = numerator.reshape(2, col_devices, rows_part, rank)
    total = reduce_z(reduce_plane(reduce_core(jnp.concatenate([summed, numerator], axis=2))))
    init_over = (whole / total[rows_own + 1][None, :, None]).reshape(k, rank)
    init_over = lax.dynamic_slice_in_dim(init_over, own_part * rows_part, rows_part, 0)
    second_part = init_over * total[rows_own + PAD :]
    both = spread_core(
        spread_plane(jnp.concatenate([own_left_rows(own_rows(left), total), second_part], axis=0))
    )
    left_out = both[:, :, :rows_own].reshape(m, rank)
    second_right = both[:, :, rows_own:].reshape(k // rank, rank, rank)
    rows_out = second_rows_out(right, second_left, second_right, slices)
    returned = exchange(rows_out.reshape(devices, per_owner * slices, rank))
    returned = returned.reshape(devices, per_owner, slices, rank).transpose(1, 0, 2, 3)
    return (left_out, returned.reshape(second_rows, rank))


def solution(mesh):
    placed = (P(None, AXES), P(), P(None, AXES), P("row", None), P(None, "col"))
    return jax.shard_map(
        body, mesh=mesh, in_specs=placed, out_specs=(P(), P(AXES, None)), check_vma=False
    )
```

```python
import functools

import jax
import jax.numpy as jnp
from jax import lax
from jax.experimental import pallas as pl
from jax.experimental.pallas import tpu as pltpu
from jax.sharding import PartitionSpec as P

AXES = ("row", "col")
F32, BF16 = jnp.float32, jnp.bfloat16
PAD = 8
ROWS = 1024
MIB = 1024 * 1024
T1_MIB = 52
PREP_KIB = 54528
VMEM_BYTES = 51 * MIB


def exchange(parts):
    return lax.all_to_all(parts, AXES, split_axis=0, concat_axis=0, tiled=True)


def send(values, row_flip, col_flip):
    rows, cols = lax.axis_size("row"), lax.axis_size("col")
    pairs = [
        (r * cols + c, (r ^ row_flip) * cols + (c ^ col_flip))
        for r in range(rows)
        for c in range(cols)
    ]
    return lax.ppermute(values, AXES, pairs)


def pick(values, index):
    return lax.dynamic_index_in_dim(values, index, 0, keepdims=False)


def tree_sum(terms):
    while len(terms) > 1:
        terms = [a + b for a, b in zip(terms[::2], terms[1::2])]
    return terms[0]


def after(values, *events):
    return lax.optimization_barrier((values,) + events)[0]


def reduce_core(parts):
    core = lax.axis_index("row") % 2
    return pick(parts, core) + send(pick(parts, 1 - core), 1, 0)


def reduce_plane(own):
    col = lax.axis_index("col")
    others = [send(pick(own, col ^ flip), 0, flip) for flip in range(1, own.shape[0])]
    return tree_sum([pick(own, col)] + others)


def reduce_plane_with(own, rider):
    col, (cols, height, _) = lax.axis_index("col"), own.shape
    others = [
        send(jnp.concatenate([pick(own, col ^ flip), rider], axis=0), 0, flip)
        for flip in range(1, cols)
    ]
    total = tree_sum([pick(own, col)] + [other[:height] for other in others])
    riders = jnp.stack([rider] + [other[height:] for other in others])
    return total, jnp.stack([pick(riders, index ^ col) for index in range(cols)])


def reduce_z(own):
    return tree_sum([own] + [send(own, flip, 0) for flip in range(2, lax.axis_size("row"), 2)])


def spread_plane(part):
    col, cols = lax.axis_index("col"), lax.axis_size("col")
    near = jnp.stack([part] + [send(part, 0, flip) for flip in range(1, cols)])
    return jnp.stack([pick(near, index ^ col) for index in range(cols)])


def spread_core(near):
    core = lax.axis_index("row") % 2
    both = jnp.stack([near, send(near, 1, 0)])
    return jnp.stack([pick(both, core), pick(both, 1 - core)])


def split(x):
    high = x.astype(BF16)
    return high, (x - high.astype(F32)).astype(BF16)


def dot(a, b):
    return jnp.dot(a, b, preferred_element_type=F32)


def divide(x, y):
    return x * pl.reciprocal(y, approx=True)


def prepare_left(left_ref, pair_ref):
    rank = left_ref.shape[1]
    high, low = split(left_ref[...])
    pair_ref[:, :rank] = high
    pair_ref[:, rank : 2 * rank] = low
    pair_ref[:, 2 * rank :] = high


def prepare_left_t(left_ref, pair_t_ref, sums_ref):
    rank = left_ref.shape[1]
    turned = left_ref[...].T
    high, low = split(turned)
    pair_t_ref[:rank, :] = high
    pair_t_ref[rank:, :] = low
    sums_ref[...] = jnp.broadcast_to(jnp.sum(turned, axis=1, keepdims=True), sums_ref.shape)


def chunks(extent, size):
    size = min(size, extent)
    return [pl.ds(start, size) for start in range(0, extent, size)]


def stacked(right):
    high, low = split(right)
    return jnp.concatenate([high, high, low], axis=0)


def quotients(slab_ref, pair_ref, right_stack, rows):
    product = dot(pair_ref[rows, :], right_stack)
    return split(divide(slab_ref[rows, :], product))


def right_update(slab_ref, pair_ref, pair_t_ref, sums_ref, right):
    rank = right.shape[0]
    high, low = quotients(slab_ref, pair_ref, stacked(right), pl.ds(0, slab_ref.shape[0]))
    both = dot(pair_t_ref[...], high)
    numerator = both[:rank] + both[rank:] + dot(pair_t_ref[:rank, :], low)
    return right * numerator / sums_ref[:, :1]


def left_numerator(slab_ref, pair_ref, right, total_ref, sums_ref, first):
    rank = right.shape[0]
    stack = stacked(right)
    right_high, right_low = split(right.T)
    right_both = jnp.concatenate([right_high, right_low], axis=1)
    row_sums = dot(jnp.ones((16, right.shape[1]), BF16), right_both)[:PAD]
    row_sums = row_sums[:, :rank] + row_sums[:, rank:]
    sums_ref[...] = jnp.where(first, row_sums, sums_ref[...] + row_sums)
    for rows in chunks(slab_ref.shape[0], ROWS):
        high, low = quotients(slab_ref, pair_ref, stack, rows)
        both = dot(high, right_both)
        term = both[:, :rank] + both[:, rank:] + dot(low, right_high)
        total_ref[rows, :] = jnp.where(first, term, total_ref[rows, :] + term)


def write_left(total_ref, row_sums_ref, extra_ref, out_ref):
    parts, tall, rank = out_ref.shape
    height = tall - PAD
    first = lax.broadcasted_iota(jnp.int32, (PAD, rank), 0) == 0
    stats = jnp.where(first, row_sums_ref[...], extra_ref[:1, :])
    for part in range(parts):
        out_ref[part, :height, :] = total_ref[pl.ds(part * height, height), :]
        out_ref[part, height:, :] = stats


def turn_kernel(
    slab_ref, left_ref, right_ref, extra_ref, right_out, left_out,
    pair_ref, pair_t_ref, sums_ref, total_ref, row_sums_ref,
):
    step = pl.program_id(0)

    @pl.when(step == 0)
    def _():
        prepare_left(left_ref, pair_ref)
        prepare_left_t(left_ref, pair_t_ref, sums_ref)

    right = right_update(slab_ref, pair_ref, pair_t_ref, sums_ref, right_ref[...])
    right_out[...] = right
    left_numerator(slab_ref, pair_ref, right, total_ref, row_sums_ref, step == 0)

    @pl.when(step == pl.num_programs(0) - 1)
    def _():
        write_left(total_ref, row_sums_ref, extra_ref, left_out)


def second_parts(slices, right_ref, second_left_ref, second_right_ref):
    rank = right_ref.shape[0]
    k = right_ref.shape[1] // slices
    second_left = jnp.concatenate(
        [second_left_ref[pl.ds(index, rank, stride=slices), :] for index in range(slices)], axis=0
    )
    second_right = jnp.concatenate(
        [second_right_ref[block] for block in range(k // rank)], axis=1
    )
    high, low = split(second_left)
    product = dot(jnp.concatenate([high, low, high], axis=1), stacked(second_right))
    block = jnp.concatenate(
        [right_ref[:, index * k : (index + 1) * k] for index in range(slices)], axis=0
    )
    return second_left, second_right, split(divide(block, product))


def numerator_kernel(slices, right_ref, second_left_ref, second_right_ref, numer_out):
    second_left, _, (high, low) = second_parts(
        slices, right_ref, second_left_ref, second_right_ref
    )
    rank = second_left.shape[1]
    left_both = jnp.concatenate(split(second_left.T), axis=0)
    both = dot(left_both, high)
    total = both[:rank] + both[rank:] + dot(left_both[:rank], low)
    for block in range(total.shape[1] // rank):
        numer_out[block] = total[:, block * rank : (block + 1) * rank]


def second_kernel(slices, right_ref, second_left_ref, second_right_ref, out_ref):
    second_left, second_right, (high, low) = second_parts(
        slices, right_ref, second_left_ref, second_right_ref
    )
    rank = second_left.shape[1]
    right_high, right_low = split(second_right.T)
    right_both = jnp.concatenate([right_high, right_low], axis=1)
    sums = dot(jnp.ones((16, right_both.shape[0]), BF16), right_both)[:1]
    both = dot(high, right_both)
    numer = both[:, :rank] + both[:, rank:] + dot(low, right_high)
    rows = second_left * numer * (1.0 / (sums[:, :rank] + sums[:, rank:]))
    for index in range(slices):
        out_ref[pl.ds(index, rank, stride=slices), :] = rows[index * rank : (index + 1) * rank]


def full(shape):
    return pl.BlockSpec(shape, lambda step: (0,) * len(shape))


def params(vmem_bytes):
    return pltpu.CompilerParams(
        dimension_semantics=("arbitrary",), vmem_limit_bytes=vmem_bytes
    )


def left_scratch(m, rank):
    return [pltpu.VMEM((m, 3 * rank), BF16)]


def right_scratch(m, rank):
    return [pltpu.VMEM((2 * rank, m), BF16), pltpu.VMEM((rank, rank), F32)]


def total_scratch(m, rank):
    return [pltpu.VMEM((m, rank), F32), pltpu.VMEM((PAD, rank), F32)]


def cost(m, rank, columns, dots):
    return pl.CostEstimate(
        flops=6 * dots * m * rank * columns, bytes_accessed=4 * m * columns, transcendentals=0
    )


def full_turn(slab, left, right, extra, block, parts, vmem_bytes):
    (m, columns), rank = slab.shape, left.shape[1]
    columns_spec = lambda height: pl.BlockSpec((height, block), lambda step: (0, step))
    tall = m // parts + PAD
    return pl.pallas_call(
        turn_kernel,
        grid=(columns // block,),
        in_specs=[columns_spec(m), full((m, rank)), columns_spec(rank), full((min(PAD, extra.shape[0]), rank))],
        out_specs=[columns_spec(rank), full((parts, tall, rank))],
        out_shape=[
            jax.ShapeDtypeStruct((rank, columns), F32),
            jax.ShapeDtypeStruct((parts, tall, rank), F32),
        ],
        scratch_shapes=left_scratch(m, rank)
        + right_scratch(m, rank)
        + total_scratch(m, rank),
        compiler_params=params(vmem_bytes),
        cost_estimate=cost(m, rank, columns, 4),
        name="turn",
    )(slab, left, right, extra)


def second_numerator(right, second_left, second_right, slices):
    return pl.pallas_call(
        functools.partial(numerator_kernel, slices),
        out_shape=jax.ShapeDtypeStruct(second_right.shape, F32),
        compiler_params=pltpu.CompilerParams(vmem_limit_bytes=VMEM_BYTES),
        cost_estimate=cost(right.shape[0], right.shape[0], right.shape[1], 2),
        name="second_numerator",
    )(right, second_left, second_right)


def second_rows_out(right, second_left, second_right, slices):
    return pl.pallas_call(
        functools.partial(second_kernel, slices),
        out_shape=jax.ShapeDtypeStruct(second_left.shape, F32),
        compiler_params=pltpu.CompilerParams(vmem_limit_bytes=VMEM_BYTES),
        cost_estimate=cost(right.shape[0], right.shape[0], right.shape[1], 2),
        name="second_rows",
    )(right, second_left, second_right)


def prepare_kernel(slices, place_ref, second_left_ref, out_ref, sums_out):
    devices, tall, rank = out_ref.shape
    second_left = second_left_ref[...]
    sums_out[...] = jnp.sum(second_left, axis=0, keepdims=True)
    for index in range(tall // slices):
        for device in range(devices):
            start = (index * devices + device) * slices
            out_ref[device, index * slices : (index + 1) * slices, :] = second_left[
                start : start + slices
            ]


def prepare(place, second_left, devices, slices, second_rows):
    rank = second_left.shape[1]
    shapes = [(devices, second_rows // devices, rank), (1, rank)]
    return pl.pallas_call(
        functools.partial(prepare_kernel, slices),
        grid_spec=pltpu.PrefetchScalarGridSpec(
            num_scalar_prefetch=1,
            grid=(1,),
            in_specs=[pl.BlockSpec((second_rows, rank), lambda step, place: (place[0], 0))],
            out_specs=[
                pl.BlockSpec(shapes[0], lambda step, place: (0, 0, 0)),
                pl.BlockSpec(shapes[1], lambda step, place: (0, 0)),
            ],
        ),
        out_shape=[jax.ShapeDtypeStruct(shape, F32) for shape in shapes],
        compiler_params=params(PREP_KIB * 1024),
        cost_estimate=pl.CostEstimate(
            flops=second_rows * rank, bytes_accessed=8 * second_rows * rank, transcendentals=0
        ),
        name="prepare",
    )(place, second_left)


def body(tensor_slab, left_init, right_init, second_left_init, second_right_init):
    row_devices = lax.axis_size("row")
    col_devices = lax.axis_size("col")
    devices = row_devices * col_devices
    own_part = (lax.axis_index("row") % 2) * col_devices + lax.axis_index("col")
    parts = 2 * col_devices
    m, rank = left_init.shape
    k = second_right_init.shape[1] * col_devices
    slices = right_init.shape[1] // k
    per_owner = rank // devices
    rows_own = m // parts

    def own_rows(left):
        return lax.dynamic_slice_in_dim(left, own_part * rows_own, rows_own, 0)

    def own_left_rows(own, total):
        return own * total[:rows_own] / total[rows_own][None, :]

    right, summed = full_turn(
        tensor_slab, left_init, right_init, left_init, k // 2, parts, T1_MIB * MIB
    )
    second_left = after(second_left_init, summed)
    summed = summed.reshape(2, col_devices, rows_own + PAD, rank)
    core_sum = reduce_core(summed)
    own_init = after(own_rows(left_init), core_sum)

    half = rank // 2
    groups = rank // second_right_init.shape[1]
    rider = lax.dynamic_slice_in_dim(second_right_init, lax.axis_index("row") % 2 * half, half, 0)
    rider = jnp.concatenate(jnp.split(rider, groups, axis=0), axis=1)
    plane, riders = reduce_plane_with(core_sum, rider)
    total = reduce_z(plane)
    near = spread_plane(own_left_rows(own_init, total))
    both = spread_core(jnp.concatenate([near, riders], axis=1))
    left = both[:, :, :rows_own].reshape(m, rank)
    whole = both[:, :, rows_own:].reshape(2, col_devices, half // groups, groups, -1)
    whole = whole.transpose(0, 3, 2, 1, 4).reshape(rank, k // rank, rank).transpose(1, 0, 2)

    second_rows = second_left_init.shape[0] // col_devices
    place = lax.axis_index("col").astype(jnp.int32)[None]
    second_left, col_part = prepare(place, second_left, devices, slices, second_rows)
    arrived = exchange(after(second_left, left))
    right, summed = full_turn(tensor_slab, left, right, col_part, k // 2, parts, VMEM_BYTES)
    arrived = after(arrived, summed)
    second_left = arrived.reshape(rank * slices, rank)
    numerator = second_numerator(right, second_left, whole, slices)

    rows_part = k // parts
    summed = summed.reshape(2, col_devices, rows_own + PAD, rank)
    numerator = numerator.reshape(2, col_devices, rows_part, rank)
    total = reduce_z(reduce_plane(reduce_core(jnp.concatenate([summed, numerator], axis=2))))
    init_over = (whole / total[rows_own + 1][None, :, None]).reshape(k, rank)
    init_over = lax.dynamic_slice_in_dim(init_over, own_part * rows_part, rows_part, 0)
    second_part = init_over * total[rows_own + PAD :]
    both = spread_core(
        spread_plane(jnp.concatenate([own_left_rows(own_rows(left), total), second_part], axis=0))
    )
    left_out = both[:, :, :rows_own].reshape(m, rank)
    second_right = both[:, :, rows_own:].reshape(k // rank, rank, rank)
    rows_out = second_rows_out(right, second_left, second_right, slices)
    returned = exchange(rows_out.reshape(devices, per_owner * slices, rank))
    returned = returned.reshape(devices, per_owner, slices, rank).transpose(1, 0, 2, 3)
    return (left_out, returned.reshape(second_rows, rank))


def solution(mesh):
    placed = (P(None, AXES), P(), P(None, AXES), P("row", None), P(None, "col"))
    return jax.shard_map(
        body, mesh=mesh, in_specs=placed, out_specs=(P(), P(AXES, None)), check_vma=False
    )
```

```python
import functools

import jax
import jax.numpy as jnp
from jax import lax
from jax.experimental import pallas as pl
from jax.experimental.pallas import tpu as pltpu
from jax.sharding import PartitionSpec as P

AXES = ("row", "col")
F32, BF16 = jnp.float32, jnp.bfloat16
PAD = 8
MIB = 1024 * 1024
T1_MIB = 52
PREP_KIB = 54528
VMEM_BYTES = 51 * MIB


def exchange(parts):
    return lax.all_to_all(parts, AXES, split_axis=0, concat_axis=0, tiled=True)


def send(values, row_flip, col_flip):
    rows, cols = lax.axis_size("row"), lax.axis_size("col")
    pairs = [
        (r * cols + c, (r ^ row_flip) * cols + (c ^ col_flip))
        for r in range(rows)
        for c in range(cols)
    ]
    return lax.ppermute(values, AXES, pairs)


def pick(values, index):
    return lax.dynamic_index_in_dim(values, index, 0, keepdims=False)


def tree_sum(terms):
    while len(terms) > 1:
        terms = [a + b for a, b in zip(terms[::2], terms[1::2])]
    return terms[0]


def after(values, *events):
    return lax.optimization_barrier((values,) + events)[0]


def reduce_core(parts):
    core = lax.axis_index("row") % 2
    return pick(parts, core) + send(pick(parts, 1 - core), 1, 0)


def reduce_plane(own):
    col = lax.axis_index("col")
    others = [send(pick(own, col ^ flip), 0, flip) for flip in range(1, own.shape[0])]
    return tree_sum([pick(own, col)] + others)


def reduce_plane_with(own, rider):
    col, (cols, height, _) = lax.axis_index("col"), own.shape
    others = [
        send(jnp.concatenate([pick(own, col ^ flip), rider], axis=0), 0, flip)
        for flip in range(1, cols)
    ]
    total = tree_sum([pick(own, col)] + [other[:height] for other in others])
    riders = jnp.stack([rider] + [other[height:] for other in others])
    return total, jnp.stack([pick(riders, index ^ col) for index in range(cols)])


def reduce_z(own):
    return tree_sum([own] + [send(own, flip, 0) for flip in range(2, lax.axis_size("row"), 2)])


def spread_plane(part):
    col, cols = lax.axis_index("col"), lax.axis_size("col")
    near = jnp.stack([part] + [send(part, 0, flip) for flip in range(1, cols)])
    return jnp.stack([pick(near, index ^ col) for index in range(cols)])


def spread_core(near):
    core = lax.axis_index("row") % 2
    both = jnp.stack([near, send(near, 1, 0)])
    return jnp.stack([pick(both, core), pick(both, 1 - core)])


def split(x):
    high = x.astype(BF16)
    return high, (x - high.astype(F32)).astype(BF16)


def dot(a, b):
    return jnp.dot(a, b, preferred_element_type=F32)


def dot_nt(a, b):
    return lax.dot_general(a, b, (((1,), (1,)), ((), ())), preferred_element_type=F32)


def divide(x, y):
    return x * pl.reciprocal(y, approx=True)


def prepare_left(left_ref, pair_ref):
    rank = left_ref.shape[1]
    high, low = split(left_ref[...])
    pair_ref[:, :rank] = high
    pair_ref[:, rank : 2 * rank] = low
    pair_ref[:, 2 * rank :] = high


def prepare_left_t(left_ref, pair_t_ref, sums_ref):
    rank = left_ref.shape[1]
    turned = left_ref[...].T
    high, low = split(turned)
    pair_t_ref[:rank, :] = high
    pair_t_ref[rank:, :] = low
    sums_ref[...] = jnp.broadcast_to(jnp.sum(turned, axis=1, keepdims=True), sums_ref.shape)


def stacked(right):
    high, low = split(right)
    return jnp.concatenate([high, high, low], axis=0)


def quotients(slab_ref, pair_ref, right_stack, rows):
    product = dot(pair_ref[rows, :], right_stack)
    return split(divide(slab_ref[rows, :], product))


def right_update(slab_ref, pair_ref, pair_t_ref, sums_ref, right):
    rank = right.shape[0]
    high, low = quotients(slab_ref, pair_ref, stacked(right), pl.ds(0, slab_ref.shape[0]))
    both = dot(pair_t_ref[...], high)
    numerator = both[:rank] + both[rank:] + dot(pair_t_ref[:rank, :], low)
    return right * numerator / sums_ref[:, :1]


def left_numerator(slab_ref, pair_ref, right, total_ref, sums_ref, first):
    rank = right.shape[0]
    stack = stacked(right)
    right_both = jnp.concatenate([stack[:rank], stack[2 * rank :]], axis=0)
    row_sums = dot_nt(jnp.ones((16, right.shape[1]), BF16), right_both)[:PAD]
    row_sums = row_sums[:, :rank] + row_sums[:, rank:]
    sums_ref[...] = jnp.where(first, row_sums, sums_ref[...] + row_sums)
    high, low = quotients(slab_ref, pair_ref, stack, pl.ds(0, slab_ref.shape[0]))
    both = dot_nt(right_both, high)
    term = both[:rank] + both[rank:] + dot_nt(stack[:rank], low)
    total_ref[...] = jnp.where(first, term, total_ref[...] + term)


def write_left(total_ref, row_sums_ref, extra_ref, out_ref):
    parts, tall, rank = out_ref.shape
    height = tall - PAD
    first = lax.broadcasted_iota(jnp.int32, (PAD, rank), 0) == 0
    stats = jnp.where(first, row_sums_ref[...], extra_ref[:1, :])
    total = total_ref[...].T
    for part in range(parts):
        out_ref[part, :height, :] = total[part * height : (part + 1) * height]
        out_ref[part, height:, :] = stats


def turn_kernel(
    slab_ref, left_ref, right_ref, extra_ref, right_out, left_out,
    pair_ref, pair_t_ref, sums_ref, total_ref, row_sums_ref,
):
    step = pl.program_id(0)

    @pl.when(step == 0)
    def _():
        prepare_left(left_ref, pair_ref)
        prepare_left_t(left_ref, pair_t_ref, sums_ref)

    right = right_update(slab_ref, pair_ref, pair_t_ref, sums_ref, right_ref[...])
    right_out[...] = right
    left_numerator(slab_ref, pair_ref, right, total_ref, row_sums_ref, step == 0)

    @pl.when(step == pl.num_programs(0) - 1)
    def _():
        write_left(total_ref, row_sums_ref, extra_ref, left_out)


def second_parts(slices, right_ref, second_left_ref, second_right_ref):
    rank = right_ref.shape[0]
    k = right_ref.shape[1] // slices
    second_left = jnp.concatenate(
        [second_left_ref[pl.ds(index, rank, stride=slices), :] for index in range(slices)], axis=0
    )
    second_right = jnp.concatenate(
        [second_right_ref[block] for block in range(k // rank)], axis=1
    )
    high, low = split(second_left)
    product = dot(jnp.concatenate([high, low, high], axis=1), stacked(second_right))
    block = jnp.concatenate(
        [right_ref[:, index * k : (index + 1) * k] for index in range(slices)], axis=0
    )
    return second_left, second_right, split(divide(block, product))


def numerator_kernel(slices, right_ref, second_left_ref, second_right_ref, numer_out):
    second_left, _, (high, low) = second_parts(
        slices, right_ref, second_left_ref, second_right_ref
    )
    rank = second_left.shape[1]
    left_both = jnp.concatenate(split(second_left.T), axis=0)
    both = dot(left_both, high)
    total = both[:rank] + both[rank:] + dot(left_both[:rank], low)
    for block in range(total.shape[1] // rank):
        numer_out[block] = total[:, block * rank : (block + 1) * rank]


def second_kernel(slices, right_ref, second_left_ref, second_right_ref, out_ref):
    second_left, second_right, (high, low) = second_parts(
        slices, right_ref, second_left_ref, second_right_ref
    )
    rank = second_left.shape[1]
    right_high, right_low = split(second_right.T)
    right_both = jnp.concatenate([right_high, right_low], axis=1)
    sums = dot(jnp.ones((16, right_both.shape[0]), BF16), right_both)[:1]
    both = dot(high, right_both)
    numer = both[:, :rank] + both[:, rank:] + dot(low, right_high)
    rows = second_left * numer * (1.0 / (sums[:, :rank] + sums[:, rank:]))
    for index in range(slices):
        out_ref[pl.ds(index, rank, stride=slices), :] = rows[index * rank : (index + 1) * rank]


def full(shape):
    return pl.BlockSpec(shape, lambda step: (0,) * len(shape))


def params(vmem_bytes):
    return pltpu.CompilerParams(
        dimension_semantics=("arbitrary",), vmem_limit_bytes=vmem_bytes
    )


def left_scratch(m, rank):
    return [pltpu.VMEM((m, 3 * rank), BF16)]


def right_scratch(m, rank):
    return [pltpu.VMEM((2 * rank, m), BF16), pltpu.VMEM((rank, rank), F32)]


def total_scratch(m, rank):
    return [pltpu.VMEM((rank, m), F32), pltpu.VMEM((PAD, rank), F32)]


def cost(m, rank, columns, dots):
    return pl.CostEstimate(
        flops=6 * dots * m * rank * columns, bytes_accessed=4 * m * columns, transcendentals=0
    )


def full_turn(slab, left, right, extra, block, parts, vmem_bytes):
    (m, columns), rank = slab.shape, left.shape[1]
    columns_spec = lambda height: pl.BlockSpec((height, block), lambda step: (0, step))
    tall = m // parts + PAD
    return pl.pallas_call(
        turn_kernel,
        grid=(columns // block,),
        in_specs=[columns_spec(m), full((m, rank)), columns_spec(rank), full((min(PAD, extra.shape[0]), rank))],
        out_specs=[columns_spec(rank), full((parts, tall, rank))],
        out_shape=[
            jax.ShapeDtypeStruct((rank, columns), F32),
            jax.ShapeDtypeStruct((parts, tall, rank), F32),
        ],
        scratch_shapes=left_scratch(m, rank)
        + right_scratch(m, rank)
        + total_scratch(m, rank),
        compiler_params=params(vmem_bytes),
        cost_estimate=cost(m, rank, columns, 4),
        name="turn",
    )(slab, left, right, extra)


def second_numerator(right, second_left, second_right, slices):
    return pl.pallas_call(
        functools.partial(numerator_kernel, slices),
        out_shape=jax.ShapeDtypeStruct(second_right.shape, F32),
        compiler_params=pltpu.CompilerParams(vmem_limit_bytes=VMEM_BYTES),
        cost_estimate=cost(right.shape[0], right.shape[0], right.shape[1], 2),
        name="second_numerator",
    )(right, second_left, second_right)


def second_rows_out(right, second_left, second_right, slices):
    return pl.pallas_call(
        functools.partial(second_kernel, slices),
        out_shape=jax.ShapeDtypeStruct(second_left.shape, F32),
        compiler_params=pltpu.CompilerParams(vmem_limit_bytes=VMEM_BYTES),
        cost_estimate=cost(right.shape[0], right.shape[0], right.shape[1], 2),
        name="second_rows",
    )(right, second_left, second_right)


def prepare_kernel(slices, place_ref, second_left_ref, out_ref, sums_out):
    devices, tall, rank = out_ref.shape
    second_left = second_left_ref[...]
    sums_out[...] = jnp.sum(second_left, axis=0, keepdims=True)
    for index in range(tall // slices):
        for device in range(devices):
            start = (index * devices + device) * slices
            out_ref[device, index * slices : (index + 1) * slices, :] = second_left[
                start : start + slices
            ]


def prepare(place, second_left, devices, slices, second_rows):
    rank = second_left.shape[1]
    shapes = [(devices, second_rows // devices, rank), (1, rank)]
    return pl.pallas_call(
        functools.partial(prepare_kernel, slices),
        grid_spec=pltpu.PrefetchScalarGridSpec(
            num_scalar_prefetch=1,
            grid=(1,),
            in_specs=[pl.BlockSpec((second_rows, rank), lambda step, place: (place[0], 0))],
            out_specs=[
                pl.BlockSpec(shapes[0], lambda step, place: (0, 0, 0)),
                pl.BlockSpec(shapes[1], lambda step, place: (0, 0)),
            ],
        ),
        out_shape=[jax.ShapeDtypeStruct(shape, F32) for shape in shapes],
        compiler_params=params(PREP_KIB * 1024),
        cost_estimate=pl.CostEstimate(
            flops=second_rows * rank, bytes_accessed=8 * second_rows * rank, transcendentals=0
        ),
        name="prepare",
    )(place, second_left)


def body(tensor_slab, left_init, right_init, second_left_init, second_right_init):
    row_devices = lax.axis_size("row")
    col_devices = lax.axis_size("col")
    devices = row_devices * col_devices
    own_part = (lax.axis_index("row") % 2) * col_devices + lax.axis_index("col")
    parts = 2 * col_devices
    m, rank = left_init.shape
    k = second_right_init.shape[1] * col_devices
    slices = right_init.shape[1] // k
    per_owner = rank // devices
    rows_own = m // parts

    def own_rows(left):
        return lax.dynamic_slice_in_dim(left, own_part * rows_own, rows_own, 0)

    def own_left_rows(own, total):
        return own * total[:rows_own] / total[rows_own][None, :]

    right, summed = full_turn(
        tensor_slab, left_init, right_init, left_init, k, parts, T1_MIB * MIB
    )
    second_left = after(second_left_init, summed)
    summed = summed.reshape(2, col_devices, rows_own + PAD, rank)
    core_sum = reduce_core(summed)
    own_init = after(own_rows(left_init), core_sum)

    half = rank // 2
    groups = rank // second_right_init.shape[1]
    rider = lax.dynamic_slice_in_dim(second_right_init, lax.axis_index("row") % 2 * half, half, 0)
    rider = jnp.concatenate(jnp.split(rider, groups, axis=0), axis=1)
    plane, riders = reduce_plane_with(core_sum, rider)
    total = reduce_z(plane)
    near = spread_plane(own_left_rows(own_init, total))
    both = spread_core(jnp.concatenate([near, riders], axis=1))
    left = both[:, :, :rows_own].reshape(m, rank)
    whole = both[:, :, rows_own:].reshape(2, col_devices, half // groups, groups, -1)
    whole = whole.transpose(0, 3, 2, 1, 4).reshape(rank, k // rank, rank).transpose(1, 0, 2)

    second_rows = second_left_init.shape[0] // col_devices
    place = lax.axis_index("col").astype(jnp.int32)[None]
    second_left, col_part = prepare(place, second_left, devices, slices, second_rows)
    arrived = exchange(after(second_left, left))
    right, summed = full_turn(tensor_slab, left, right, col_part, k, parts, VMEM_BYTES)
    arrived = after(arrived, summed)
    second_left = arrived.reshape(rank * slices, rank)
    numerator = second_numerator(right, second_left, whole, slices)

    rows_part = k // parts
    summed = summed.reshape(2, col_devices, rows_own + PAD, rank)
    numerator = numerator.reshape(2, col_devices, rows_part, rank)
    total = reduce_z(reduce_plane(reduce_core(jnp.concatenate([summed, numerator], axis=2))))
    init_over = (whole / total[rows_own + 1][None, :, None]).reshape(k, rank)
    init_over = lax.dynamic_slice_in_dim(init_over, own_part * rows_part, rows_part, 0)
    second_part = init_over * total[rows_own + PAD :]
    both = spread_core(
        spread_plane(jnp.concatenate([own_left_rows(own_rows(left), total), second_part], axis=0))
    )
    left_out = both[:, :, :rows_own].reshape(m, rank)
    second_right = both[:, :, rows_own:].reshape(k // rank, rank, rank)
    rows_out = second_rows_out(right, second_left, second_right, slices)
    returned = exchange(rows_out.reshape(devices, per_owner * slices, rank))
    returned = returned.reshape(devices, per_owner, slices, rank).transpose(1, 0, 2, 3)
    return (left_out, returned.reshape(second_rows, rank))


def solution(mesh):
    placed = (P(None, AXES), P(), P(None, AXES), P("row", None), P(None, "col"))
    return jax.shard_map(
        body, mesh=mesh, in_specs=placed, out_specs=(P(), P(AXES, None)), check_vma=False
    )
```

```python
import functools

import jax
import jax.numpy as jnp
from jax import lax
from jax.experimental import pallas as pl
from jax.experimental.pallas import tpu as pltpu
from jax.sharding import PartitionSpec as P

AXES = ("row", "col")
F32, BF16 = jnp.float32, jnp.bfloat16
PAD = 8
MIB = 1024 * 1024
T1_MIB = 52
PREP_KIB = 54528
VMEM_BYTES = 51 * MIB


def exchange(parts):
    return lax.all_to_all(parts, AXES, split_axis=0, concat_axis=0, tiled=True)


def send(values, row_flip, col_flip):
    rows, cols = lax.axis_size("row"), lax.axis_size("col")
    pairs = [
        (r * cols + c, (r ^ row_flip) * cols + (c ^ col_flip))
        for r in range(rows)
        for c in range(cols)
    ]
    return lax.ppermute(values, AXES, pairs)


def pick(values, index):
    return lax.dynamic_index_in_dim(values, index, 0, keepdims=False)


def tree_sum(terms):
    while len(terms) > 1:
        terms = [a + b for a, b in zip(terms[::2], terms[1::2])]
    return terms[0]


def after(values, *events):
    return lax.optimization_barrier((values,) + events)[0]


def reduce_core(parts):
    core = lax.axis_index("row") % 2
    return pick(parts, core) + send(pick(parts, 1 - core), 1, 0)


def reduce_plane(own):
    col = lax.axis_index("col")
    others = [send(pick(own, col ^ flip), 0, flip) for flip in range(1, own.shape[0])]
    return tree_sum([pick(own, col)] + others)


def reduce_plane_with(own, rider):
    col, (cols, height, _) = lax.axis_index("col"), own.shape
    others = [
        send(jnp.concatenate([pick(own, col ^ flip), rider], axis=0), 0, flip)
        for flip in range(1, cols)
    ]
    total = tree_sum([pick(own, col)] + [other[:height] for other in others])
    riders = jnp.stack([rider] + [other[height:] for other in others])
    return total, jnp.stack([pick(riders, index ^ col) for index in range(cols)])


def reduce_z(own):
    return tree_sum([own] + [send(own, flip, 0) for flip in range(2, lax.axis_size("row"), 2)])


def spread_plane(part):
    col, cols = lax.axis_index("col"), lax.axis_size("col")
    near = jnp.stack([part] + [send(part, 0, flip) for flip in range(1, cols)])
    return jnp.stack([pick(near, index ^ col) for index in range(cols)])


def spread_core(near):
    core = lax.axis_index("row") % 2
    both = jnp.stack([near, send(near, 1, 0)])
    return jnp.stack([pick(both, core), pick(both, 1 - core)])


def split(x):
    high = x.astype(BF16)
    return high, (x - high.astype(F32)).astype(BF16)


def dot(a, b):
    return jnp.dot(a, b, preferred_element_type=F32)


def dot_nt(a, b):
    return lax.dot_general(a, b, (((1,), (1,)), ((), ())), preferred_element_type=F32)


def divide(x, y):
    return x * pl.reciprocal(y, approx=True)


def prepare_left(left_ref, pair_ref):
    rank = left_ref.shape[1]
    high, low = split(left_ref[...])
    pair_ref[:, :rank] = high
    pair_ref[:, rank : 2 * rank] = low
    pair_ref[:, 2 * rank :] = high


def prepare_left_t(left_ref, pair_t_ref, sums_ref):
    rank = left_ref.shape[1]
    turned = left_ref[...].T
    high, low = split(turned)
    pair_t_ref[:rank, :] = high
    pair_t_ref[rank:, :] = low
    sums_ref[...] = jnp.broadcast_to(jnp.sum(turned, axis=1, keepdims=True), sums_ref.shape)


def stacked(right):
    high, low = split(right)
    return jnp.concatenate([high, high, low], axis=0)


def quotients(slab_ref, pair_ref, right_stack, rows):
    product = dot(pair_ref[rows, :], right_stack)
    return split(divide(slab_ref[rows, :], product))


def right_update(slab_ref, pair_ref, pair_t_ref, sums_ref, right):
    rank = right.shape[0]
    high, low = quotients(slab_ref, pair_ref, stacked(right), pl.ds(0, slab_ref.shape[0]))
    both = dot(pair_t_ref[...], high)
    numerator = both[:rank] + both[rank:] + dot(pair_t_ref[:rank, :], low)
    return right * numerator / sums_ref[:, :1]


def left_numerator(slab_ref, pair_ref, right, total_ref, sums_ref, first):
    rank = right.shape[0]
    stack = stacked(right)
    right_both = jnp.concatenate([stack[:rank], stack[2 * rank :]], axis=0)
    row_sums = dot_nt(jnp.ones((16, right.shape[1]), BF16), right_both)[:PAD]
    row_sums = row_sums[:, :rank] + row_sums[:, rank:]
    sums_ref[...] = jnp.where(first, row_sums, sums_ref[...] + row_sums)
    high, low = quotients(slab_ref, pair_ref, stack, pl.ds(0, slab_ref.shape[0]))
    both = dot_nt(right_both, high)
    term = both[:rank] + both[rank:] + dot_nt(stack[:rank], low)
    total_ref[...] = jnp.where(first, term, total_ref[...] + term)


def write_left(total_ref, row_sums_ref, extra_ref, out_ref):
    parts, tall, rank = out_ref.shape
    height = tall - PAD
    first = lax.broadcasted_iota(jnp.int32, (PAD, rank), 0) == 0
    stats = jnp.where(first, row_sums_ref[...], extra_ref[:1, :])
    total = total_ref[...].T
    for part in range(parts):
        out_ref[part, :height, :] = total[part * height : (part + 1) * height]
        out_ref[part, height:, :] = stats


def turn_kernel(
    slab_ref, left_ref, right_ref, extra_ref, right_out, left_out,
    pair_ref, pair_t_ref, sums_ref, total_ref, row_sums_ref,
):
    step = pl.program_id(0)

    @pl.when(step == 0)
    def _():
        prepare_left(left_ref, pair_ref)
        prepare_left_t(left_ref, pair_t_ref, sums_ref)

    right = right_update(slab_ref, pair_ref, pair_t_ref, sums_ref, right_ref[...])
    right_out[...] = right
    left_numerator(slab_ref, pair_ref, right, total_ref, row_sums_ref, step == 0)

    @pl.when(step == pl.num_programs(0) - 1)
    def _():
        write_left(total_ref, row_sums_ref, extra_ref, left_out)


def second_parts(slices, right_ref, second_left_ref, second_right_ref):
    rank = right_ref.shape[0]
    k = right_ref.shape[1] // slices
    second_left = jnp.concatenate(
        [second_left_ref[pl.ds(index, rank, stride=slices), :] for index in range(slices)], axis=0
    )
    second_right = jnp.concatenate(
        [second_right_ref[block] for block in range(k // rank)], axis=1
    )
    high, low = split(second_left)
    product = dot(jnp.concatenate([high, low, high], axis=1), stacked(second_right))
    block = jnp.concatenate(
        [right_ref[:, index * k : (index + 1) * k] for index in range(slices)], axis=0
    )
    return second_left, second_right, split(divide(block, product))


def numerator_kernel(slices, right_ref, second_left_ref, second_right_ref, numer_out):
    second_left, _, (high, low) = second_parts(
        slices, right_ref, second_left_ref, second_right_ref
    )
    rank = second_left.shape[1]
    left_both = jnp.concatenate(split(second_left.T), axis=0)
    both = dot(left_both, high)
    total = both[:rank] + both[rank:] + dot(left_both[:rank], low)
    for block in range(total.shape[1] // rank):
        numer_out[block] = total[:, block * rank : (block + 1) * rank]


def second_kernel(slices, right_ref, second_left_ref, second_right_ref, out_ref):
    second_left, second_right, (high, low) = second_parts(
        slices, right_ref, second_left_ref, second_right_ref
    )
    rank = second_left.shape[1]
    right_high, right_low = split(second_right.T)
    right_both = jnp.concatenate([right_high, right_low], axis=1)
    sums = dot(jnp.ones((16, right_both.shape[0]), BF16), right_both)[:1]
    both = dot(high, right_both)
    numer = both[:, :rank] + both[:, rank:] + dot(low, right_high)
    rows = second_left * numer * (1.0 / (sums[:, :rank] + sums[:, rank:]))
    for index in range(slices):
        out_ref[pl.ds(index, rank, stride=slices), :] = rows[index * rank : (index + 1) * rank]


def full(shape):
    return pl.BlockSpec(shape, lambda step: (0,) * len(shape))


def params(vmem_bytes):
    return pltpu.CompilerParams(
        dimension_semantics=("arbitrary",), vmem_limit_bytes=vmem_bytes
    )


def left_scratch(m, rank):
    return [pltpu.VMEM((m, 3 * rank), BF16)]


def right_scratch(m, rank):
    return [pltpu.VMEM((2 * rank, m), BF16), pltpu.VMEM((rank, rank), F32)]


def total_scratch(m, rank):
    return [pltpu.VMEM((rank, m), F32), pltpu.VMEM((PAD, rank), F32)]


def cost(m, rank, columns, dots):
    return pl.CostEstimate(
        flops=6 * dots * m * rank * columns, bytes_accessed=4 * m * columns, transcendentals=0
    )


def full_turn(slab, left, right, extra, block, parts, vmem_bytes):
    (m, columns), rank = slab.shape, left.shape[1]
    columns_spec = lambda height: pl.BlockSpec((height, block), lambda step: (0, step))
    tall = m // parts + PAD
    return pl.pallas_call(
        turn_kernel,
        grid=(columns // block,),
        in_specs=[columns_spec(m), full((m, rank)), columns_spec(rank), full((min(PAD, extra.shape[0]), rank))],
        out_specs=[columns_spec(rank), full((parts, tall, rank))],
        out_shape=[
            jax.ShapeDtypeStruct((rank, columns), F32),
            jax.ShapeDtypeStruct((parts, tall, rank), F32),
        ],
        scratch_shapes=left_scratch(m, rank)
        + right_scratch(m, rank)
        + total_scratch(m, rank),
        compiler_params=params(vmem_bytes),
        cost_estimate=cost(m, rank, columns, 4),
        name="turn",
    )(slab, left, right, extra)


def second_numerator(right, second_left, second_right, slices):
    return pl.pallas_call(
        functools.partial(numerator_kernel, slices),
        out_shape=jax.ShapeDtypeStruct(second_right.shape, F32),
        compiler_params=pltpu.CompilerParams(vmem_limit_bytes=VMEM_BYTES),
        cost_estimate=cost(right.shape[0], right.shape[0], right.shape[1], 2),
        name="second_numerator",
    )(right, second_left, second_right)


def second_rows_out(right, second_left, second_right, slices):
    return pl.pallas_call(
        functools.partial(second_kernel, slices),
        out_shape=jax.ShapeDtypeStruct(second_left.shape, F32),
        compiler_params=pltpu.CompilerParams(vmem_limit_bytes=VMEM_BYTES),
        cost_estimate=cost(right.shape[0], right.shape[0], right.shape[1], 2),
        name="second_rows",
    )(right, second_left, second_right)


def prepare_kernel(slices, place_ref, second_left_ref, out_ref, sums_out):
    devices, tall, rank = out_ref.shape
    second_left = second_left_ref[...]
    sums_out[...] = jnp.sum(second_left, axis=0, keepdims=True)
    for index in range(tall // slices):
        for device in range(devices):
            start = (index * devices + device) * slices
            out_ref[device, index * slices : (index + 1) * slices, :] = second_left[
                start : start + slices
            ]


def prepare(place, second_left, devices, slices, second_rows):
    rank = second_left.shape[1]
    shapes = [(devices, second_rows // devices, rank), (1, rank)]
    return pl.pallas_call(
        functools.partial(prepare_kernel, slices),
        grid_spec=pltpu.PrefetchScalarGridSpec(
            num_scalar_prefetch=1,
            grid=(1,),
            in_specs=[pl.BlockSpec((second_rows, rank), lambda step, place: (place[0], 0))],
            out_specs=[
                pl.BlockSpec(shapes[0], lambda step, place: (0, 0, 0)),
                pl.BlockSpec(shapes[1], lambda step, place: (0, 0)),
            ],
        ),
        out_shape=[jax.ShapeDtypeStruct(shape, F32) for shape in shapes],
        compiler_params=params(PREP_KIB * 1024),
        cost_estimate=pl.CostEstimate(
            flops=second_rows * rank, bytes_accessed=8 * second_rows * rank, transcendentals=0
        ),
        name="prepare",
    )(place, second_left)


def body(tensor_slab, left_init, right_init, second_left_init, second_right_init):
    row_devices = lax.axis_size("row")
    col_devices = lax.axis_size("col")
    devices = row_devices * col_devices
    own_part = (lax.axis_index("row") % 2) * col_devices + lax.axis_index("col")
    parts = 2 * col_devices
    m, rank = left_init.shape
    k = second_right_init.shape[1] * col_devices
    slices = right_init.shape[1] // k
    per_owner = rank // devices
    rows_own = m // parts

    def own_rows(left):
        return lax.dynamic_slice_in_dim(left, own_part * rows_own, rows_own, 0)

    def own_left_rows(own, total):
        return own * total[:rows_own] / total[rows_own][None, :]

    right, summed = full_turn(
        tensor_slab, left_init, right_init, left_init, 2 * k, parts, T1_MIB * MIB
    )
    second_left = after(second_left_init, summed)
    summed = summed.reshape(2, col_devices, rows_own + PAD, rank)
    core_sum = reduce_core(summed)
    own_init = after(own_rows(left_init), core_sum)

    half = rank // 2
    groups = rank // second_right_init.shape[1]
    rider = lax.dynamic_slice_in_dim(second_right_init, lax.axis_index("row") % 2 * half, half, 0)
    rider = jnp.concatenate(jnp.split(rider, groups, axis=0), axis=1)
    plane, riders = reduce_plane_with(core_sum, rider)
    total = reduce_z(plane)
    near = spread_plane(own_left_rows(own_init, total))
    both = spread_core(jnp.concatenate([near, riders], axis=1))
    left = both[:, :, :rows_own].reshape(m, rank)
    whole = both[:, :, rows_own:].reshape(2, col_devices, half // groups, groups, -1)
    whole = whole.transpose(0, 3, 2, 1, 4).reshape(rank, k // rank, rank).transpose(1, 0, 2)

    second_rows = second_left_init.shape[0] // col_devices
    place = lax.axis_index("col").astype(jnp.int32)[None]
    second_left, col_part = prepare(place, second_left, devices, slices, second_rows)
    arrived = exchange(after(second_left, left))
    right, summed = full_turn(tensor_slab, left, right, col_part, 2 * k, parts, VMEM_BYTES)
    arrived = after(arrived, summed)
    second_left = arrived.reshape(rank * slices, rank)
    numerator = second_numerator(right, second_left, whole, slices)

    rows_part = k // parts
    summed = summed.reshape(2, col_devices, rows_own + PAD, rank)
    numerator = numerator.reshape(2, col_devices, rows_part, rank)
    total = reduce_z(reduce_plane(reduce_core(jnp.concatenate([summed, numerator], axis=2))))
    init_over = (whole / total[rows_own + 1][None, :, None]).reshape(k, rank)
    init_over = lax.dynamic_slice_in_dim(init_over, own_part * rows_part, rows_part, 0)
    second_part = init_over * total[rows_own + PAD :]
    both = spread_core(
        spread_plane(jnp.concatenate([own_left_rows(own_rows(left), total), second_part], axis=0))
    )
    left_out = both[:, :, :rows_own].reshape(m, rank)
    second_right = both[:, :, rows_own:].reshape(k // rank, rank, rank)
    rows_out = second_rows_out(right, second_left, second_right, slices)
    returned = exchange(rows_out.reshape(devices, per_owner * slices, rank))
    returned = returned.reshape(devices, per_owner, slices, rank).transpose(1, 0, 2, 3)
    return (left_out, returned.reshape(second_rows, rank))


def solution(mesh):
    placed = (P(None, AXES), P(), P(None, AXES), P("row", None), P(None, "col"))
    return jax.shard_map(
        body, mesh=mesh, in_specs=placed, out_specs=(P(), P(AXES, None)), check_vma=False
    )
```
